256 devices in a mesh: row: 8 (over x, core), cent: 32 (over y, z).
Axes of the slice: x: 4, y: 4, z: 8, core: 2. Of those that a mesh axis runs over, the one named last changes fastest.
Arguments:
- sketches: bfloat16 [65536, 512], P('row'), may hold values from -50 to 50
- centroids: float32 [8192, 512], P('cent'), may hold values from -5 to 5
- coarse_init: float32 [256, 512], replicated, may hold values from -4 to 4
Outputs:
- fine_centroids: float32 [8192, 512], P('cent')
- fine_counts: float32 [8192], P('cent')
- coarse_centroids: float32 [256, 512], replicated
- coarse_mass: float32 [256], replicated
- row_score: float32 [65536], P('row')
The draws below stay inside these ranges and needn't reach their ends.
All inputs are finite; a program needn't handle non-finite values.
Results may differ from the reference program's by a relative error of at most 0.0045.
Values sent between devices are 32-bit elements; how exact they have to be, the bound alone decides.
No kernel may reach another device: no remote copies, remote signals or barrier semaphores. Data moves between devices by JAX's collectives and lax.ppermute only.
A program may use at most 64 MiB of HBM per device.

```python
import jax
import jax.numpy as jnp
from jax import lax

D = 512
K = 8192
KC = 256
ROUNDS = 2
COARSE_ITERS = 3
ROWS = 65536


def shared_centroids(key):
    return jax.random.truncated_normal(key, -5.0, 5.0, (K, D), jnp.float32)


def draw_centroids(key, part):
    base = shared_centroids(key)
    return base


def draw_sketches(key, part):
    key = jax.random.fold_in(key, 12)
    values = jax.random.truncated_normal(key, -5.0, 5.0, (ROWS, D), jnp.float32)
    return values.astype(jnp.bfloat16)


def bell_draw(key, extent, width, bound, held_as=jnp.bfloat16):
    values = jax.random.normal(key, extent, jnp.float32) * width
    return jnp.minimum(jnp.maximum(values, -bound), bound).astype(held_as)


def setup_inputs(seed: int = 0) -> dict:
    keys = jax.random.split(jax.random.key(seed), 4)
    sketches = draw_sketches(jax.random.fold_in(keys[3], 71), 0)
    centroids = draw_centroids(jax.random.fold_in(keys[3], 71), 0)
    coarse_init = bell_draw(keys[2], (KC, D), 0.5, 4.0, jnp.float32)
    return dict(sketches=sketches, centroids=centroids, coarse_init=coarse_init)


def fine_round(sketches, cents):
    scale = D ** -0.5
    cb = cents.astype(jnp.bfloat16)
    half = 0.5 * scale * jnp.sum(cents * cents, axis=1)
    block_rows = min(2048, ROWS)
    blocks = sketches.reshape(ROWS // block_rows, block_rows, D)

    def step(carry, rows):
        sums, counts = carry
        scores = scale * lax.dot_general(rows, cb, (((1,), (1,)), ((), ())), preferred_element_type=jnp.float32) - half[None, :]
        top = jnp.max(scores, axis=1)
        lse = top + jnp.log(jnp.sum(jnp.exp(scores - top[:, None]), axis=1))
        probs = jnp.exp(scores - lse[:, None])
        sums = sums + lax.dot_general(probs.astype(jnp.bfloat16), rows, (((0,), (0,)), ((), ())), preferred_element_type=jnp.float32)
        counts = counts + jnp.sum(probs, axis=0)
        return (sums, counts), lse

    start = (jnp.zeros((K, D), jnp.float32), jnp.zeros((K,), jnp.float32))
    (sums, counts), lse = lax.scan(step, start, blocks)
    fresh = (sums + cents) / (counts + 1.0)[:, None]
    return fresh, counts, lse.reshape(ROWS)


def coarse_step(coarse, fine, counts):
    sharp = 4.0 * D ** -0.5
    inner = jnp.dot(fine, coarse.T, precision=lax.Precision.HIGHEST, preferred_element_type=jnp.float32)
    logits = sharp * (inner - 0.5 * jnp.sum(coarse * coarse, axis=1)[None, :])
    weights = counts[:, None] * jax.nn.softmax(logits, axis=1)
    totals = jnp.dot(weights.T, fine, precision=lax.Precision.HIGHEST, preferred_element_type=jnp.float32)
    mass = jnp.sum(weights, axis=0)
    return (totals + coarse) / (mass + 1.0)[:, None], mass


def reference(sketches, centroids, coarse_init):
    cents = centroids
    for round_index in range(ROUNDS):
        cents, counts, lse = fine_round(sketches, cents)
    coarse = coarse_init
    mass = jnp.zeros((KC,), jnp.float32)
    for iteration in range(COARSE_ITERS):
        coarse, mass = coarse_step(coarse, cents, counts)
    return cents, counts, coarse, mass * (K / ROWS), lse
```

```python
import jax
import jax.numpy as jnp
from jax import lax
from jax.sharding import PartitionSpec as P

ROUNDS = 2
COARSE_ITERS = 3


def swap(x, axis, bit):
    size = lax.axis_size(axis)
    return lax.ppermute(x, axis, [(i, i ^ bit) for i in range(size)])


def bits_of(size):
    return [1 << b for b in range(size.bit_length() - 1)]


def all_lse(x, axis):
    for bit in bits_of(lax.axis_size(axis)):
        other = swap(x, axis, bit)
        x = jnp.maximum(x, other) + jnp.log1p(jnp.exp(-jnp.abs(x - other)))
    return x


def all_sum(x, axis):
    for bit in bits_of(lax.axis_size(axis)):
        x = x + swap(x, axis, bit)
    return x


def scatter_sum(x, axis):
    size = lax.axis_size(axis)
    me = lax.axis_index(axis)
    x = x.reshape((1, size) + x.shape[1:])
    for bit in bits_of(size):
        remaining = x.shape[1]
        x = x.reshape((remaining // 2, 2) + x.shape[2:])
        mine = (me // bit) % 2
        keep = lax.dynamic_index_in_dim(x, mine, 1, keepdims=False)
        send = lax.dynamic_index_in_dim(x, 1 - mine, 1, keepdims=False)
        x = (keep + swap(send, axis, bit))[None]
    return x[0, 0]


def gather(x, axis):
    size = lax.axis_size(axis)
    me = lax.axis_index(axis)
    x = x[None]
    for bit in reversed(bits_of(size)):
        other = swap(x, axis, bit)
        low = (me // bit) % 2 == 0
        first = jnp.where(low, x, other)
        second = jnp.where(low, other, x)
        x = jnp.stack([first, second], axis=1).reshape((2 * x.shape[0],) + x.shape[1:])
    return x


def per_device(sketches, centroids, coarse_init):
    n_row = lax.axis_size("row")
    n_cent = lax.axis_size("cent")
    width = sketches.shape[1]
    local_k = centroids.shape[0]
    sub_k = local_k // n_row
    rows = sketches.shape[0]
    r = lax.axis_index("row")
    scale = width ** (-0.5)
    cents = centroids
    for round_index in range(ROUNDS):
        cb = cents.astype(jnp.bfloat16)
        half = 0.5 * scale * jnp.sum(cents * cents, axis=1)
        scores = (
            scale
            * lax.dot_general(
                sketches, cb, (((1,), (1,)), ((), ())), preferred_element_type=jnp.float32
            )
            - half[None, :]
        )
        local_top = jnp.max(scores, axis=1)
        local = local_top + jnp.log(jnp.sum(jnp.exp(scores - local_top[:, None]), axis=1))
        lse = all_lse(local, "cent")
        probs = jnp.exp(scores - lse[:, None])
        sums = lax.dot_general(
            probs.astype(jnp.bfloat16),
            sketches,
            (((0,), (0,)), ((), ())),
            preferred_element_type=jnp.float32,
        )
        counts = jnp.sum(probs, axis=0)
        packed = jnp.concatenate(
            [
                sums.reshape(n_row, sub_k, width),
                jnp.pad(counts.reshape(n_row, 1, sub_k), ((0, 0), (0, 0), (0, width - sub_k))),
            ],
            axis=1,
        )
        total = scatter_sum(packed, "row")
        my_counts = total[sub_k, :sub_k]
        old = lax.dynamic_slice_in_dim(cents, r * sub_k, sub_k, 0)
        fresh = (total[:sub_k] + old) / (my_counts + 1.0)[:, None]
        block = jnp.concatenate([fresh, total[sub_k:]], axis=0)
        gathered = gather(block, "row")
        cents = gathered[:, :sub_k].reshape(local_k, width)
        counts = gathered[:, sub_k, :sub_k].reshape(local_k)

    n_coarse = coarse_init.shape[0]
    sub_m = n_coarse // n_row
    sharp = 4.0 * width ** (-0.5)
    mine = lax.dynamic_slice_in_dim(coarse_init, r * sub_m, sub_m, 0)

    def logits_of(coarse):
        inner = jnp.dot(
            cents, coarse.T, precision=lax.Precision.HIGHEST, preferred_element_type=jnp.float32
        )
        return sharp * (inner - 0.5 * jnp.sum(coarse * coarse, axis=1)[None, :])

    for iteration in range(COARSE_ITERS):
        if iteration == 0:
            logits = logits_of(coarse_init)
            norm = jax.nn.logsumexp(logits, axis=1)
            logits = lax.dynamic_slice_in_dim(logits, r * sub_m, sub_m, 1)
        else:
            logits = logits_of(mine)
            norm = all_lse(jax.nn.logsumexp(logits, axis=1), "row")
        weights = counts[:, None] * jnp.exp(logits - norm[:, None])
        totals = lax.dot_general(
            weights,
            cents,
            (((0,), (0,)), ((), ())),
            precision=lax.Precision.HIGHEST,
            preferred_element_type=jnp.float32,
        )
        mass = jnp.sum(weights, axis=0)
        packed = jnp.concatenate([totals, jnp.broadcast_to(mass[:, None], (sub_m, 128))], axis=1)
        packed = all_sum(packed, "cent")
        mass = packed[:, width:]
        mine = (packed[:, :width] + mine) / (mass[:, :1] + 1.0)
    full = gather(jnp.concatenate([mine, mass], axis=1), "row")
    full = full.reshape(n_coarse, width + 128)
    coarse = full[:, :width]
    mass = full[:, width]
    all_rows = rows * n_row
    all_cents = local_k * n_cent
    return (cents, counts, coarse, mass * (all_cents / all_rows), lse)


def solution(mesh):
    in_specs = (P("row", None), P("cent", None), P())
    out_specs = (P("cent", None), P("cent"), P(), P(), P("row"))
    return jax.shard_map(
        per_device, mesh=mesh, in_specs=in_specs, out_specs=out_specs, check_vma=False
    )
```

```python
import functools
import math

import jax
import jax.numpy as jnp
from jax import lax
from jax.experimental import pallas as pl
from jax.experimental.pallas import tpu as pltpu
from jax.sharding import Mesh, PartitionSpec as P

ROUNDS = 2
COARSE_ITERS = 3
LANES = 128
TILES = 8


def swap(x, axis, bits):
    size = lax.axis_size(axis)
    return lax.ppermute(x, axis, [(i, i ^ bits) for i in range(size)])


def add_logs(a, b):
    return jnp.maximum(a, b) + jnp.log1p(jnp.exp(-jnp.abs(a - b)))


def reduce_four(x, axis, combine):
    far = swap(x, axis, 2)
    near = swap(x, axis, 1)
    wrap = swap(x, axis, 3)
    return combine(combine(x, far), combine(near, wrap))


def reduce_eight(x, axis, combine):
    x = combine(x, swap(x, axis, 1))
    far = swap(x, axis, 5)
    up = swap(x, axis, 2)
    down = swap(x, axis, 6)
    return combine(combine(x, up), combine(far, down))


def reduce_cent(x, combine):
    return reduce_eight(reduce_four(x, "y", combine), "z", combine)


def reduce_row(x, combine):
    return reduce_four(combine(x, swap(x, "core", 1)), "x", combine)


def score_tile(c_bf, half, x, factor):
    dots = lax.dot_general(c_bf, x, (((1,), (1,)), ((), ())), preferred_element_type=jnp.float32)
    dots = dots - half
    top = jnp.max(dots, axis=0, keepdims=True)
    exps = jnp.exp2((dots - top) * (factor * math.log2(math.e)))
    total = jnp.sum(exps, axis=0, keepdims=True)
    top = top * factor
    return exps, top, top + jnp.log(total)


def score_load_kernel(x_ref, c_ref, e_ref, xv_ref, top_ref, lse_ref, sems):
    tile = xv_ref.shape[0] // TILES
    factor = c_ref.shape[1] ** -0.5
    copies = [
        pltpu.make_async_copy(
            x_ref.at[pl.ds(i * tile, tile)], xv_ref.at[pl.ds(i * tile, tile)], sems.at[i]
        )
        for i in range(TILES)
    ]
    for copy in copies:
        copy.start()
    c = c_ref[...]
    c_bf = c.astype(jnp.bfloat16)
    half = 0.5 * jnp.sum(c * c, axis=1, keepdims=True)
    for i in range(TILES):
        copies[i].wait()
        exps, top, lse = score_tile(c_bf, half, xv_ref[i * tile : (i + 1) * tile, :], factor)
        e_ref[:, i * tile : (i + 1) * tile] = exps
        top_ref[i : i + 1, :] = top
        lse_ref[i : i + 1, :] = lse


def score_kernel(xv_ref, c_ref, e_ref, top_ref, lse_ref):
    tile = xv_ref.shape[0] // TILES
    factor = c_ref.shape[1] ** -0.5
    c = c_ref[...]
    c_bf = c.astype(jnp.bfloat16)
    half = 0.5 * jnp.sum(c * c, axis=1, keepdims=True)
    for i in range(TILES):
        exps, top, lse = score_tile(c_bf, half, xv_ref[i * tile : (i + 1) * tile, :], factor)
        e_ref[:, i * tile : (i + 1) * tile] = exps
        top_ref[i : i + 1, :] = top
        lse_ref[i : i + 1, :] = lse


def sums_kernel(core_ref, e_ref, xv_ref, top_ref, lse_ref, keep_ref, send_ref, sums_ref, counts_ref):
    tile = xv_ref.shape[0] // TILES
    local_k, width = sums_ref.shape
    nx = keep_ref.shape[0]
    sub_k = local_k // (2 * nx)
    counts = jnp.zeros((local_k, LANES), jnp.float32)
    for i in range(TILES):
        rows = slice(i * tile, (i + 1) * tile)
        scale = jnp.exp(top_ref[i : i + 1, :] - lse_ref[i : i + 1, :])
        p = e_ref[:, rows] * scale
        part = p[:, :LANES]
        for j in range(1, tile // LANES):
            part = part + p[:, j * LANES : (j + 1) * LANES]
        counts = counts + part
        dots = jnp.dot(p.astype(jnp.bfloat16), xv_ref[rows, :], preferred_element_type=jnp.float32)
        if i == 0:
            sums_ref[...] = dots
        else:
            sums_ref[...] += dots
    counts_ref[...] = jnp.broadcast_to(jnp.sum(counts, axis=1, keepdims=True), counts.shape)
    core = core_ref[0]
    lane = lax.broadcasted_iota(jnp.int32, (8, LANES), 1)
    for out, which in ((keep_ref, core), (send_ref, 1 - core)):
        for chip in range(nx):
            base = pl.multiple_of((chip * 2 + which) * sub_k, sub_k)
            for d in range(width // LANES):
                out[chip, d * sub_k : (d + 1) * sub_k, :] = sums_ref[
                    pl.ds(base, sub_k), d * LANES : (d + 1) * LANES
                ]
            packed = jnp.zeros((8, LANES), jnp.float32)
            for j in range(sub_k // 8):
                packed = jnp.where(lane == j, counts_ref[pl.ds(base + 8 * j, 8), :], packed)
            out[chip, (width // LANES) * sub_k :, :] = packed


def update_kernel(a_ref, b_ref, c_ref, d_ref, old_ref, out_ref):
    total = (a_ref[...] + b_ref[...]) + (c_ref[...] + d_ref[...])
    blocks, sub_k, _ = old_ref.shape
    counts = total[blocks * sub_k :, :]
    inverse = [
        1.0 / (jnp.broadcast_to(counts[:, j : j + 1], (8, LANES)) + 1.0) for j in range(sub_k // 8)
    ]
    for d in range(blocks):
        for j in range(sub_k // 8):
            at = d * sub_k + 8 * j
            out_ref[at : at + 8, :] = (
                total[at : at + 8, :] + old_ref[d, 8 * j : 8 * j + 8, :]
            ) * inverse[j]
    out_ref[blocks * sub_k :, :] = counts


def assemble_kernel(place_ref, mine_ref, theirs_ref, c_ref, counts_ref):
    local_k, width = c_ref.shape
    nx = mine_ref.shape[0]
    sub_k = local_k // (2 * nx)
    blocks = width // LANES
    chip, core = place_ref[0], place_ref[1]
    for ref, which in ((mine_ref, core), (theirs_ref, 1 - core)):
        for s in range(nx):
            base = pl.multiple_of((lax.bitwise_xor(chip, s) * 2 + which) * sub_k, sub_k)
            for d in range(blocks):
                c_ref[pl.ds(base, sub_k), d * LANES : (d + 1) * LANES] = ref[
                    s, d * sub_k : (d + 1) * sub_k, :
                ]
            for j in range(sub_k // 8):
                counts_ref[pl.ds(base + 8 * j, 8), :] = jnp.broadcast_to(
                    ref[s, blocks * sub_k :, j : j + 1], (8, LANES)
                )


def vmem():
    return pl.BlockSpec(memory_space=pltpu.VMEM)


def smem():
    return pl.BlockSpec(memory_space=pltpu.SMEM)


def struct(*shape, dtype=jnp.float32):
    return jax.ShapeDtypeStruct(shape, dtype)


def params():
    return pltpu.CompilerParams(vmem_limit_bytes=24 * 1024 * 1024)


def per_device(sketches, centroids, coarse_init):
    nx, nc = lax.axis_size("x"), lax.axis_size("core")
    ny, nz = lax.axis_size("y"), lax.axis_size("z")
    n_row, n_cent = nx * nc, ny * nz
    rows, width = sketches.shape
    local_k = centroids.shape[0]
    sub_k = local_k // n_row
    blocks = width // LANES
    packed_rows = blocks * sub_k + 8
    chip, core = lax.axis_index("x"), lax.axis_index("core")
    r = chip * nc + core
    place = jnp.stack([chip, core]).astype(jnp.int32)
    core_scalar = place[1:]
    tile = rows // TILES
    flops = 2 * rows * local_k * width

    cents = centroids
    held = None
    for round_index in range(ROUNDS):
        rows_out = [struct(TILES, tile), struct(TILES, tile)]
        exps_out = pltpu.VMEM((local_k, rows), jnp.float32)
        if round_index == 0:
            exps, held, top, local = pl.pallas_call(
                score_load_kernel,
                out_shape=[exps_out, pltpu.VMEM((rows, width), jnp.bfloat16)] + rows_out,
                in_specs=[pl.BlockSpec(memory_space=pl.ANY), vmem()],
                out_specs=[vmem()] * 4,
                scratch_shapes=[pltpu.SemaphoreType.DMA((TILES,))],
                compiler_params=params(),
                name="scores_first",
            )(pltpu.with_memory_space_constraint(sketches, pltpu.HBM), cents)
        else:
            exps, top, local = pl.pallas_call(
                score_kernel,
                out_shape=[exps_out] + rows_out,
                in_specs=[vmem()] * 2,
                out_specs=[vmem()] * 3,
                compiler_params=params(),
                name="scores",
            )(held, cents)
        lse = reduce_cent(local, add_logs)
        keep, send = pl.pallas_call(
            sums_kernel,
            out_shape=[struct(nx, packed_rows, LANES)] * 2,
            in_specs=[smem()] + [vmem()] * 4,
            out_specs=[vmem()] * 2,
            scratch_shapes=[
                pltpu.VMEM((local_k, width), jnp.float32),
                pltpu.VMEM((local_k, LANES), jnp.float32),
            ],
            compiler_params=params(),
            name="sums",
        )(core_scalar, exps, held, top, lse)
        half = keep + swap(send, "core", 1)
        chunks = [lax.dynamic_index_in_dim(half, chip ^ s, 0, keepdims=False) for s in range(nx)]
        far = swap(chunks[2], "x", 2)
        near = swap(chunks[1], "x", 1)
        wrap = swap(chunks[3], "x", 3)
        old = lax.dynamic_slice_in_dim(cents, r * sub_k, sub_k, 0)
        old = old.reshape(sub_k, blocks, LANES).transpose(1, 0, 2)
        block = pl.pallas_call(
            update_kernel,
            out_shape=struct(packed_rows, LANES),
            in_specs=[vmem()] * 5,
            out_specs=vmem(),
            compiler_params=params(),
            name="update",
        )(chunks[0], far, near, wrap, old)
        far = swap(block, "x", 2)
        near = swap(block, "x", 1)
        wrap = swap(block, "x", 3)
        mine = jnp.stack([block, near, far, wrap])
        theirs = swap(mine, "core", 1)
        cents, counts = pl.pallas_call(
            assemble_kernel,
            out_shape=[struct(local_k, width), struct(local_k, LANES)],
            in_specs=[smem()] + [vmem()] * 2,
            out_specs=[vmem()] * 2,
            compiler_params=params(),
            name="assemble",
        )(place, mine, theirs)
    counts = counts[:, 0]

    n_coarse = coarse_init.shape[0]
    sub_m = n_coarse // n_row
    sharp = 4.0 * width ** (-0.5)
    mine = lax.dynamic_slice_in_dim(coarse_init, r * sub_m, sub_m, 0)

    def logits_of(coarse):
        inner = jnp.dot(
            cents, coarse.T, precision=lax.Precision.HIGHEST, preferred_element_type=jnp.float32
        )
        return sharp * (inner - 0.5 * jnp.sum(coarse * coarse, axis=1)[None, :])

    for iteration in range(COARSE_ITERS):
        if iteration == 0:
            logits = logits_of(coarse_init)
            norm = jax.nn.logsumexp(logits, axis=1)
            logits = lax.dynamic_slice_in_dim(logits, r * sub_m, sub_m, 1)
        else:
            logits = logits_of(mine)
            norm = reduce_row(jax.nn.logsumexp(logits, axis=1), add_logs)
        weights = counts[:, None] * jnp.exp(logits - norm[:, None])
        totals = lax.dot_general(
            weights,
            cents,
            (((0,), (0,)), ((), ())),
            precision=lax.Precision.HIGHEST,
            preferred_element_type=jnp.float32,
        )
        mass = jnp.sum(weights, axis=0)
        packed = jnp.concatenate([totals, jnp.broadcast_to(mass[:, None], (sub_m, LANES))], axis=1)
        packed = reduce_cent(packed, jnp.add)
        mass = packed[:, width:]
        mine = (packed[:, :width] + mine) / (mass[:, :1] + 1.0)

    mine = jnp.concatenate([mine, mass], axis=1)
    far = swap(mine, "x", 2)
    near = swap(mine, "x", 1)
    wrap = swap(mine, "x", 3)
    mine = jnp.stack([mine, near, far, wrap])
    theirs = swap(mine, "core", 1)
    full = jnp.zeros((nx, nc) + mine.shape[1:], jnp.float32)
    first = jnp.where(core == 0, mine, theirs)
    second = jnp.where(core == 0, theirs, mine)
    full = jnp.stack([first, second], axis=1)
    full = jnp.stack(
        [lax.dynamic_index_in_dim(full, chip ^ s, 0, keepdims=False) for s in range(nx)]
    )
    full = full.reshape(n_coarse, width + LANES)
    coarse = full[:, :width]
    mass = full[:, width]
    all_rows = rows * n_row
    all_cents = local_k * n_cent
    return (cents, counts, coarse, mass * (all_cents / all_rows), lse.reshape(rows))


def solution(mesh):
    n_row, n_cent = mesh.shape["row"], mesh.shape["cent"]
    fine = Mesh(mesh.devices.reshape(n_row // 2, 2, n_cent // 8, 8), ("x", "core", "y", "z"))
    row, cent = ("x", "core"), ("y", "z")
    in_specs = (P(row, None), P(cent, None), P())
    out_specs = (P(cent, None), P(cent), P(), P(), P(row))
    return jax.shard_map(
        per_device, mesh=fine, in_specs=in_specs, out_specs=out_specs, check_vma=False
    )
```

```python
import functools
import math

import jax
import jax.numpy as jnp
from jax import lax
from jax.experimental import pallas as pl
from jax.experimental.pallas import tpu as pltpu
from jax.sharding import Mesh, PartitionSpec as P

ROUNDS = 2
COARSE_ITERS = 3
LANES = 128
TILES = 8
WINDOW = 3
SUB = 32


def swap(x, axis, bits):
    size = lax.axis_size(axis)
    return lax.ppermute(x, axis, [(i, i ^ bits) for i in range(size)])


def add_logs(a, b):
    return jnp.maximum(a, b) + jnp.log1p(jnp.exp(-jnp.abs(a - b)))


def burst(chunks, axis):
    near = swap(chunks[1], axis, 1)
    wrap = swap(chunks[3], axis, 3)
    far = swap(chunks[2], axis, 2)
    return near, far, wrap


def reduce_four(x, axis, combine):
    near, far, wrap = burst([x] * 4, axis)
    return combine(combine(x, far), combine(near, wrap))


def reduce_four_near(x, axis, combine):
    x = combine(x, swap(x, axis, 1))
    return combine(x, swap(x, axis, 3))


def reduce_eight(x, axis, combine):
    x = combine(x, swap(x, axis, 1))
    up = swap(x, axis, 2)
    down = swap(x, axis, 6)
    far = swap(x, axis, 5)
    return combine(combine(x, up), combine(far, down))


def reduce_row(x, combine):
    return reduce_four(combine(x, swap(x, "core", 1)), "x", combine)


def score_tile(c_bf, half, x, factor):
    dots = lax.dot_general(c_bf, x, (((1,), (1,)), ((), ())), preferred_element_type=jnp.float32)
    dots = dots - half
    top = jnp.max(dots, axis=0, keepdims=True)
    exps = jnp.exp2((dots - top) * (factor * math.log2(math.e)))
    total = jnp.sum(exps, axis=0, keepdims=True)
    top = top * factor
    return exps, top, top + jnp.log(total)


def score_load_kernel(place_ref, x_ref, c_ref, e_ref, xv_ref, cv_ref, top_ref, lse_ref, sems, c_sem):
    tile = xv_ref.shape[0] // TILES
    factor = c_ref.shape[1] ** -0.5
    c_copy = pltpu.make_async_copy(c_ref, cv_ref, c_sem)
    c_copy.start()
    copies = [
        pltpu.make_async_copy(
            x_ref.at[pl.ds(i * tile, tile)], xv_ref.at[pl.ds(i * tile, tile)], sems.at[i]
        )
        for i in range(TILES)
    ]
    for copy in copies[:WINDOW]:
        copy.start()
    c_copy.wait()
    c = cv_ref[...]
    c_bf = c.astype(jnp.bfloat16)
    half = 0.5 * jnp.sum(c * c, axis=1, keepdims=True)
    for i in range(TILES):
        copies[i].wait()
        if i + WINDOW < TILES:
            copies[i + WINDOW].start()
        exps, top, lse = score_tile(c_bf, half, xv_ref[i * tile : (i + 1) * tile, :], factor)
        e_ref[:, i * tile : (i + 1) * tile] = exps
        top_ref[i : i + 1, :] = top
        lse_ref[i : i + 1, :] = lse


def score_kernel(xv_ref, c_ref, e_ref, top_ref, lse_ref):
    tile = xv_ref.shape[0] // TILES
    factor = c_ref.shape[1] ** -0.5
    c = c_ref[...]
    c_bf = c.astype(jnp.bfloat16)
    half = 0.5 * jnp.sum(c * c, axis=1, keepdims=True)
    for i in range(TILES):
        exps, top, lse = score_tile(c_bf, half, xv_ref[i * tile : (i + 1) * tile, :], factor)
        e_ref[:, i * tile : (i + 1) * tile] = exps
        top_ref[i : i + 1, :] = top
        lse_ref[i : i + 1, :] = lse


def pack_column(ref, base, sub):
    lane = lax.broadcasted_iota(jnp.int32, (8, LANES), 1)
    packed = jnp.zeros((8, LANES), jnp.float32)
    for j in range(sub // 8):
        packed = jnp.where(lane == j, ref[pl.ds(base + 8 * j, 8), :], packed)
    return packed


def sums_kernel(place_ref, e_ref, xv_ref, top_ref, lse_ref, keep_ref, send_ref, sums_ref, counts_ref):
    tile = xv_ref.shape[0] // TILES
    local_k, width = sums_ref.shape
    nx = keep_ref.shape[0]
    sub_k = local_k // (2 * nx)
    counts = jnp.zeros((local_k, LANES), jnp.float32)
    for i in range(TILES):
        rows = slice(i * tile, (i + 1) * tile)
        scale = jnp.exp(top_ref[i : i + 1, :] - lse_ref[i : i + 1, :])
        p = e_ref[:, rows] * scale
        part = p[:, :LANES]
        for j in range(1, tile // LANES):
            part = part + p[:, j * LANES : (j + 1) * LANES]
        counts = counts + part
        dots = jnp.dot(p.astype(jnp.bfloat16), xv_ref[rows, :], preferred_element_type=jnp.float32)
        if i == 0:
            sums_ref[...] = dots
        else:
            sums_ref[...] += dots
    counts_ref[...] = jnp.broadcast_to(jnp.sum(counts, axis=1, keepdims=True), counts.shape)
    core = place_ref[1]
    for out, which in ((keep_ref, core), (send_ref, 1 - core)):
        for chip in range(nx):
            base = pl.multiple_of((chip * 2 + which) * sub_k, sub_k)
            for d in range(width // LANES):
                out[chip, d * sub_k : (d + 1) * sub_k, :] = sums_ref[
                    pl.ds(base, sub_k), d * LANES : (d + 1) * LANES
                ]
            out[chip, (width // LANES) * sub_k :, :] = pack_column(counts_ref, base, sub_k)


def chunks_kernel(place_ref, keep_ref, got_ref, *out_refs):
    for s, out in enumerate(out_refs):
        chip = lax.bitwise_xor(place_ref[0], s)
        out[...] = keep_ref[chip] + got_ref[chip]


def updated(total, old):
    blocks, sub = len(old), old[0].shape[0]
    counts = total[blocks * sub :, :]
    parts = []
    for d in range(blocks):
        for j in range(sub // 8):
            at = d * sub + 8 * j
            under = jnp.broadcast_to(counts[:, j : j + 1], (8, LANES)) + 1.0
            parts.append((total[at : at + 8, :] + old[d][8 * j : 8 * j + 8, :]) / under)
    return jnp.concatenate(parts, axis=0), counts


def update_kernel(place_ref, a_ref, b_ref, c_ref, d_ref, old_ref, out_ref):
    total = (a_ref[...] + b_ref[...]) + (c_ref[...] + d_ref[...])
    local_k, width = old_ref.shape
    blocks = width // LANES
    sub = (total.shape[0] - 8) // blocks
    base = pl.multiple_of((place_ref[0] * 2 + place_ref[1]) * sub, sub)
    old = [old_ref[pl.ds(base, sub), d * LANES : (d + 1) * LANES] for d in range(blocks)]
    fresh, counts = updated(total, old)
    out_ref[: blocks * sub, :] = fresh
    out_ref[blocks * sub :, :] = counts


def assemble_kernel(place_ref, mine_ref, theirs_ref, c_ref, row_ref, counts_ref):
    local_k, width = c_ref.shape
    nx = mine_ref.shape[0]
    sub_k = local_k // (2 * nx)
    blocks = width // LANES
    chip, core = place_ref[0], place_ref[1]
    for ref, which in ((mine_ref, core), (theirs_ref, 1 - core)):
        for s in range(nx):
            base = pl.multiple_of((lax.bitwise_xor(chip, s) * 2 + which) * sub_k, sub_k)
            for d in range(blocks):
                c_ref[pl.ds(base, sub_k), d * LANES : (d + 1) * LANES] = ref[
                    s, d * sub_k : (d + 1) * sub_k, :
                ]
            for j in range(sub_k // 8):
                counts_ref[pl.ds(base + 8 * j, 8), :] = jnp.broadcast_to(
                    ref[s, blocks * sub_k :, j : j + 1], (8, LANES)
                )
    row_ref[...] = jnp.transpose(counts_ref[...])[:1, :]


def coarse_logits(g, f):
    inner = lax.dot_general(
        g,
        f,
        (((1,), (1,)), ((), ())),
        precision=lax.Precision.HIGHEST,
        preferred_element_type=jnp.float32,
    )
    sharp = 4.0 * g.shape[1] ** -0.5
    return sharp * (inner - 0.5 * jnp.sum(g * g, axis=1, keepdims=True))


def column_lse(logits):
    top = jnp.max(logits, axis=0, keepdims=True)
    return top + jnp.log(jnp.sum(jnp.exp(logits - top), axis=0, keepdims=True))


def weigh(logits, norm, row, f, out_ref, mass_ref):
    weights = row * jnp.exp(logits - norm)
    totals = lax.dot_general(
        weights,
        f,
        (((1,), (0,)), ((), ())),
        precision=lax.Precision.HIGHEST,
        preferred_element_type=jnp.float32,
    )
    sub, width = totals.shape
    blocks = width // LANES
    for d in range(blocks):
        out_ref[d * sub : (d + 1) * sub, :] = totals[:, d * LANES : (d + 1) * LANES]
    mass_ref[...] = jnp.broadcast_to(jnp.sum(weights, axis=1, keepdims=True), (sub, LANES))
    out_ref[blocks * sub :, :] = pack_column(mass_ref, 0, sub)


def coarse_first_kernel(place_ref, f_ref, row_ref, g_ref, out_ref, logits_ref, mass_ref):
    f = f_ref[...]
    logits = coarse_logits(g_ref[...], f)
    logits_ref[...] = logits
    sub = mass_ref.shape[0]
    base = pl.multiple_of((place_ref[0] * 2 + place_ref[1]) * sub, sub)
    weigh(logits_ref[pl.ds(base, sub), :], column_lse(logits), row_ref[...], f, out_ref, mass_ref)


def read_old(place_ref, old_ref, sub, blocks):
    if old_ref.shape[1] == LANES:
        return [old_ref[d * sub : (d + 1) * sub, :] for d in range(blocks)]
    base = pl.multiple_of((place_ref[0] * 2 + place_ref[1]) * sub, sub)
    return [old_ref[pl.ds(base, sub), d * LANES : (d + 1) * LANES] for d in range(blocks)]


def coarse_logits_kernel(place_ref, total_ref, old_ref, f_ref, g_ref, logits_ref, lse_ref):
    blocks = f_ref.shape[1] // LANES
    sub = logits_ref.shape[0]
    fresh, _ = updated(total_ref[...], read_old(place_ref, old_ref, sub, blocks))
    g_ref[...] = fresh
    g = jnp.concatenate([fresh[d * sub : (d + 1) * sub, :] for d in range(blocks)], axis=1)
    logits = coarse_logits(g, f_ref[...])
    logits_ref[...] = logits
    lse_ref[...] = column_lse(logits)


def coarse_weights_kernel(logits_ref, norm_ref, row_ref, f_ref, out_ref, mass_ref):
    weigh(logits_ref[...], norm_ref[...], row_ref[...], f_ref[...], out_ref, mass_ref)


def coarse_last_kernel(total_ref, old_ref, out_ref):
    sub = SUB
    blocks = old_ref.shape[0] // sub
    fresh, mass = updated(total_ref[...], [old_ref[d * sub : (d + 1) * sub, :] for d in range(blocks)])
    out_ref[: blocks * sub, :] = fresh
    out_ref[blocks * sub :, :] = mass


def vmem():
    return pl.BlockSpec(memory_space=pltpu.VMEM)


def smem():
    return pl.BlockSpec(memory_space=pltpu.SMEM)


def struct(*shape, dtype=jnp.float32):
    return jax.ShapeDtypeStruct(shape, dtype)


def kernel_call(body, out_shape, name, scratch=(), smem_first=True, in_hbm=0, n_in=0):
    specs = [smem()] if smem_first else []
    specs += [pl.BlockSpec(memory_space=pl.ANY)] * in_hbm
    specs += [vmem()] * (n_in - len(specs))
    return pl.pallas_call(
        body,
        out_shape=out_shape,
        in_specs=specs,
        out_specs=jax.tree.map(lambda _: vmem(), out_shape, is_leaf=lambda o: hasattr(o, "shape")),
        scratch_shapes=list(scratch),
        compiler_params=pltpu.CompilerParams(vmem_limit_bytes=24 * 1024 * 1024),
        name=name,
    )


def gather_row(block):
    near, far, wrap = burst([block] * 4, "x")
    mine = jnp.stack([block, near, far, wrap])
    return mine, swap(mine, "core", 1)


def per_device(sketches, centroids, coarse_init):
    nx, nc = lax.axis_size("x"), lax.axis_size("core")
    ny, nz = lax.axis_size("y"), lax.axis_size("z")
    n_row, n_cent = nx * nc, ny * nz
    rows, width = sketches.shape
    local_k = centroids.shape[0]
    packed_rows = width // LANES * SUB + 8
    tile = rows // TILES
    place = jnp.stack([lax.axis_index("x"), lax.axis_index("core")]).astype(jnp.int32)

    block = struct(packed_rows, LANES)
    column = pltpu.VMEM((local_k, LANES), jnp.float32)
    exps_out = pltpu.VMEM((local_k, rows), jnp.float32)
    cents_out = pltpu.VMEM((local_k, width), jnp.float32)
    rows_out = [struct(TILES, tile), struct(TILES, tile)]

    def assemble(gathered, out, name):
        return kernel_call(
            assemble_kernel, [out, struct(1, local_k)], name, scratch=[column], n_in=3
        )(place, *gathered)

    for round_index in range(ROUNDS):
        if round_index == 0:
            exps, held, cents, top, local = kernel_call(
                score_load_kernel,
                [exps_out, pltpu.VMEM((rows, width), jnp.bfloat16), cents_out] + rows_out,
                "scores_first",
                scratch=[pltpu.SemaphoreType.DMA((TILES,)), pltpu.SemaphoreType.DMA],
                in_hbm=2,
                n_in=3,
            )(
                place,
                pltpu.with_memory_space_constraint(sketches, pltpu.HBM),
                pltpu.with_memory_space_constraint(centroids, pltpu.HBM),
            )
        else:
            exps, top, local = kernel_call(
                score_kernel, [exps_out] + rows_out, "scores", smem_first=False, n_in=2
            )(held, cents)
        lse = reduce_eight(reduce_four(local, "y", add_logs), "z", add_logs)
        keep, send = kernel_call(
            sums_kernel,
            [struct(nx, packed_rows, LANES)] * 2,
            "sums",
            scratch=[pltpu.VMEM((local_k, width), jnp.float32), column],
            n_in=5,
        )(place, exps, held, top, lse)
        chunks = kernel_call(chunks_kernel, [block] * nx, "chunks", n_in=3)(
            place, keep, swap(send, "core", 1)
        )
        near, far, wrap = burst(chunks, "x")
        fresh = kernel_call(update_kernel, block, "update", n_in=6)(
            place, chunks[0], far, near, wrap, cents
        )
        cents, row = assemble(gather_row(fresh), cents_out, "assemble")

    for iteration in range(COARSE_ITERS):
        mass = pltpu.VMEM((SUB, LANES), jnp.float32)
        if iteration == 0:
            packed = kernel_call(
                coarse_first_kernel,
                block,
                "coarse_first",
                scratch=[pltpu.VMEM((coarse_init.shape[0], local_k), jnp.float32), mass],
                n_in=4,
            )(place, cents, row, coarse_init)
            old = coarse_init
        else:
            old, logits, local = kernel_call(
                coarse_logits_kernel,
                [struct(packed_rows - 8, LANES), struct(SUB, local_k), struct(1, local_k)],
                "coarse_logits",
                n_in=4,
            )(place, packed, old, cents)
            norm = reduce_row(local, add_logs)
            packed = kernel_call(
                coarse_weights_kernel, block, "coarse_weights", scratch=[mass], smem_first=False, n_in=4
            )(logits, norm, row, cents)
        packed = reduce_four_near(packed, "y", jnp.add)
        packed = reduce_eight(packed, "z", jnp.add)
    last = kernel_call(coarse_last_kernel, block, "coarse_last", smem_first=False, n_in=2)(packed, old)
    coarse, mass = assemble(gather_row(last), struct(local_k, width), "assemble_coarse")
    all_rows = rows * n_row
    all_cents = local_k * n_cent
    return (
        cents + 0.0,
        row.reshape(local_k),
        coarse,
        mass.reshape(local_k) * (all_cents / all_rows),
        lse.reshape(rows),
    )


def solution(mesh):
    n_row, n_cent = mesh.shape["row"], mesh.shape["cent"]
    fine = Mesh(mesh.devices.reshape(n_row // 2, 2, n_cent // 8, 8), ("x", "core", "y", "z"))
    row, cent = ("x", "core"), ("y", "z")
    in_specs = (P(row, None), P(cent, None), P())
    out_specs = (P(cent, None), P(cent), P(), P(), P(row))
    return jax.shard_map(
        per_device, mesh=fine, in_specs=in_specs, out_specs=out_specs, check_vma=False
    )
```

```python
import functools
import math

import jax
import jax.numpy as jnp
from jax import lax
from jax.experimental import pallas as pl
from jax.experimental.pallas import tpu as pltpu
from jax.sharding import Mesh, PartitionSpec as P

ROUNDS = 2
COARSE_ITERS = 3
LANES = 128
TILES = 8
WINDOW = 3
LOADS = 8
SUB = 32


def swap(x, axis, bits):
    size = lax.axis_size(axis)
    return lax.ppermute(x, axis, [(i, i ^ bits) for i in range(size)])


def add_logs(a, b):
    return jnp.maximum(a, b) + jnp.log1p(jnp.exp(-jnp.abs(a - b)))


def burst(chunks, axis):
    near = swap(chunks[1], axis, 1)
    wrap = swap(chunks[3], axis, 3)
    far = swap(chunks[2], axis, 2)
    return near, far, wrap


def burst(x, axis, order):
    return [swap(x, axis, bits) for bits in order]


def partners(axis):
    return (6, 2, 5) if axis == "z" else (3, 1, 2)


def four(combine, far, one, two, x):
    return combine(combine(x, far), combine(one, two))


def four_z(combine, far, one, two, x):
    return combine(combine(x, one), combine(far, two))


def score_tile(c_bf, half, x, factor):
    dots = lax.dot_general(c_bf, x, (((1,), (1,)), ((), ())), preferred_element_type=jnp.float32)
    dots = dots - half
    top = jnp.max(dots, axis=0, keepdims=True)
    exps = jnp.exp2((dots - top) * (factor * math.log2(math.e)))
    total = jnp.sum(exps, axis=0, keepdims=True)
    top = top * factor
    return exps, top, top + jnp.log(total)


def score_load_kernel(x_ref, c_ref, e_ref, xv_ref, cv_ref, top_ref, lse_ref, sems, c_sem):
    tile = xv_ref.shape[0] // TILES
    step = tile // LOADS
    factor = c_ref.shape[1] ** -0.5
    c_copy = pltpu.make_async_copy(c_ref, cv_ref, c_sem)
    c_copy.start()
    copies = [
        pltpu.make_async_copy(
            x_ref.at[pl.ds(i * step, step)], xv_ref.at[pl.ds(i * step, step)], sems.at[i]
        )
        for i in range(TILES * LOADS)
    ]
    for copy in copies[: WINDOW * LOADS]:
        copy.start()
    c_copy.wait()
    c = cv_ref[...]
    c_bf = c.astype(jnp.bfloat16)
    half = 0.5 * jnp.sum(c * c, axis=1, keepdims=True)
    for i in range(TILES):
        for copy in copies[i * LOADS : (i + 1) * LOADS]:
            copy.wait()
        for copy in copies[(i + WINDOW) * LOADS : (i + WINDOW + 1) * LOADS]:
            copy.start()
        exps, top, lse = score_tile(c_bf, half, xv_ref[i * tile : (i + 1) * tile, :], factor)
        e_ref[:, i * tile : (i + 1) * tile] = exps
        top_ref[i : i + 1, :] = top
        lse_ref[i : i + 1, :] = lse


def score_kernel(xv_ref, mine_ref, theirs_ref, e_ref, cv_ref, top_ref, lse_ref):
    tile = xv_ref.shape[0] // TILES
    factor = cv_ref.shape[1] ** -0.5
    place_halves(mine_ref, theirs_ref, cv_ref)
    c = cv_ref[...]
    c_bf = c.astype(jnp.bfloat16)
    half = 0.5 * jnp.sum(c * c, axis=1, keepdims=True)
    for i in range(TILES):
        exps, top, lse = score_tile(c_bf, half, xv_ref[i * tile : (i + 1) * tile, :], factor)
        e_ref[:, i * tile : (i + 1) * tile] = exps
        top_ref[i : i + 1, :] = top
        lse_ref[i : i + 1, :] = lse


def pack_column(ref, base, sub):
    lane = lax.broadcasted_iota(jnp.int32, (8, LANES), 1)
    packed = jnp.zeros((8, LANES), jnp.float32)
    for j in range(sub // 8):
        packed = jnp.where(lane == j, ref[pl.ds(base + 8 * j, 8), :], packed)
    return packed


def combine_lse_kernel(two_ref, one_ref, far_ref, x_ref, out_ref):
    out_ref[...] = four(add_logs, far_ref[...], one_ref[...], two_ref[...], x_ref[...])


def combine_sum_kernel(two_ref, one_ref, far_ref, x_ref, out_ref):
    out_ref[...] = four(jnp.add, far_ref[...], one_ref[...], two_ref[...], x_ref[...])


def sums_kernel(
    two_ref, one_ref, far_ref, part_ref, e_ref, xv_ref, top_ref,
    keep_ref, send_ref, lse_ref, sums_ref, counts_ref,
):
    tile = xv_ref.shape[0] // TILES
    local_k, width = sums_ref.shape
    parts = keep_ref.shape[0]
    sub = local_k // (2 * parts)
    lse = four_z(add_logs, far_ref[...], one_ref[...], two_ref[...], part_ref[...])
    lse_ref[...] = lse
    scales = jnp.exp(top_ref[...] - lse)
    counts = jnp.zeros((local_k, LANES), jnp.float32)
    for i in range(TILES):
        rows = slice(i * tile, (i + 1) * tile)
        p = e_ref[:, rows] * scales[i : i + 1, :]
        part = p[:, :LANES]
        for j in range(1, tile // LANES):
            part = part + p[:, j * LANES : (j + 1) * LANES]
        counts = counts + part
        dots = jnp.dot(p.astype(jnp.bfloat16), xv_ref[rows, :], preferred_element_type=jnp.float32)
        if i == 0:
            sums_ref[...] = dots
        else:
            sums_ref[...] += dots
    counts_ref[...] = jnp.broadcast_to(jnp.sum(counts, axis=1, keepdims=True), counts.shape)
    core = lax.axis_index("core")
    for out, which in ((keep_ref, core), (send_ref, 1 - core)):
        for h in range(parts):
            base = pl.multiple_of((which * parts + h) * sub, sub)
            for d in range(width // LANES):
                out[h, d * sub : (d + 1) * sub, :] = sums_ref[
                    pl.ds(base, sub), d * LANES : (d + 1) * LANES
                ]
            out[h, (width // LANES) * sub :, :] = pack_column(counts_ref, base, sub)


def halves_kernel(keep_ref, got_ref, a_ref, b_ref):
    a_ref[...] = keep_ref[0] + got_ref[0]
    b_ref[...] = keep_ref[1] + got_ref[1]


def updated(total, old):
    blocks, sub = len(old), old[0].shape[0]
    counts = total[blocks * sub :, :]
    under = [jnp.broadcast_to(counts[:, j : j + 1], (8, LANES)) + 1.0 for j in range(sub // 8)]
    parts = []
    for d in range(blocks):
        for j in range(sub // 8):
            at = d * sub + 8 * j
            parts.append((total[at : at + 8, :] + old[d][8 * j : 8 * j + 8, :]) / under[j])
    return jnp.concatenate(parts, axis=0), counts


def update_kernel(a_ref, a_got_ref, b_ref, b_got_ref, old_ref, out_ref):
    local_k, width = old_ref.shape
    blocks = width // LANES
    sub = local_k // 4
    core = lax.axis_index("core")
    for h, (ref, got_ref) in enumerate(((a_ref, a_got_ref), (b_ref, b_got_ref))):
        base = pl.multiple_of((core * 2 + h) * sub, sub)
        old = [old_ref[pl.ds(base, sub), d * LANES : (d + 1) * LANES] for d in range(blocks)]
        fresh, counts = updated(ref[...] + got_ref[...], old)
        out_ref[h, : blocks * sub, :] = fresh
        out_ref[h, blocks * sub :, :] = counts


def place_halves(mine_ref, theirs_ref, c_ref, counts_ref=None):
    local_k, width = c_ref.shape
    blocks = width // LANES
    sub = local_k // 4
    core = lax.axis_index("core")
    for ref, which in ((mine_ref, core), (theirs_ref, 1 - core)):
        for h in range(2):
            base = pl.multiple_of((which * 2 + h) * sub, sub)
            for d in range(blocks):
                c_ref[pl.ds(base, sub), d * LANES : (d + 1) * LANES] = ref[
                    h, d * sub : (d + 1) * sub, :
                ]
            if counts_ref is not None:
                for j in range(sub // 8):
                    counts_ref[pl.ds(base + 8 * j, 8), :] = jnp.broadcast_to(
                        ref[h, blocks * sub :, j : j + 1], (8, LANES)
                    )


def coarse_logits(g, f):
    inner = lax.dot_general(
        g,
        f,
        (((1,), (1,)), ((), ())),
        precision=lax.Precision.HIGHEST,
        preferred_element_type=jnp.float32,
    )
    sharp = 4.0 * g.shape[1] ** -0.5
    return sharp * (inner - 0.5 * jnp.sum(g * g, axis=1, keepdims=True))


def column_lse(logits):
    top = jnp.max(logits, axis=0, keepdims=True)
    return top + jnp.log(jnp.sum(jnp.exp(logits - top), axis=0, keepdims=True))


def weigh(logits, norm, row, f, out_ref, mass_ref):
    weights = row * jnp.exp(logits - norm)
    totals = lax.dot_general(
        weights,
        f,
        (((1,), (0,)), ((), ())),
        precision=lax.Precision.HIGHEST,
        preferred_element_type=jnp.float32,
    )
    sub, width = totals.shape
    blocks = width // LANES
    for d in range(blocks):
        out_ref[d * sub : (d + 1) * sub, :] = totals[:, d * LANES : (d + 1) * LANES]
    mass_ref[...] = jnp.broadcast_to(jnp.sum(weights, axis=1, keepdims=True), (sub, LANES))
    out_ref[blocks * sub :, :] = pack_column(mass_ref, 0, sub)


def coarse_base():
    return pl.multiple_of((lax.axis_index("x") * 2 + lax.axis_index("core")) * SUB, SUB)


def coarse_first_kernel(
    mine_ref, theirs_ref, g_ref, out_ref, f_ref, row_ref, counts_ref, logits_ref, mass_ref
):
    place_halves(mine_ref, theirs_ref, f_ref, counts_ref)
    row = jnp.transpose(counts_ref[...])[:1, :]
    row_ref[...] = row
    f = f_ref[...]
    logits = coarse_logits(g_ref[...], f)
    logits_ref[...] = logits
    weigh(logits_ref[pl.ds(coarse_base(), SUB), :], column_lse(logits), row, f, out_ref, mass_ref)


def read_old(old_ref):
    if old_ref.shape[1] == LANES:
        return [old_ref[at : at + SUB, :] for at in range(0, old_ref.shape[0], SUB)]
    base = coarse_base()
    return [old_ref[pl.ds(base, SUB), at : at + LANES] for at in range(0, old_ref.shape[1], LANES)]


def coarse_logits_kernel(
    two_ref, one_ref, far_ref, part_ref, old_ref, f_ref, g_ref, logits_ref, lse_ref
):
    total = four_z(jnp.add, far_ref[...], one_ref[...], two_ref[...], part_ref[...])
    fresh, _ = updated(total, read_old(old_ref))
    g_ref[...] = fresh
    g = jnp.concatenate([fresh[at : at + SUB, :] for at in range(0, fresh.shape[0], SUB)], axis=1)
    logits = coarse_logits(g, f_ref[...])
    logits_ref[...] = logits
    lse_ref[...] = column_lse(logits)


def coarse_weights_kernel(
    two_ref, one_ref, far_ref, part_ref, logits_ref, row_ref, f_ref, out_ref, mass_ref
):
    norm = four(add_logs, far_ref[...], one_ref[...], two_ref[...], part_ref[...])
    weigh(logits_ref[...], norm, row_ref[...], f_ref[...], out_ref, mass_ref)


def coarse_last_kernel(two_ref, one_ref, far_ref, part_ref, old_ref, out_ref):
    total = four_z(jnp.add, far_ref[...], one_ref[...], two_ref[...], part_ref[...])
    fresh, mass = updated(total, read_old(old_ref))
    out_ref[: fresh.shape[0], :] = fresh
    out_ref[fresh.shape[0] :, :] = mass


def stack_kernel(two_ref, one_ref, far_ref, x_ref, out_ref):
    for s, ref in enumerate((x_ref, one_ref, far_ref, two_ref)):
        out_ref[s] = ref[...]


def assemble_kernel(mine_ref, theirs_ref, g_ref, row_ref, counts_ref):
    width = g_ref.shape[1]
    blocks = width // LANES
    chip, core = lax.axis_index("x"), lax.axis_index("core")
    for ref, which in ((mine_ref, core), (theirs_ref, 1 - core)):
        for s in range(mine_ref.shape[0]):
            base = pl.multiple_of((lax.bitwise_xor(chip, s) * 2 + which) * SUB, SUB)
            for d in range(blocks):
                g_ref[pl.ds(base, SUB), d * LANES : (d + 1) * LANES] = ref[
                    s, d * SUB : (d + 1) * SUB, :
                ]
            for j in range(SUB // 8):
                counts_ref[pl.ds(base + 8 * j, 8), :] = jnp.broadcast_to(
                    ref[s, blocks * SUB :, j : j + 1], (8, LANES)
                )
    row_ref[...] = jnp.transpose(counts_ref[...])[:1, :]


def struct(*shape, dtype=jnp.float32):
    return jax.ShapeDtypeStruct(shape, dtype)


def kernel_call(body, out_shape, name, n_in, scratch=(), in_hbm=0):
    many = isinstance(out_shape, list)
    spec = pl.BlockSpec(memory_space=pltpu.VMEM)
    return pl.pallas_call(
        body,
        out_shape=out_shape,
        in_specs=[pl.BlockSpec(memory_space=pl.ANY)] * in_hbm + [spec] * (n_in - in_hbm),
        out_specs=[spec] * len(out_shape) if many else spec,
        scratch_shapes=list(scratch),
        compiler_params=pltpu.CompilerParams(vmem_limit_bytes=24 * 1024 * 1024),
        name=name,
    )


def per_device(sketches, centroids, coarse_init):
    nx, nc = lax.axis_size("x"), lax.axis_size("core")
    ny, nz = lax.axis_size("y"), lax.axis_size("z")
    n_row, n_cent = nx * nc, ny * nz
    rows, width = sketches.shape
    local_k = centroids.shape[0]
    tile = rows // TILES
    blocks = width // LANES

    small = struct(blocks * SUB + 8, LANES)
    half = struct(blocks * local_k // 4 + 8, LANES)
    halves = struct(2, blocks * local_k // 4 + 8, LANES)
    column = pltpu.VMEM((local_k, LANES), jnp.float32)
    exps_out = pltpu.VMEM((local_k, rows), jnp.float32)
    cents_out = pltpu.VMEM((local_k, width), jnp.float32)
    by_row = struct(TILES, tile)

    for round_index in range(ROUNDS):
        if round_index == 0:
            exps, held, cents, top, part = kernel_call(
                score_load_kernel,
                [exps_out, pltpu.VMEM((rows, width), jnp.bfloat16), cents_out, by_row, by_row],
                "scores_first",
                2,
                scratch=[pltpu.SemaphoreType.DMA((TILES * LOADS,)), pltpu.SemaphoreType.DMA],
                in_hbm=2,
            )(
                pltpu.with_memory_space_constraint(sketches, pltpu.HBM),
                pltpu.with_memory_space_constraint(centroids, pltpu.HBM),
            )
        else:
            exps, cents, top, part = kernel_call(
                score_kernel, [exps_out, cents_out, by_row, by_row], "scores", 3
            )(held, mine, theirs)
        part = kernel_call(combine_lse_kernel, by_row, "lse_y", 4)(
            *burst(part, "y", partners("y")), part
        )
        part = add_logs(part, swap(part, "z", 1))
        keep, send, lse = kernel_call(
            sums_kernel,
            [halves, halves, by_row],
            "sums",
            7,
            scratch=[pltpu.VMEM((local_k, width), jnp.float32), column],
        )(*burst(part, "z", partners("z")), part, exps, held, top)
        a, b = kernel_call(halves_kernel, [half, half], "halves", 2)(keep, swap(send, "core", 1))
        a_got, b_got = swap(a, "x", 1), swap(b, "x", 3)
        a, b = a + a_got, b + b_got
        mine = kernel_call(update_kernel, halves, "update", 5)(
            a, swap(a, "x", 3), b, swap(b, "x", 1), cents
        )
        theirs = swap(mine, "core", 1)

    mass = pltpu.VMEM((SUB, LANES), jnp.float32)
    for iteration in range(COARSE_ITERS):
        if iteration == 0:
            packed, cents, row = kernel_call(
                coarse_first_kernel,
                [small, cents_out, pltpu.VMEM((1, local_k), jnp.float32)],
                "coarse_first",
                3,
                scratch=[column, pltpu.VMEM((coarse_init.shape[0], local_k), jnp.float32), mass],
            )(mine, theirs, coarse_init)
            old = coarse_init
        else:
            old, logits, part = kernel_call(
                coarse_logits_kernel,
                [struct(blocks * SUB, LANES), struct(SUB, local_k), struct(1, local_k)],
                "coarse_logits",
                6,
            )(*z_parts, packed, old, cents)
            part = add_logs(part, swap(part, "core", 1))
            packed = kernel_call(coarse_weights_kernel, small, "coarse_weights", 7, scratch=[mass])(
                *burst(part, "x", partners("x")), part, logits, row, cents
            )
        packed = kernel_call(combine_sum_kernel, small, "sum_y", 4)(
            *burst(packed, "y", partners("y")), packed
        )
        packed = packed + swap(packed, "z", 1)
        z_parts = burst(packed, "z", partners("z"))
    last = kernel_call(coarse_last_kernel, small, "coarse_last", 5)(*z_parts, packed, old)
    mine = kernel_call(stack_kernel, struct(nx, *small.shape), "stack", 4)(
        *burst(last, "x", partners("x")), last
    )
    coarse, masses = kernel_call(
        assemble_kernel, [struct(local_k, width), struct(1, local_k)], "assemble", 2, scratch=[column]
    )(mine, swap(mine, "core", 1))
    all_rows = rows * n_row
    all_cents = local_k * n_cent
    return (
        cents + 0.0,
        row.reshape(local_k),
        coarse,
        masses.reshape(local_k) * (all_cents / all_rows),
        lse.reshape(rows),
    )


def solution(mesh):
    n_row, n_cent = mesh.shape["row"], mesh.shape["cent"]
    fine = Mesh(mesh.devices.reshape(n_row // 2, 2, n_cent // 8, 8), ("x", "core", "y", "z"))
    row, cent = ("x", "core"), ("y", "z")
    in_specs = (P(row, None), P(cent, None), P())
    out_specs = (P(cent, None), P(cent), P(), P(), P(row))
    return jax.shard_map(
        per_device, mesh=fine, in_specs=in_specs, out_specs=out_specs, check_vma=False
    )
```

```python
import functools
import math

import jax
import jax.numpy as jnp
from jax import lax
from jax.experimental import pallas as pl
from jax.experimental.pallas import tpu as pltpu
from jax.sharding import Mesh, PartitionSpec as P

ROUNDS = 2
COARSE_ITERS = 3
LANES = 128
TILES = 8
WINDOW = 4
LOADS = 2
SUB = 32


def swap(x, axis, bits):
    size = lax.axis_size(axis)
    return lax.ppermute(x, axis, [(i, i ^ bits) for i in range(size)])


def add_logs(a, b):
    return jnp.maximum(a, b) + jnp.log1p(jnp.exp(-jnp.abs(a - b)))


def burst(chunks, axis):
    near = swap(chunks[1], axis, 1)
    wrap = swap(chunks[3], axis, 3)
    far = swap(chunks[2], axis, 2)
    return near, far, wrap


def burst(x, axis, order):
    return [swap(x, axis, bits) for bits in order]


def partners(axis):
    return (6, 2, 5) if axis == "z" else (3, 1, 2)


def four(combine, far, one, two, x):
    return combine(combine(x, far), combine(one, two))


def four_z(combine, far, one, two, x):
    return combine(combine(x, one), combine(far, two))


def tile_dots(c_bf, x_ref, i, tile):
    return lax.dot_general(
        c_bf,
        x_ref[i * tile : (i + 1) * tile, :],
        (((1,), (1,)), ((), ())),
        preferred_element_type=jnp.float32,
    )


def finish_tile(dots, half, i, factor, e_ref, top_ref, lse_ref):
    tile = dots.shape[1]
    dots = dots - half
    top = jnp.max(dots, axis=0, keepdims=True)
    exps = jnp.exp2((dots - top) * (factor * math.log2(math.e)))
    total = jnp.sum(exps, axis=0, keepdims=True)
    top = top * factor
    e_ref[:, i * tile : (i + 1) * tile] = exps
    top_ref[i : i + 1, :] = top
    lse_ref[i : i + 1, :] = top + jnp.log(total)


def score_all(c, xv_ref, e_ref, top_ref, lse_ref, ready):
    tile = xv_ref.shape[0] // TILES
    factor = c.shape[1] ** -0.5
    c_bf = c.astype(jnp.bfloat16)
    half = 0.5 * jnp.sum(c * c, axis=1, keepdims=True)
    previous = None
    for i in range(TILES):
        ready(i)
        dots = tile_dots(c_bf, xv_ref, i, tile)
        if i:
            finish_tile(previous, half, i - 1, factor, e_ref, top_ref, lse_ref)
        previous = dots
    finish_tile(previous, half, TILES - 1, factor, e_ref, top_ref, lse_ref)


def score_load_kernel(x_ref, c_ref, e_ref, xv_ref, cv_ref, top_ref, lse_ref, sems, c_sem):
    step = xv_ref.shape[0] // (TILES * LOADS)
    c_copy = pltpu.make_async_copy(c_ref, cv_ref, c_sem)
    c_copy.start()
    copies = [
        pltpu.make_async_copy(
            x_ref.at[pl.ds(i * step, step)], xv_ref.at[pl.ds(i * step, step)], sems.at[i]
        )
        for i in range(TILES * LOADS)
    ]
    for copy in copies[: WINDOW * LOADS]:
        copy.start()
    c_copy.wait()

    def ready(i):
        for copy in copies[i * LOADS : (i + 1) * LOADS]:
            copy.wait()
        for copy in copies[(i + WINDOW) * LOADS : (i + WINDOW + 1) * LOADS]:
            copy.start()

    score_all(cv_ref[...], xv_ref, e_ref, top_ref, lse_ref, ready)


def score_kernel(xv_ref, mine_ref, theirs_ref, e_ref, cv_ref, top_ref, lse_ref):
    place_halves(mine_ref, theirs_ref, cv_ref)
    score_all(cv_ref[...], xv_ref, e_ref, top_ref, lse_ref, lambda i: None)


def pack_column(ref, base, sub):
    lane = lax.broadcasted_iota(jnp.int32, (8, LANES), 1)
    packed = jnp.zeros((8, LANES), jnp.float32)
    for j in range(sub // 8):
        packed = jnp.where(lane == j, ref[pl.ds(base + 8 * j, 8), :], packed)
    return packed


def combine_lse_kernel(two_ref, one_ref, far_ref, x_ref, out_ref):
    out_ref[...] = four(add_logs, far_ref[...], one_ref[...], two_ref[...], x_ref[...])


def combine_sum_kernel(two_ref, one_ref, far_ref, x_ref, out_ref):
    out_ref[...] = four(jnp.add, far_ref[...], one_ref[...], two_ref[...], x_ref[...])


def sums_kernel(
    two_ref, one_ref, far_ref, part_ref, e_ref, xv_ref, top_ref,
    keep_ref, send_ref, lse_ref, sums_ref, counts_ref,
):
    tile = xv_ref.shape[0] // TILES
    local_k, width = sums_ref.shape
    parts = keep_ref.shape[0]
    sub = local_k // (2 * parts)
    lse = four_z(add_logs, far_ref[...], one_ref[...], two_ref[...], part_ref[...])
    lse_ref[...] = lse
    scales = jnp.exp(top_ref[...] - lse)
    counts = jnp.zeros((local_k, LANES), jnp.float32)
    for i in range(TILES):
        rows = slice(i * tile, (i + 1) * tile)
        p = e_ref[:, rows] * scales[i : i + 1, :]
        part = p[:, :LANES]
        for j in range(1, tile // LANES):
            part = part + p[:, j * LANES : (j + 1) * LANES]
        counts = counts + part
        dots = jnp.dot(p.astype(jnp.bfloat16), xv_ref[rows, :], preferred_element_type=jnp.float32)
        if i == 0:
            sums_ref[...] = dots
        else:
            sums_ref[...] += dots
    counts_ref[...] = jnp.broadcast_to(jnp.sum(counts, axis=1, keepdims=True), counts.shape)
    core = lax.axis_index("core")
    for out, which in ((keep_ref, core), (send_ref, 1 - core)):
        for h in range(parts):
            base = pl.multiple_of((which * parts + h) * sub, sub)
            for d in range(width // LANES):
                out[h, d * sub : (d + 1) * sub, :] = sums_ref[
                    pl.ds(base, sub), d * LANES : (d + 1) * LANES
                ]
            out[h, (width // LANES) * sub :, :] = pack_column(counts_ref, base, sub)


def halves_kernel(keep_ref, got_ref, a_ref, b_ref):
    a_ref[...] = keep_ref[0] + got_ref[0]
    b_ref[...] = keep_ref[1] + got_ref[1]


def updated(total, old):
    blocks, sub = len(old), old[0].shape[0]
    counts = total[blocks * sub :, :]
    under = [jnp.broadcast_to(counts[:, j : j + 1], (8, LANES)) + 1.0 for j in range(sub // 8)]
    parts = []
    for d in range(blocks):
        for j in range(sub // 8):
            at = d * sub + 8 * j
            parts.append((total[at : at + 8, :] + old[d][8 * j : 8 * j + 8, :]) / under[j])
    return jnp.concatenate(parts, axis=0), counts


def update_kernel(a_ref, a_got_ref, b_ref, b_got_ref, old_ref, out_ref):
    local_k, width = old_ref.shape
    blocks = width // LANES
    sub = local_k // 4
    core = lax.axis_index("core")
    for h, (ref, got_ref) in enumerate(((a_ref, a_got_ref), (b_ref, b_got_ref))):
        base = pl.multiple_of((core * 2 + h) * sub, sub)
        old = [old_ref[pl.ds(base, sub), d * LANES : (d + 1) * LANES] for d in range(blocks)]
        fresh, counts = updated(ref[...] + got_ref[...], old)
        out_ref[h, : blocks * sub, :] = fresh
        out_ref[h, blocks * sub :, :] = counts


def place_halves(mine_ref, theirs_ref, c_ref, counts_ref=None):
    local_k, width = c_ref.shape
    blocks = width // LANES
    sub = local_k // 4
    core = lax.axis_index("core")
    for ref, which in ((mine_ref, core), (theirs_ref, 1 - core)):
        for h in range(2):
            base = pl.multiple_of((which * 2 + h) * sub, sub)
            for d in range(blocks):
                c_ref[pl.ds(base, sub), d * LANES : (d + 1) * LANES] = ref[
                    h, d * sub : (d + 1) * sub, :
                ]
            if counts_ref is not None:
                for j in range(sub // 8):
                    counts_ref[pl.ds(base + 8 * j, 8), :] = jnp.broadcast_to(
                        ref[h, blocks * sub :, j : j + 1], (8, LANES)
                    )


def coarse_logits(g, f):
    inner = lax.dot_general(
        g,
        f,
        (((1,), (1,)), ((), ())),
        precision=lax.Precision.HIGHEST,
        preferred_element_type=jnp.float32,
    )
    sharp = 4.0 * g.shape[1] ** -0.5
    return sharp * (inner - 0.5 * jnp.sum(g * g, axis=1, keepdims=True))


def column_lse(logits):
    top = jnp.max(logits, axis=0, keepdims=True)
    return top + jnp.log(jnp.sum(jnp.exp(logits - top), axis=0, keepdims=True))


def weigh(logits, norm, row, f, out_ref, mass_ref):
    weights = row * jnp.exp(logits - norm)
    totals = lax.dot_general(
        weights,
        f,
        (((1,), (0,)), ((), ())),
        precision=lax.Precision.HIGHEST,
        preferred_element_type=jnp.float32,
    )
    sub, width = totals.shape
    blocks = width // LANES
    for d in range(blocks):
        out_ref[d * sub : (d + 1) * sub, :] = totals[:, d * LANES : (d + 1) * LANES]
    mass_ref[...] = jnp.broadcast_to(jnp.sum(weights, axis=1, keepdims=True), (sub, LANES))
    out_ref[blocks * sub :, :] = pack_column(mass_ref, 0, sub)


def coarse_base():
    return pl.multiple_of((lax.axis_index("x") * 2 + lax.axis_index("core")) * SUB, SUB)


def coarse_first_kernel(
    mine_ref, theirs_ref, g_ref, out_ref, f_ref, row_ref, counts_ref, logits_ref, mass_ref
):
    place_halves(mine_ref, theirs_ref, f_ref, counts_ref)
    row = jnp.transpose(counts_ref[...])[:1, :]
    row_ref[...] = row
    f = f_ref[...]
    logits = coarse_logits(g_ref[...], f)
    logits_ref[...] = logits
    weigh(logits_ref[pl.ds(coarse_base(), SUB), :], column_lse(logits), row, f, out_ref, mass_ref)


def read_old(old_ref):
    if old_ref.shape[1] == LANES:
        return [old_ref[at : at + SUB, :] for at in range(0, old_ref.shape[0], SUB)]
    base = coarse_base()
    return [old_ref[pl.ds(base, SUB), at : at + LANES] for at in range(0, old_ref.shape[1], LANES)]


def coarse_logits_kernel(
    two_ref, one_ref, far_ref, part_ref, old_ref, f_ref, g_ref, logits_ref, lse_ref
):
    total = four_z(jnp.add, far_ref[...], one_ref[...], two_ref[...], part_ref[...])
    fresh, _ = updated(total, read_old(old_ref))
    g_ref[...] = fresh
    g = jnp.concatenate([fresh[at : at + SUB, :] for at in range(0, fresh.shape[0], SUB)], axis=1)
    logits = coarse_logits(g, f_ref[...])
    logits_ref[...] = logits
    lse_ref[...] = column_lse(logits)


def coarse_logits_out_kernel(
    two_ref, one_ref, far_ref, part_ref, old_ref, f_ref, row_ref, score_ref,
    g_ref, logits_ref, lse_ref, f_out, row_out, score_out, flat_ref, sems,
):
    copies = [
        pltpu.make_async_copy(f_ref, f_out, sems.at[0]),
        pltpu.make_async_copy(row_ref, row_out, sems.at[1]),
        pltpu.make_async_copy(flat_ref, score_out, sems.at[2]),
    ]
    copies[0].start()
    copies[1].start()
    per = score_ref.shape[1] // LANES
    for i in range(score_ref.shape[0]):
        for j in range(per):
            flat_ref[i * per + j : i * per + j + 1, :] = score_ref[
                i : i + 1, j * LANES : (j + 1) * LANES
            ]
    copies[2].start()
    coarse_logits_kernel(
        two_ref, one_ref, far_ref, part_ref, old_ref, f_ref, g_ref, logits_ref, lse_ref
    )
    for copy in copies:
        copy.wait()


def coarse_weights_kernel(
    two_ref, one_ref, far_ref, part_ref, logits_ref, row_ref, f_ref, out_ref, mass_ref
):
    norm = four(add_logs, far_ref[...], one_ref[...], two_ref[...], part_ref[...])
    weigh(logits_ref[...], norm, row_ref[...], f_ref[...], out_ref, mass_ref)


def coarse_last_kernel(two_ref, one_ref, far_ref, part_ref, old_ref, out_ref):
    total = four_z(jnp.add, far_ref[...], one_ref[...], two_ref[...], part_ref[...])
    fresh, mass = updated(total, read_old(old_ref))
    out_ref[: fresh.shape[0], :] = fresh
    out_ref[fresh.shape[0] :, :] = mass


def stack_kernel(two_ref, one_ref, far_ref, x_ref, out_ref):
    for s, ref in enumerate((x_ref, one_ref, far_ref, two_ref)):
        out_ref[s] = ref[...]


def assemble_kernel(factor, mine_ref, theirs_ref, g_ref, row_ref, counts_ref):
    width = g_ref.shape[1]
    blocks = width // LANES
    chip, core = lax.axis_index("x"), lax.axis_index("core")
    for ref, which in ((mine_ref, core), (theirs_ref, 1 - core)):
        for s in range(mine_ref.shape[0]):
            base = pl.multiple_of((lax.bitwise_xor(chip, s) * 2 + which) * SUB, SUB)
            for d in range(blocks):
                g_ref[pl.ds(base, SUB), d * LANES : (d + 1) * LANES] = ref[
                    s, d * SUB : (d + 1) * SUB, :
                ]
            for j in range(SUB // 8):
                counts_ref[pl.ds(base + 8 * j, 8), :] = jnp.broadcast_to(
                    ref[s, blocks * SUB :, j : j + 1], (8, LANES)
                )
    row_ref[...] = jnp.transpose(counts_ref[...])[:1, :] * factor


def struct(*shape, dtype=jnp.float32):
    return jax.ShapeDtypeStruct(shape, dtype)


def kernel_call(body, out_shape, name, n_in, scratch=(), in_hbm=0, out_hbm=0):
    many = isinstance(out_shape, list)
    anywhere = pl.BlockSpec(memory_space=pl.ANY)
    spec = pl.BlockSpec(memory_space=pltpu.VMEM)
    return pl.pallas_call(
        body,
        out_shape=out_shape,
        in_specs=[anywhere] * in_hbm + [spec] * (n_in - in_hbm),
        out_specs=[spec] * (len(out_shape) - out_hbm) + [anywhere] * out_hbm if many else spec,
        scratch_shapes=list(scratch),
        compiler_params=pltpu.CompilerParams(vmem_limit_bytes=24 * 1024 * 1024),
        name=name,
    )


def per_device(sketches, centroids, coarse_init):
    nx, nc = lax.axis_size("x"), lax.axis_size("core")
    ny, nz = lax.axis_size("y"), lax.axis_size("z")
    n_row, n_cent = nx * nc, ny * nz
    rows, width = sketches.shape
    local_k = centroids.shape[0]
    tile = rows // TILES
    blocks = width // LANES

    small = struct(blocks * SUB + 8, LANES)
    half = struct(blocks * local_k // 4 + 8, LANES)
    halves = struct(2, blocks * local_k // 4 + 8, LANES)
    column = pltpu.VMEM((local_k, LANES), jnp.float32)
    exps_out = pltpu.VMEM((local_k, rows), jnp.float32)
    cents_out = pltpu.VMEM((local_k, width), jnp.float32)
    by_row = struct(TILES, tile)

    for round_index in range(ROUNDS):
        if round_index == 0:
            exps, held, cents, top, part = kernel_call(
                score_load_kernel,
                [exps_out, pltpu.VMEM((rows, width), jnp.bfloat16), cents_out, by_row, by_row],
                "scores_first",
                2,
                scratch=[pltpu.SemaphoreType.DMA((TILES * LOADS,)), pltpu.SemaphoreType.DMA],
                in_hbm=2,
            )(
                pltpu.with_memory_space_constraint(sketches, pltpu.HBM),
                pltpu.with_memory_space_constraint(centroids, pltpu.HBM),
            )
        else:
            exps, cents, top, part = kernel_call(
                score_kernel, [exps_out, cents_out, by_row, by_row], "scores", 3
            )(held, mine, theirs)
        part = kernel_call(combine_lse_kernel, by_row, "lse_y", 4)(
            *burst(part, "y", partners("y")), part
        )
        part = add_logs(part, swap(part, "z", 1))
        keep, send, lse = kernel_call(
            sums_kernel,
            [halves, halves, by_row],
            "sums",
            7,
            scratch=[pltpu.VMEM((local_k, width), jnp.float32), column],
        )(*burst(part, "z", partners("z")), part, exps, held, top)
        a, b = kernel_call(halves_kernel, [half, half], "halves", 2)(keep, swap(send, "core", 1))
        a_got, b_got = swap(a, "x", 1), swap(b, "x", 3)
        a, b = a + a_got, b + b_got
        mine = kernel_call(update_kernel, halves, "update", 5)(
            a, swap(a, "x", 3), b, swap(b, "x", 1), cents
        )
        theirs = swap(mine, "core", 1)

    mass = pltpu.VMEM((SUB, LANES), jnp.float32)
    for iteration in range(COARSE_ITERS):
        if iteration == 0:
            packed, cents, row = kernel_call(
                coarse_first_kernel,
                [small, cents_out, pltpu.VMEM((1, local_k), jnp.float32)],
                "coarse_first",
                3,
                scratch=[column, pltpu.VMEM((coarse_init.shape[0], local_k), jnp.float32), mass],
            )(mine, theirs, coarse_init)
            old = coarse_init
        else:
            outs = [struct(blocks * SUB, LANES), struct(SUB, local_k), struct(1, local_k)]
            if iteration == 1:
                old, logits, part, fine_centroids, fine_counts, row_score = kernel_call(
                    coarse_logits_out_kernel,
                    outs
                    + [
                        pltpu.HBM((local_k, width), jnp.float32),
                        pltpu.HBM((1, local_k), jnp.float32),
                        pltpu.HBM((rows // LANES, LANES), jnp.float32),
                    ],
                    "coarse_logits_out",
                    8,
                    scratch=[
                        pltpu.VMEM((rows // LANES, LANES), jnp.float32),
                        pltpu.SemaphoreType.DMA((3,)),
                    ],
                    out_hbm=3,
                )(*z_parts, packed, old, cents, row, lse)
            else:
                old, logits, part = kernel_call(coarse_logits_kernel, outs, "coarse_logits", 6)(
                    *z_parts, packed, old, cents
                )
            part = add_logs(part, swap(part, "core", 1))
            packed = kernel_call(coarse_weights_kernel, small, "coarse_weights", 7, scratch=[mass])(
                *burst(part, "x", partners("x")), part, logits, row, cents
            )
        packed = kernel_call(combine_sum_kernel, small, "sum_y", 4)(
            *burst(packed, "y", partners("y")), packed
        )
        packed = packed + swap(packed, "z", 1)
        z_parts = burst(packed, "z", partners("z"))
    last = kernel_call(coarse_last_kernel, small, "coarse_last", 5)(*z_parts, packed, old)
    mine = kernel_call(stack_kernel, struct(nx, *small.shape), "stack", 4)(
        *burst(last, "x", partners("x")), last
    )
    all_rows = rows * n_row
    all_cents = local_k * n_cent
    coarse, masses = kernel_call(
        functools.partial(assemble_kernel, all_cents / all_rows),
        [struct(local_k, width), struct(1, local_k)],
        "assemble",
        2,
        scratch=[column],
    )(mine, swap(mine, "core", 1))
    return (
        fine_centroids,
        fine_counts.reshape(local_k),
        coarse,
        masses.reshape(local_k),
        row_score.reshape(rows),
    )


def solution(mesh):
    n_row, n_cent = mesh.shape["row"], mesh.shape["cent"]
    fine = Mesh(mesh.devices.reshape(n_row // 2, 2, n_cent // 8, 8), ("x", "core", "y", "z"))
    row, cent = ("x", "core"), ("y", "z")
    in_specs = (P(row, None), P(cent, None), P())
    out_specs = (P(cent, None), P(cent), P(), P(), P(row))
    return jax.shard_map(
        per_device, mesh=fine, in_specs=in_specs, out_specs=out_specs, check_vma=False
    )
```

```python
import functools
import math

import jax
import jax.numpy as jnp
from jax import lax
from jax.experimental import pallas as pl
from jax.experimental.pallas import tpu as pltpu
from jax.sharding import Mesh, PartitionSpec as P

ROUNDS = 2
COARSE_ITERS = 3
LANES = 128
TILES = 8
WINDOW = 4
LOADS = 2
SUB = 32


def swap(x, axis, bits):
    size = lax.axis_size(axis)
    return lax.ppermute(x, axis, [(i, i ^ bits) for i in range(size)])


def add_logs(a, b):
    return jnp.maximum(a, b) + jnp.log1p(jnp.exp(-jnp.abs(a - b)))


def burst(chunks, axis):
    near = swap(chunks[1], axis, 1)
    wrap = swap(chunks[3], axis, 3)
    far = swap(chunks[2], axis, 2)
    return near, far, wrap


def burst(x, axis, order):
    return [swap(x, axis, bits) for bits in order]


def partners(axis):
    return (6, 2, 5) if axis == "z" else (3, 1, 2)


def four(combine, far, one, two, x):
    return combine(combine(x, far), combine(one, two))


def four_z(combine, far, one, two, x):
    return combine(combine(x, one), combine(far, two))


def tile_dots(c_bf, x_ref, i, tile):
    return lax.dot_general(
        c_bf,
        x_ref[i * tile : (i + 1) * tile, :],
        (((1,), (1,)), ((), ())),
        preferred_element_type=jnp.float32,
    )


def finish_tile(dots, half, i, factor, e_ref, top_ref, lse_ref):
    tile = dots.shape[1]
    dots = dots - half
    top = jnp.max(dots, axis=0, keepdims=True)
    exps = jnp.exp2((dots - top) * (factor * math.log2(math.e)))
    total = jnp.sum(exps, axis=0, keepdims=True)
    top = top * factor
    e_ref[:, i * tile : (i + 1) * tile] = exps
    top_ref[i : i + 1, :] = top
    lse_ref[i : i + 1, :] = top + jnp.log(total)


def score_all(c, xv_ref, e_ref, top_ref, lse_ref, ready):
    tile = xv_ref.shape[0] // TILES
    factor = c.shape[1] ** -0.5
    c_bf = c.astype(jnp.bfloat16)
    half = 0.5 * jnp.sum(c * c, axis=1, keepdims=True)
    previous = None
    for i in range(TILES):
        ready(i)
        dots = tile_dots(c_bf, xv_ref, i, tile)
        if i:
            finish_tile(previous, half, i - 1, factor, e_ref, top_ref, lse_ref)
        previous = dots
    finish_tile(previous, half, TILES - 1, factor, e_ref, top_ref, lse_ref)


def score_load_kernel(x_ref, c_ref, e_ref, xv_ref, cv_ref, top_ref, lse_ref, sems, c_sem):
    step = xv_ref.shape[0] // (TILES * LOADS)
    c_copy = pltpu.make_async_copy(c_ref, cv_ref, c_sem)
    c_copy.start()
    copies = [
        pltpu.make_async_copy(
            x_ref.at[pl.ds(i * step, step)], xv_ref.at[pl.ds(i * step, step)], sems.at[i]
        )
        for i in range(TILES * LOADS)
    ]
    for i in range(WINDOW * LOADS):
        copies[i].start(priority=i % 2)
    c_copy.wait()

    def ready(i):
        for copy in copies[i * LOADS : (i + 1) * LOADS]:
            copy.wait()
        for j, copy in enumerate(copies[(i + WINDOW) * LOADS : (i + WINDOW + 1) * LOADS]):
            copy.start(priority=j % 2)

    score_all(cv_ref[...], xv_ref, e_ref, top_ref, lse_ref, ready)


def score_kernel(xv_ref, mine_ref, theirs_ref, e_ref, cv_ref, top_ref, lse_ref):
    place_halves(mine_ref, theirs_ref, cv_ref)
    score_all(cv_ref[...], xv_ref, e_ref, top_ref, lse_ref, lambda i: None)


def pack_column(ref, base, sub):
    lane = lax.broadcasted_iota(jnp.int32, (8, LANES), 1)
    packed = jnp.zeros((8, LANES), jnp.float32)
    for j in range(sub // 8):
        packed = jnp.where(lane == j, ref[pl.ds(base + 8 * j, 8), :], packed)
    return packed


def combine_lse_kernel(two_ref, one_ref, far_ref, x_ref, out_ref):
    out_ref[...] = four(add_logs, far_ref[...], one_ref[...], two_ref[...], x_ref[...])


def combine_sum_pass_kernel(two_ref, one_ref, far_ref, x_ref, other_ref, out_ref, pass_ref):
    out_ref[...] = four(jnp.add, far_ref[...], one_ref[...], two_ref[...], x_ref[...])
    pass_ref[...] = other_ref[...]


def combine_sum_kernel(two_ref, one_ref, far_ref, x_ref, out_ref):
    out_ref[...] = four(jnp.add, far_ref[...], one_ref[...], two_ref[...], x_ref[...])


def sums_kernel(
    two_ref, one_ref, far_ref, part_ref, e_ref, xv_ref, top_ref,
    keep_ref, send_ref, lse_ref, sums_ref, counts_ref,
):
    tile = xv_ref.shape[0] // TILES
    local_k, width = sums_ref.shape
    parts = keep_ref.shape[0]
    sub = local_k // (2 * parts)
    lse = four_z(add_logs, far_ref[...], one_ref[...], two_ref[...], part_ref[...])
    lse_ref[...] = lse
    scales = jnp.exp(top_ref[...] - lse)
    counts = jnp.zeros((local_k, LANES), jnp.float32)
    for i in range(TILES):
        rows = slice(i * tile, (i + 1) * tile)
        p = e_ref[:, rows] * scales[i : i + 1, :]
        part = p[:, :LANES]
        for j in range(1, tile // LANES):
            part = part + p[:, j * LANES : (j + 1) * LANES]
        counts = counts + part
        dots = jnp.dot(p.astype(jnp.bfloat16), xv_ref[rows, :], preferred_element_type=jnp.float32)
        if i == 0:
            sums_ref[...] = dots
        else:
            sums_ref[...] += dots
    counts_ref[...] = jnp.broadcast_to(jnp.sum(counts, axis=1, keepdims=True), counts.shape)
    core = lax.axis_index("core")
    for out, which in ((keep_ref, core), (send_ref, 1 - core)):
        for h in range(parts):
            base = pl.multiple_of((which * parts + h) * sub, sub)
            for d in range(width // LANES):
                out[h, d * sub : (d + 1) * sub, :] = sums_ref[
                    pl.ds(base, sub), d * LANES : (d + 1) * LANES
                ]
            out[h, (width // LANES) * sub :, :] = pack_column(counts_ref, base, sub)


def halves_kernel(keep_ref, got_ref, a_ref, b_ref):
    a_ref[...] = keep_ref[0] + got_ref[0]
    b_ref[...] = keep_ref[1] + got_ref[1]


def updated(total, old):
    blocks, sub = len(old), old[0].shape[0]
    counts = total[blocks * sub :, :]
    under = [jnp.broadcast_to(counts[:, j : j + 1], (8, LANES)) + 1.0 for j in range(sub // 8)]
    parts = []
    for d in range(blocks):
        for j in range(sub // 8):
            at = d * sub + 8 * j
            parts.append((total[at : at + 8, :] + old[d][8 * j : 8 * j + 8, :]) / under[j])
    return jnp.concatenate(parts, axis=0), counts


def update_kernel(a_ref, a_got_ref, b_ref, b_got_ref, old_ref, out_ref):
    local_k, width = old_ref.shape
    blocks = width // LANES
    sub = local_k // 4
    core = lax.axis_index("core")
    for h, (ref, got_ref) in enumerate(((a_ref, a_got_ref), (b_ref, b_got_ref))):
        base = pl.multiple_of((core * 2 + h) * sub, sub)
        old = [old_ref[pl.ds(base, sub), d * LANES : (d + 1) * LANES] for d in range(blocks)]
        fresh, counts = updated(ref[...] + got_ref[...], old)
        out_ref[h, : blocks * sub, :] = fresh
        out_ref[h, blocks * sub :, :] = counts


def place_halves(mine_ref, theirs_ref, c_ref, counts_ref=None):
    local_k, width = c_ref.shape
    blocks = width // LANES
    sub = local_k // 4
    core = lax.axis_index("core")
    for ref, which in ((mine_ref, core), (theirs_ref, 1 - core)):
        for h in range(2):
            base = pl.multiple_of((which * 2 + h) * sub, sub)
            for d in range(blocks):
                c_ref[pl.ds(base, sub), d * LANES : (d + 1) * LANES] = ref[
                    h, d * sub : (d + 1) * sub, :
                ]
            if counts_ref is not None:
                for j in range(sub // 8):
                    counts_ref[pl.ds(base + 8 * j, 8), :] = jnp.broadcast_to(
                        ref[h, blocks * sub :, j : j + 1], (8, LANES)
                    )


def coarse_logits(g, f):
    inner = lax.dot_general(
        g,
        f,
        (((1,), (1,)), ((), ())),
        precision=lax.Precision.HIGHEST,
        preferred_element_type=jnp.float32,
    )
    sharp = 4.0 * g.shape[1] ** -0.5
    return sharp * (inner - 0.5 * jnp.sum(g * g, axis=1, keepdims=True))


def column_lse(logits):
    top = jnp.max(logits, axis=0, keepdims=True)
    return top + jnp.log(jnp.sum(jnp.exp(logits - top), axis=0, keepdims=True))


def weigh(logits, norm, row, f, out_ref, mass_ref):
    weights = row * jnp.exp(logits - norm)
    totals = lax.dot_general(
        weights,
        f,
        (((1,), (0,)), ((), ())),
        precision=lax.Precision.HIGHEST,
        preferred_element_type=jnp.float32,
    )
    sub, width = totals.shape
    blocks = width // LANES
    for d in range(blocks):
        out_ref[d * sub : (d + 1) * sub, :] = totals[:, d * LANES : (d + 1) * LANES]
    mass_ref[...] = jnp.broadcast_to(jnp.sum(weights, axis=1, keepdims=True), (sub, LANES))
    out_ref[blocks * sub :, :] = pack_column(mass_ref, 0, sub)


def coarse_base():
    return pl.multiple_of((lax.axis_index("x") * 2 + lax.axis_index("core")) * SUB, SUB)


def coarse_first_kernel(
    mine_ref, theirs_ref, g_ref, out_ref, f_ref, row_ref, pass_ref, counts_ref, logits_ref, mass_ref
):
    pass_ref[...] = mine_ref[...]
    place_halves(mine_ref, theirs_ref, f_ref, counts_ref)
    row = jnp.transpose(counts_ref[...])[:1, :]
    row_ref[...] = row
    f = f_ref[...]
    logits = coarse_logits(g_ref[...], f)
    logits_ref[...] = logits
    weigh(logits_ref[pl.ds(coarse_base(), SUB), :], column_lse(logits), row, f, out_ref, mass_ref)


def read_old(old_ref):
    if old_ref.shape[1] == LANES:
        return [old_ref[at : at + SUB, :] for at in range(0, old_ref.shape[0], SUB)]
    base = coarse_base()
    return [old_ref[pl.ds(base, SUB), at : at + LANES] for at in range(0, old_ref.shape[1], LANES)]


def coarse_logits_kernel(
    two_ref, one_ref, far_ref, part_ref, old_ref, f_ref, g_ref, logits_ref, lse_ref
):
    total = four_z(jnp.add, far_ref[...], one_ref[...], two_ref[...], part_ref[...])
    fresh, _ = updated(total, read_old(old_ref))
    g_ref[...] = fresh
    g = jnp.concatenate([fresh[at : at + SUB, :] for at in range(0, fresh.shape[0], SUB)], axis=1)
    logits = coarse_logits(g, f_ref[...])
    logits_ref[...] = logits
    lse_ref[...] = column_lse(logits)


def coarse_logits_out_kernel(
    two_ref, one_ref, far_ref, part_ref, old_ref, f2_ref, f_ref, row_ref, score_ref,
    g_ref, logits_ref, lse_ref, f_out, row_out, score_out, flat_ref, sems,
):
    copies = [
        pltpu.make_async_copy(f_ref, f_out, sems.at[0]),
        pltpu.make_async_copy(row_ref, row_out, sems.at[1]),
        pltpu.make_async_copy(flat_ref, score_out, sems.at[2]),
    ]
    copies[0].start()
    copies[1].start()
    per = score_ref.shape[1] // LANES
    for i in range(score_ref.shape[0]):
        for j in range(per):
            flat_ref[i * per + j : i * per + j + 1, :] = score_ref[
                i : i + 1, j * LANES : (j + 1) * LANES
            ]
    copies[2].start()
    coarse_logits_kernel(
        two_ref, one_ref, far_ref, part_ref, old_ref, f2_ref, g_ref, logits_ref, lse_ref
    )
    for copy in copies:
        copy.wait()


def pair_kernel(mine_ref, theirs_ref, f_ref, row_ref, f2_ref, row2_ref, counts_ref, other_ref):
    local_k = f_ref.shape[0]
    place_halves(mine_ref, theirs_ref, other_ref, counts_ref)
    other_row = jnp.transpose(counts_ref[...])[:1, :]
    odd = lax.rem(lax.axis_index("z"), 2)
    f2_ref[pl.ds(pl.multiple_of(odd * local_k, local_k), local_k), :] = f_ref[...]
    f2_ref[pl.ds(pl.multiple_of((1 - odd) * local_k, local_k), local_k), :] = other_ref[...]
    row = row_ref[...]
    is_odd = jnp.full(row.shape, odd, jnp.int32) == 1
    row2_ref[:, :local_k] = jnp.where(is_odd, other_row, row)
    row2_ref[:, local_k:] = jnp.where(is_odd, row, other_row)


def coarse_weights_kernel(
    two_ref, one_ref, far_ref, part_ref, logits_ref, row_ref, f_ref, out_ref, mass_ref
):
    norm = four(add_logs, far_ref[...], one_ref[...], two_ref[...], part_ref[...])
    weigh(logits_ref[...], norm, row_ref[...], f_ref[...], out_ref, mass_ref)


def coarse_last_kernel(two_ref, one_ref, far_ref, part_ref, old_ref, out_ref):
    total = four_z(jnp.add, far_ref[...], one_ref[...], two_ref[...], part_ref[...])
    fresh, mass = updated(total, read_old(old_ref))
    out_ref[: fresh.shape[0], :] = fresh
    out_ref[fresh.shape[0] :, :] = mass


def stack_kernel(two_ref, one_ref, far_ref, x_ref, out_ref):
    for s, ref in enumerate((x_ref, one_ref, far_ref, two_ref)):
        out_ref[s] = ref[...]


def assemble_kernel(factor, mine_ref, theirs_ref, g_ref, row_ref, counts_ref):
    width = g_ref.shape[1]
    blocks = width // LANES
    chip, core = lax.axis_index("x"), lax.axis_index("core")
    for ref, which in ((mine_ref, core), (theirs_ref, 1 - core)):
        for s in range(mine_ref.shape[0]):
            base = pl.multiple_of((lax.bitwise_xor(chip, s) * 2 + which) * SUB, SUB)
            for d in range(blocks):
                g_ref[pl.ds(base, SUB), d * LANES : (d + 1) * LANES] = ref[
                    s, d * SUB : (d + 1) * SUB, :
                ]
            for j in range(SUB // 8):
                counts_ref[pl.ds(base + 8 * j, 8), :] = jnp.broadcast_to(
                    ref[s, blocks * SUB :, j : j + 1], (8, LANES)
                )
    row_ref[...] = jnp.transpose(counts_ref[...])[:1, :] * factor


def struct(*shape, dtype=jnp.float32):
    return jax.ShapeDtypeStruct(shape, dtype)


def kernel_call(body, out_shape, name, n_in, scratch=(), in_hbm=0, out_hbm=0):
    many = isinstance(out_shape, list)
    anywhere = pl.BlockSpec(memory_space=pl.ANY)
    spec = pl.BlockSpec(memory_space=pltpu.VMEM)
    return pl.pallas_call(
        body,
        out_shape=out_shape,
        in_specs=[anywhere] * in_hbm + [spec] * (n_in - in_hbm),
        out_specs=[spec] * (len(out_shape) - out_hbm) + [anywhere] * out_hbm if many else spec,
        scratch_shapes=list(scratch),
        compiler_params=pltpu.CompilerParams(vmem_limit_bytes=24 * 1024 * 1024),
        name=name,
    )


def per_device(sketches, centroids, coarse_init):
    nx, nc = lax.axis_size("x"), lax.axis_size("core")
    ny, nz = lax.axis_size("y"), lax.axis_size("z")
    n_row, n_cent = nx * nc, ny * nz
    rows, width = sketches.shape
    local_k = centroids.shape[0]
    tile = rows // TILES
    blocks = width // LANES

    small = struct(blocks * SUB + 8, LANES)
    half = struct(blocks * local_k // 4 + 8, LANES)
    halves = struct(2, blocks * local_k // 4 + 8, LANES)
    column = pltpu.VMEM((local_k, LANES), jnp.float32)
    exps_out = pltpu.VMEM((local_k, rows), jnp.float32)
    cents_out = pltpu.VMEM((local_k, width), jnp.float32)
    by_row = struct(TILES, tile)

    for round_index in range(ROUNDS):
        if round_index == 0:
            exps, held, cents, top, part = kernel_call(
                score_load_kernel,
                [exps_out, pltpu.VMEM((rows, width), jnp.bfloat16), cents_out, by_row, by_row],
                "scores_first",
                2,
                scratch=[pltpu.SemaphoreType.DMA((TILES * LOADS,)), pltpu.SemaphoreType.DMA],
                in_hbm=2,
            )(
                pltpu.with_memory_space_constraint(sketches, pltpu.HBM),
                pltpu.with_memory_space_constraint(centroids, pltpu.HBM),
            )
        else:
            exps, cents, top, part = kernel_call(
                score_kernel, [exps_out, cents_out, by_row, by_row], "scores", 3
            )(held, mine, theirs)
        part = kernel_call(combine_lse_kernel, by_row, "lse_y", 4)(
            *burst(part, "y", partners("y")), part
        )
        part = add_logs(part, swap(part, "z", 1))
        keep, send, lse = kernel_call(
            sums_kernel,
            [halves, halves, by_row],
            "sums",
            7,
            scratch=[pltpu.VMEM((local_k, width), jnp.float32), column],
        )(*burst(part, "z", partners("z")), part, exps, held, top)
        a, b = kernel_call(halves_kernel, [half, half], "halves", 2)(keep, swap(send, "core", 1))
        a_got, b_got = swap(a, "x", 1), swap(b, "x", 3)
        a, b = a + a_got, b + b_got
        mine = kernel_call(update_kernel, halves, "update", 5)(
            a, swap(a, "x", 3), b, swap(b, "x", 1), cents
        )
        theirs = swap(mine, "core", 1)

    mass = pltpu.VMEM((SUB, LANES), jnp.float32)
    for iteration in range(COARSE_ITERS):
        if iteration == 0:
            packed, cents, row, mine = kernel_call(
                coarse_first_kernel,
                [small, cents_out, pltpu.VMEM((1, local_k), jnp.float32), halves],
                "coarse_first",
                3,
                scratch=[column, pltpu.VMEM((coarse_init.shape[0], local_k), jnp.float32), mass],
            )(mine, theirs, coarse_init)
            old = coarse_init
        else:
            outs = [struct(blocks * SUB, LANES), struct(SUB, 2 * local_k), struct(1, 2 * local_k)]
            if iteration == 1:
                cents_pair, row_pair = kernel_call(
                    pair_kernel,
                    [
                        pltpu.VMEM((2 * local_k, width), jnp.float32),
                        pltpu.VMEM((1, 2 * local_k), jnp.float32),
                    ],
                    "pair",
                    4,
                    scratch=[column, pltpu.VMEM((local_k, width), jnp.float32)],
                )(*pair, cents, row)
                old, logits, part, fine_centroids, fine_counts, row_score = kernel_call(
                    coarse_logits_out_kernel,
                    outs
                    + [
                        pltpu.HBM((local_k, width), jnp.float32),
                        pltpu.HBM((1, local_k), jnp.float32),
                        pltpu.HBM((rows // LANES, LANES), jnp.float32),
                    ],
                    "coarse_logits_out",
                    9,
                    scratch=[
                        pltpu.VMEM((rows // LANES, LANES), jnp.float32),
                        pltpu.SemaphoreType.DMA((3,)),
                    ],
                    out_hbm=3,
                )(*z_parts, packed, old, cents_pair, cents, row, lse)
            else:
                old, logits, part = kernel_call(coarse_logits_kernel, outs, "coarse_logits", 6)(
                    *z_parts, packed, old, cents_pair
                )
            part = add_logs(part, swap(part, "core", 1))
            packed = kernel_call(coarse_weights_kernel, small, "coarse_weights", 7, scratch=[mass])(
                *burst(part, "x", partners("x")), part, logits, row_pair, cents_pair
            )
        parts = (*burst(packed, "y", partners("y")), packed)
        if iteration == 0:
            packed, pair = kernel_call(combine_sum_pass_kernel, [small, halves], "sum_y_pass", 5)(
                *parts, swap(mine, "z", 1)
            )
            pair = (pair, swap(pair, "core", 1))
            packed = packed + swap(packed, "z", 1)
        else:
            packed = kernel_call(combine_sum_kernel, small, "sum_y", 4)(*parts)
        z_parts = burst(packed, "z", partners("z"))
    last = kernel_call(coarse_last_kernel, small, "coarse_last", 5)(*z_parts, packed, old)
    mine = kernel_call(stack_kernel, struct(nx, *small.shape), "stack", 4)(
        *burst(last, "x", partners("x")), last
    )
    all_rows = rows * n_row
    all_cents = local_k * n_cent
    coarse, masses = kernel_call(
        functools.partial(assemble_kernel, all_cents / all_rows),
        [struct(local_k, width), struct(1, local_k)],
        "assemble",
        2,
        scratch=[column],
    )(mine, swap(mine, "core", 1))
    return (
        fine_centroids,
        fine_counts.reshape(local_k),
        coarse,
        masses.reshape(local_k),
        row_score.reshape(rows),
    )


def solution(mesh):
    n_row, n_cent = mesh.shape["row"], mesh.shape["cent"]
    fine = Mesh(mesh.devices.reshape(n_row // 2, 2, n_cent // 8, 8), ("x", "core", "y", "z"))
    row, cent = ("x", "core"), ("y", "z")
    in_specs = (P(row, None), P(cent, None), P())
    out_specs = (P(cent, None), P(cent), P(), P(), P(row))
    return jax.shard_map(
        per_device, mesh=fine, in_specs=in_specs, out_specs=out_specs, check_vma=False
    )
```

```python
import functools
import math

import jax
import jax.numpy as jnp
from jax import lax
from jax.experimental import pallas as pl
from jax.experimental.pallas import tpu as pltpu
from jax.sharding import Mesh, PartitionSpec as P

ROUNDS = 2
COARSE_ITERS = 3
LANES = 128
TILES = 8
WINDOW = 8
LOADS = 2
SUB = 32


def swap(x, axis, bits):
    size = lax.axis_size(axis)
    return lax.ppermute(x, axis, [(i, i ^ bits) for i in range(size)])


def add_logs(a, b):
    return jnp.maximum(a, b) + jnp.log1p(jnp.exp(-jnp.abs(a - b)))


def fetch(x, axis, source):
    return lax.ppermute(x, axis, [(source(i), i) for i in range(lax.axis_size(axis))])


def burst(x, axis):
    if axis == "z":
        size = lax.axis_size(axis)
        return [
            fetch(x, axis, lambda i: (i + 1 if i % 2 else i - 1) % size),
            fetch(x, axis, lambda i: (i - 2 if i % 2 else i + 2) % size),
            swap(x, axis, 5),
        ]
    return [swap(x, axis, bits) for bits in (3, 1, 2)]


def four(combine, far, one, two, x):
    return combine(combine(x, far), combine(one, two))


def four_z(combine, far, one, two, x):
    z = lax.axis_index("z")
    swapped = lax.rem(lax.shift_right_logical(z, 1) + lax.rem(z, 2), 2)
    mask = jnp.full(x.shape, swapped, jnp.int32) == 0
    first = jnp.where(mask, one, two)
    second = jnp.where(mask, two, one)
    return combine(combine(x, first), combine(second, far))


def tile_dots(c_bf, x_ref, i, tile):
    return lax.dot_general(
        c_bf,
        x_ref[i * tile : (i + 1) * tile, :],
        (((1,), (1,)), ((), ())),
        preferred_element_type=jnp.float32,
    )


def finish_tile(dots, half, i, factor, e_ref, top_ref, lse_ref):
    tile = dots.shape[1]
    dots = dots - half
    top = jnp.max(dots, axis=0, keepdims=True)
    exps = jnp.exp2((dots - top) * (factor * math.log2(math.e)))
    total = jnp.sum(exps, axis=0, keepdims=True)
    top = top * factor
    e_ref[:, i * tile : (i + 1) * tile] = exps
    top_ref[i : i + 1, :] = top
    lse_ref[i : i + 1, :] = top + jnp.log(total)


def score_all(c, xv_ref, e_ref, top_ref, lse_ref, ready):
    tile = xv_ref.shape[0] // TILES
    factor = c.shape[1] ** -0.5
    c_bf = c.astype(jnp.bfloat16)
    half = 0.5 * jnp.sum(c * c, axis=1, keepdims=True)
    previous = None
    for i in range(TILES):
        ready(i)
        dots = tile_dots(c_bf, xv_ref, i, tile)
        if i:
            finish_tile(previous, half, i - 1, factor, e_ref, top_ref, lse_ref)
        previous = dots
    finish_tile(previous, half, TILES - 1, factor, e_ref, top_ref, lse_ref)


def score_load_kernel(x_ref, c_ref, e_ref, xv_ref, cv_ref, top_ref, lse_ref, sems, c_sem):
    step = xv_ref.shape[0] // (TILES * LOADS)
    c_copy = pltpu.make_async_copy(c_ref, cv_ref, c_sem)
    c_copy.start()
    copies = [
        pltpu.make_async_copy(
            x_ref.at[pl.ds(i * step, step)], xv_ref.at[pl.ds(i * step, step)], sems.at[i]
        )
        for i in range(TILES * LOADS)
    ]
    for i in range(WINDOW * LOADS):
        copies[i].start(priority=i % 2)
    c_copy.wait()

    def ready(i):
        for copy in copies[i * LOADS : (i + 1) * LOADS]:
            copy.wait()
        for j, copy in enumerate(copies[(i + WINDOW) * LOADS : (i + WINDOW + 1) * LOADS]):
            copy.start(priority=j % 2)

    score_all(cv_ref[...], xv_ref, e_ref, top_ref, lse_ref, ready)


def score_kernel(xv_ref, mine_ref, theirs_ref, e_ref, cv_ref, top_ref, lse_ref):
    place_halves(mine_ref, theirs_ref, cv_ref)
    score_all(cv_ref[...], xv_ref, e_ref, top_ref, lse_ref, lambda i: None)


def pack_column(ref, base, sub):
    lane = lax.broadcasted_iota(jnp.int32, (8, LANES), 1)
    packed = jnp.zeros((8, LANES), jnp.float32)
    for j in range(sub // 8):
        packed = jnp.where(lane == j, ref[pl.ds(base + 8 * j, 8), :], packed)
    return packed


def combine_lse_kernel(two_ref, one_ref, far_ref, x_ref, out_ref):
    out_ref[...] = four(add_logs, far_ref[...], one_ref[...], two_ref[...], x_ref[...])


def combine_sum_pass_kernel(two_ref, one_ref, far_ref, x_ref, other_ref, out_ref, pass_ref):
    out_ref[...] = four(jnp.add, far_ref[...], one_ref[...], two_ref[...], x_ref[...])
    pass_ref[...] = other_ref[...]


def combine_sum_kernel(two_ref, one_ref, far_ref, x_ref, out_ref):
    out_ref[...] = four(jnp.add, far_ref[...], one_ref[...], two_ref[...], x_ref[...])


def sums_kernel(
    two_ref, one_ref, far_ref, part_ref, e_ref, xv_ref, top_ref,
    keep_ref, send_ref, lse_ref, sums_ref, counts_ref,
):
    tile = xv_ref.shape[0] // TILES
    local_k, width = sums_ref.shape
    parts = keep_ref.shape[0]
    sub = local_k // (2 * parts)
    lse = four_z(add_logs, far_ref[...], one_ref[...], two_ref[...], part_ref[...])
    lse_ref[...] = lse
    scales = jnp.exp(top_ref[...] - lse)
    counts = jnp.zeros((local_k, LANES), jnp.float32)
    for i in range(TILES):
        rows = slice(i * tile, (i + 1) * tile)
        p = e_ref[:, rows] * scales[i : i + 1, :]
        part = p[:, :LANES]
        for j in range(1, tile // LANES):
            part = part + p[:, j * LANES : (j + 1) * LANES]
        counts = counts + part
        dots = jnp.dot(p.astype(jnp.bfloat16), xv_ref[rows, :], preferred_element_type=jnp.float32)
        if i == 0:
            sums_ref[...] = dots
        else:
            sums_ref[...] += dots
    counts_ref[...] = jnp.broadcast_to(jnp.sum(counts, axis=1, keepdims=True), counts.shape)
    core = lax.axis_index("core")
    for out, which in ((keep_ref, core), (send_ref, 1 - core)):
        for h in range(parts):
            base = pl.multiple_of((which * parts + h) * sub, sub)
            for d in range(width // LANES):
                out[h, d * sub : (d + 1) * sub, :] = sums_ref[
                    pl.ds(base, sub), d * LANES : (d + 1) * LANES
                ]
            out[h, (width // LANES) * sub :, :] = pack_column(counts_ref, base, sub)


def halves_kernel(keep_ref, got_ref, a_ref, b_ref):
    a_ref[...] = keep_ref[0] + got_ref[0]
    b_ref[...] = keep_ref[1] + got_ref[1]


def updated(total, old):
    blocks, sub = len(old), old[0].shape[0]
    counts = total[blocks * sub :, :]
    under = [jnp.broadcast_to(counts[:, j : j + 1], (8, LANES)) + 1.0 for j in range(sub // 8)]
    parts = []
    for d in range(blocks):
        for j in range(sub // 8):
            at = d * sub + 8 * j
            parts.append((total[at : at + 8, :] + old[d][8 * j : 8 * j + 8, :]) / under[j])
    return jnp.concatenate(parts, axis=0), counts


def update_kernel(a_ref, a_got_ref, b_ref, b_got_ref, old_ref, out_ref):
    local_k, width = old_ref.shape
    blocks = width // LANES
    sub = local_k // 4
    core = lax.axis_index("core")
    for h, (ref, got_ref) in enumerate(((a_ref, a_got_ref), (b_ref, b_got_ref))):
        base = pl.multiple_of((core * 2 + h) * sub, sub)
        old = [old_ref[pl.ds(base, sub), d * LANES : (d + 1) * LANES] for d in range(blocks)]
        fresh, counts = updated(ref[...] + got_ref[...], old)
        out_ref[h, : blocks * sub, :] = fresh
        out_ref[h, blocks * sub :, :] = counts


def place_halves(mine_ref, theirs_ref, c_ref, counts_ref=None):
    local_k, width = c_ref.shape
    blocks = width // LANES
    sub = local_k // 4
    core = lax.axis_index("core")
    for ref, which in ((mine_ref, core), (theirs_ref, 1 - core)):
        for h in range(2):
            base = pl.multiple_of((which * 2 + h) * sub, sub)
            for d in range(blocks):
                c_ref[pl.ds(base, sub), d * LANES : (d + 1) * LANES] = ref[
                    h, d * sub : (d + 1) * sub, :
                ]
            if counts_ref is not None:
                for j in range(sub // 8):
                    counts_ref[pl.ds(base + 8 * j, 8), :] = jnp.broadcast_to(
                        ref[h, blocks * sub :, j : j + 1], (8, LANES)
                    )


def coarse_logits(g, f):
    inner = lax.dot_general(
        g,
        f,
        (((1,), (1,)), ((), ())),
        precision=lax.Precision.HIGHEST,
        preferred_element_type=jnp.float32,
    )
    sharp = 4.0 * g.shape[1] ** -0.5
    return sharp * (inner - 0.5 * jnp.sum(g * g, axis=1, keepdims=True))


def column_lse(logits):
    top = jnp.max(logits, axis=0, keepdims=True)
    return top + jnp.log(jnp.sum(jnp.exp(logits - top), axis=0, keepdims=True))


def weigh(logits, norm, row, f, out_ref, mass_ref):
    weights = row * jnp.exp(logits - norm)
    totals = lax.dot_general(
        weights,
        f,
        (((1,), (0,)), ((), ())),
        precision=lax.Precision.HIGHEST,
        preferred_element_type=jnp.float32,
    )
    sub, width = totals.shape
    blocks = width // LANES
    for d in range(blocks):
        out_ref[d * sub : (d + 1) * sub, :] = totals[:, d * LANES : (d + 1) * LANES]
    mass_ref[...] = jnp.broadcast_to(jnp.sum(weights, axis=1, keepdims=True), (sub, LANES))
    out_ref[blocks * sub :, :] = pack_column(mass_ref, 0, sub)


def coarse_base():
    return pl.multiple_of((lax.axis_index("x") * 2 + lax.axis_index("core")) * SUB, SUB)


def coarse_first_kernel(
    mine_ref, theirs_ref, g_ref, out_ref, f_ref, row_ref, pass_ref, counts_ref, logits_ref, mass_ref
):
    pass_ref[...] = mine_ref[...]
    place_halves(mine_ref, theirs_ref, f_ref, counts_ref)
    row = jnp.transpose(counts_ref[...])[:1, :]
    row_ref[...] = row
    f = f_ref[...]
    logits = coarse_logits(g_ref[...], f)
    logits_ref[...] = logits
    weigh(logits_ref[pl.ds(coarse_base(), SUB), :], column_lse(logits), row, f, out_ref, mass_ref)


def read_old(old_ref):
    if old_ref.shape[1] == LANES:
        return [old_ref[at : at + SUB, :] for at in range(0, old_ref.shape[0], SUB)]
    base = coarse_base()
    return [old_ref[pl.ds(base, SUB), at : at + LANES] for at in range(0, old_ref.shape[1], LANES)]


def coarse_logits_kernel(
    two_ref, one_ref, far_ref, part_ref, old_ref, f_ref, g_ref, logits_ref, lse_ref
):
    total = four_z(jnp.add, far_ref[...], one_ref[...], two_ref[...], part_ref[...])
    fresh, _ = updated(total, read_old(old_ref))
    g_ref[...] = fresh
    g = jnp.concatenate([fresh[at : at + SUB, :] for at in range(0, fresh.shape[0], SUB)], axis=1)
    logits = coarse_logits(g, f_ref[...])
    logits_ref[...] = logits
    lse_ref[...] = column_lse(logits)


def coarse_logits_out_kernel(
    two_ref, one_ref, far_ref, part_ref, old_ref, f2_ref, f_ref, row_ref, score_ref,
    g_ref, logits_ref, lse_ref, f_out, row_out, score_out, flat_ref, sems,
):
    copies = [
        pltpu.make_async_copy(f_ref, f_out, sems.at[0]),
        pltpu.make_async_copy(row_ref, row_out, sems.at[1]),
        pltpu.make_async_copy(flat_ref, score_out, sems.at[2]),
    ]
    copies[0].start()
    copies[1].start()
    per = score_ref.shape[1] // LANES
    for i in range(score_ref.shape[0]):
        for j in range(per):
            flat_ref[i * per + j : i * per + j + 1, :] = score_ref[
                i : i + 1, j * LANES : (j + 1) * LANES
            ]
    copies[2].start()
    coarse_logits_kernel(
        two_ref, one_ref, far_ref, part_ref, old_ref, f2_ref, g_ref, logits_ref, lse_ref
    )
    for copy in copies:
        copy.wait()


def pair_kernel(mine_ref, theirs_ref, f_ref, row_ref, f2_ref, row2_ref, counts_ref, other_ref):
    local_k = f_ref.shape[0]
    place_halves(mine_ref, theirs_ref, other_ref, counts_ref)
    other_row = jnp.transpose(counts_ref[...])[:1, :]
    odd = lax.rem(lax.axis_index("z"), 2)
    f2_ref[pl.ds(pl.multiple_of(odd * local_k, local_k), local_k), :] = f_ref[...]
    f2_ref[pl.ds(pl.multiple_of((1 - odd) * local_k, local_k), local_k), :] = other_ref[...]
    row = row_ref[...]
    is_odd = jnp.full(row.shape, odd, jnp.int32) == 1
    row2_ref[:, :local_k] = jnp.where(is_odd, other_row, row)
    row2_ref[:, local_k:] = jnp.where(is_odd, row, other_row)


def coarse_weights_kernel(
    two_ref, one_ref, far_ref, part_ref, logits_ref, row_ref, f_ref, out_ref, mass_ref
):
    norm = four(add_logs, far_ref[...], one_ref[...], two_ref[...], part_ref[...])
    weigh(logits_ref[...], norm, row_ref[...], f_ref[...], out_ref, mass_ref)


def coarse_last_kernel(two_ref, one_ref, far_ref, part_ref, old_ref, out_ref):
    total = four_z(jnp.add, far_ref[...], one_ref[...], two_ref[...], part_ref[...])
    fresh, mass = updated(total, read_old(old_ref))
    out_ref[: fresh.shape[0], :] = fresh
    out_ref[fresh.shape[0] :, :] = mass


def stack_kernel(two_ref, one_ref, far_ref, x_ref, out_ref):
    for s, ref in enumerate((x_ref, one_ref, far_ref, two_ref)):
        out_ref[s] = ref[...]


def assemble_kernel(factor, mine_ref, theirs_ref, g_ref, row_ref, counts_ref):
    width = g_ref.shape[1]
    blocks = width // LANES
    chip, core = lax.axis_index("x"), lax.axis_index("core")
    for ref, which in ((mine_ref, core), (theirs_ref, 1 - core)):
        for s in range(mine_ref.shape[0]):
            base = pl.multiple_of((lax.bitwise_xor(chip, s) * 2 + which) * SUB, SUB)
            for d in range(blocks):
                g_ref[pl.ds(base, SUB), d * LANES : (d + 1) * LANES] = ref[
                    s, d * SUB : (d + 1) * SUB, :
                ]
            for j in range(SUB // 8):
                counts_ref[pl.ds(base + 8 * j, 8), :] = jnp.broadcast_to(
                    ref[s, blocks * SUB :, j : j + 1], (8, LANES)
                )
    row_ref[...] = jnp.transpose(counts_ref[...])[:1, :] * factor


def struct(*shape, dtype=jnp.float32):
    return jax.ShapeDtypeStruct(shape, dtype)


def kernel_call(body, out_shape, name, n_in, scratch=(), in_hbm=0, out_hbm=0):
    many = isinstance(out_shape, list)
    anywhere = pl.BlockSpec(memory_space=pl.ANY)
    spec = pl.BlockSpec(memory_space=pltpu.VMEM)
    return pl.pallas_call(
        body,
        out_shape=out_shape,
        in_specs=[anywhere] * in_hbm + [spec] * (n_in - in_hbm),
        out_specs=[spec] * (len(out_shape) - out_hbm) + [anywhere] * out_hbm if many else spec,
        scratch_shapes=list(scratch),
        compiler_params=pltpu.CompilerParams(vmem_limit_bytes=24 * 1024 * 1024),
        name=name,
    )


def per_device(sketches, centroids, coarse_init):
    nx, nc = lax.axis_size("x"), lax.axis_size("core")
    ny, nz = lax.axis_size("y"), lax.axis_size("z")
    n_row, n_cent = nx * nc, ny * nz
    rows, width = sketches.shape
    local_k = centroids.shape[0]
    tile = rows // TILES
    blocks = width // LANES

    small = struct(blocks * SUB + 8, LANES)
    half = struct(blocks * local_k // 4 + 8, LANES)
    halves = struct(2, blocks * local_k // 4 + 8, LANES)
    column = pltpu.VMEM((local_k, LANES), jnp.float32)
    exps_out = pltpu.VMEM((local_k, rows), jnp.float32)
    cents_out = pltpu.VMEM((local_k, width), jnp.float32)
    by_row = struct(TILES, tile)

    for round_index in range(ROUNDS):
        if round_index == 0:
            exps, held, cents, top, part = kernel_call(
                score_load_kernel,
                [exps_out, pltpu.VMEM((rows, width), jnp.bfloat16), cents_out, by_row, by_row],
                "scores_first",
                2,
                scratch=[pltpu.SemaphoreType.DMA((TILES * LOADS,)), pltpu.SemaphoreType.DMA],
                in_hbm=2,
            )(
                pltpu.with_memory_space_constraint(sketches, pltpu.HBM),
                pltpu.with_memory_space_constraint(centroids, pltpu.HBM),
            )
        else:
            exps, cents, top, part = kernel_call(
                score_kernel, [exps_out, cents_out, by_row, by_row], "scores", 3
            )(held, mine, theirs)
        part = kernel_call(combine_lse_kernel, by_row, "lse_y", 4)(
            *burst(part, "y"), part
        )
        part = add_logs(part, swap(part, "z", 1))
        keep, send, lse = kernel_call(
            sums_kernel,
            [halves, halves, by_row],
            "sums",
            7,
            scratch=[pltpu.VMEM((local_k, width), jnp.float32), column],
        )(*burst(part, "z"), part, exps, held, top)
        a, b = kernel_call(halves_kernel, [half, half], "halves", 2)(keep, swap(send, "core", 1))
        a_got, b_got = swap(a, "x", 1), swap(b, "x", 3)
        a, b = a + a_got, b + b_got
        mine = kernel_call(update_kernel, halves, "update", 5)(
            a, swap(a, "x", 3), b, swap(b, "x", 1), cents
        )
        theirs = swap(mine, "core", 1)

    mass = pltpu.VMEM((SUB, LANES), jnp.float32)
    for iteration in range(COARSE_ITERS):
        if iteration == 0:
            packed, cents, row, mine = kernel_call(
                coarse_first_kernel,
                [small, cents_out, pltpu.VMEM((1, local_k), jnp.float32), halves],
                "coarse_first",
                3,
                scratch=[column, pltpu.VMEM((coarse_init.shape[0], local_k), jnp.float32), mass],
            )(mine, theirs, coarse_init)
            old = coarse_init
        else:
            outs = [struct(blocks * SUB, LANES), struct(SUB, 2 * local_k), struct(1, 2 * local_k)]
            if iteration == 1:
                cents_pair, row_pair = kernel_call(
                    pair_kernel,
                    [
                        pltpu.VMEM((2 * local_k, width), jnp.float32),
                        pltpu.VMEM((1, 2 * local_k), jnp.float32),
                    ],
                    "pair",
                    4,
                    scratch=[column, pltpu.VMEM((local_k, width), jnp.float32)],
                )(*pair, cents, row)
                old, logits, part, fine_centroids, fine_counts, row_score = kernel_call(
                    coarse_logits_out_kernel,
                    outs
                    + [
                        pltpu.HBM((local_k, width), jnp.float32),
                        pltpu.HBM((1, local_k), jnp.float32),
                        pltpu.HBM((rows // LANES, LANES), jnp.float32),
                    ],
                    "coarse_logits_out",
                    9,
                    scratch=[
                        pltpu.VMEM((rows // LANES, LANES), jnp.float32),
                        pltpu.SemaphoreType.DMA((3,)),
                    ],
                    out_hbm=3,
                )(*z_parts, packed, old, cents_pair, cents, row, lse)
            else:
                old, logits, part = kernel_call(coarse_logits_kernel, outs, "coarse_logits", 6)(
                    *z_parts, packed, old, cents_pair
                )
            part = add_logs(part, swap(part, "core", 1))
            packed = kernel_call(coarse_weights_kernel, small, "coarse_weights", 7, scratch=[mass])(
                *burst(part, "x"), part, logits, row_pair, cents_pair
            )
        parts = (*burst(packed, "y"), packed)
        if iteration == 0:
            packed, pair = kernel_call(combine_sum_pass_kernel, [small, halves], "sum_y_pass", 5)(
                *parts, swap(mine, "z", 1)
            )
            pair = (pair, swap(pair, "core", 1))
            packed = packed + swap(packed, "z", 1)
        else:
            packed = kernel_call(combine_sum_kernel, small, "sum_y", 4)(*parts)
        z_parts = burst(packed, "z")
    last = kernel_call(coarse_last_kernel, small, "coarse_last", 5)(*z_parts, packed, old)
    mine = kernel_call(stack_kernel, struct(nx, *small.shape), "stack", 4)(
        *burst(last, "x"), last
    )
    all_rows = rows * n_row
    all_cents = local_k * n_cent
    coarse, masses = kernel_call(
        functools.partial(assemble_kernel, all_cents / all_rows),
        [struct(local_k, width), struct(1, local_k)],
        "assemble",
        2,
        scratch=[column],
    )(mine, swap(mine, "core", 1))
    return (
        fine_centroids,
        fine_counts.reshape(local_k),
        coarse,
        masses.reshape(local_k),
        row_score.reshape(rows),
    )


def solution(mesh):
    n_row, n_cent = mesh.shape["row"], mesh.shape["cent"]
    fine = Mesh(mesh.devices.reshape(n_row // 2, 2, n_cent // 8, 8), ("x", "core", "y", "z"))
    row, cent = ("x", "core"), ("y", "z")
    in_specs = (P(row, None), P(cent, None), P())
    out_specs = (P(cent, None), P(cent), P(), P(), P(row))
    return jax.shard_map(
        per_device, mesh=fine, in_specs=in_specs, out_specs=out_specs, check_vma=False
    )
```

```python
import functools
import math

import jax
import jax.numpy as jnp
from jax import lax
from jax.experimental import pallas as pl
from jax.experimental.pallas import tpu as pltpu
from jax.sharding import Mesh, PartitionSpec as P

ROUNDS = 2
COARSE_ITERS = 3
LANES = 128
TILES = 8
WINDOW = 3
LOADS = 2
SUB = 32


def swap(x, axis, bits):
    size = lax.axis_size(axis)
    return lax.ppermute(x, axis, [(i, i ^ bits) for i in range(size)])


def add_logs(a, b):
    return jnp.maximum(a, b) + jnp.log1p(jnp.exp(-jnp.abs(a - b)))


def fetch(x, axis, source):
    return lax.ppermute(x, axis, [(source(i), i) for i in range(lax.axis_size(axis))])


def burst(x, axis):
    if axis == "z":
        size = lax.axis_size(axis)
        return [
            fetch(x, axis, lambda i: (i + 1 if i % 2 else i - 1) % size),
            fetch(x, axis, lambda i: (i - 2 if i % 2 else i + 2) % size),
            swap(x, axis, 5),
        ]
    return [swap(x, axis, bits) for bits in (3, 1, 2)]


def four(combine, far, one, two, x):
    return combine(combine(x, far), combine(one, two))


def four_z(combine, far, one, two, x):
    z = lax.axis_index("z")
    swapped = lax.rem(lax.shift_right_logical(z, 1) + lax.rem(z, 2), 2)
    mask = jnp.full(x.shape, swapped, jnp.int32) == 0
    first = jnp.where(mask, one, two)
    second = jnp.where(mask, two, one)
    return combine(combine(x, first), combine(second, far))


def tile_dots(c_bf, x_ref, i, tile):
    return lax.dot_general(
        c_bf,
        x_ref[i * tile : (i + 1) * tile, :],
        (((1,), (1,)), ((), ())),
        preferred_element_type=jnp.float32,
    )


def finish_tile(dots, half, i, factor, e_ref, top_ref, lse_ref):
    tile = dots.shape[1]
    dots = dots - half
    top = jnp.max(dots, axis=0, keepdims=True)
    exps = jnp.exp2((dots - top) * (factor * math.log2(math.e)))
    total = jnp.sum(exps, axis=0, keepdims=True)
    top = top * factor
    e_ref[:, i * tile : (i + 1) * tile] = exps
    top_ref[i : i + 1, :] = top
    lse_ref[i : i + 1, :] = top + jnp.log(total)


def score_all(c, xv_ref, e_ref, top_ref, lse_ref, ready):
    tile = xv_ref.shape[0] // TILES
    factor = c.shape[1] ** -0.5
    c_bf = c.astype(jnp.bfloat16)
    half = 0.5 * jnp.sum(c * c, axis=1, keepdims=True)
    previous = None
    for i in range(TILES):
        ready(i)
        dots = tile_dots(c_bf, xv_ref, i, tile)
        if i:
            finish_tile(previous, half, i - 1, factor, e_ref, top_ref, lse_ref)
        previous = dots
    finish_tile(previous, half, TILES - 1, factor, e_ref, top_ref, lse_ref)


def score_load_kernel(x_ref, c_ref, e_ref, xv_ref, cv_ref, top_ref, lse_ref, sems, c_sem):
    step = xv_ref.shape[0] // (TILES * LOADS)
    c_copy = pltpu.make_async_copy(c_ref, cv_ref, c_sem)
    c_copy.start()
    copies = [
        pltpu.make_async_copy(
            x_ref.at[pl.ds(i * step, step)], xv_ref.at[pl.ds(i * step, step)], sems.at[i]
        )
        for i in range(TILES * LOADS)
    ]
    for i in range(LOADS):
        copies[i].start(priority=i % 2)
    c_copy.wait()
    for i in range(LOADS, (WINDOW + 1) * LOADS):
        copies[i].start(priority=i % 2)

    def ready(i):
        for copy in copies[i * LOADS : (i + 1) * LOADS]:
            copy.wait()
        for j, copy in enumerate(copies[(i + WINDOW + 1) * LOADS : (i + WINDOW + 2) * LOADS]):
            copy.start(priority=j % 2)

    score_all(cv_ref[...], xv_ref, e_ref, top_ref, lse_ref, ready)


def score_kernel(xv_ref, mine_ref, theirs_ref, e_ref, cv_ref, top_ref, lse_ref):
    place_halves(mine_ref, theirs_ref, cv_ref)
    score_all(cv_ref[...], xv_ref, e_ref, top_ref, lse_ref, lambda i: None)


def pack_column(ref, base, sub):
    lane = lax.broadcasted_iota(jnp.int32, (8, LANES), 1)
    packed = jnp.zeros((8, LANES), jnp.float32)
    for j in range(sub // 8):
        packed = jnp.where(lane == j, ref[pl.ds(base + 8 * j, 8), :], packed)
    return packed


def combine_lse_kernel(two_ref, one_ref, far_ref, x_ref, out_ref):
    out_ref[...] = four(add_logs, far_ref[...], one_ref[...], two_ref[...], x_ref[...])


def combine_sum_pass_kernel(two_ref, one_ref, far_ref, x_ref, other_ref, out_ref, pass_ref):
    out_ref[...] = four(jnp.add, far_ref[...], one_ref[...], two_ref[...], x_ref[...])
    pass_ref[...] = other_ref[...]


def combine_sum_kernel(two_ref, one_ref, far_ref, x_ref, out_ref):
    out_ref[...] = four(jnp.add, far_ref[...], one_ref[...], two_ref[...], x_ref[...])


def sums_kernel(
    two_ref, one_ref, far_ref, part_ref, e_ref, xv_ref, top_ref,
    keep_ref, send_ref, lse_ref, sums_ref, counts_ref,
):
    tile = xv_ref.shape[0] // TILES
    local_k, width = sums_ref.shape
    parts = keep_ref.shape[0]
    sub = local_k // (2 * parts)
    lse = four_z(add_logs, far_ref[...], one_ref[...], two_ref[...], part_ref[...])
    lse_ref[...] = lse
    scales = jnp.exp(top_ref[...] - lse)
    counts = jnp.zeros((local_k, LANES), jnp.float32)
    for i in range(TILES):
        rows = slice(i * tile, (i + 1) * tile)
        p = e_ref[:, rows] * scales[i : i + 1, :]
        part = p[:, :LANES]
        for j in range(1, tile // LANES):
            part = part + p[:, j * LANES : (j + 1) * LANES]
        counts = counts + part
        dots = jnp.dot(p.astype(jnp.bfloat16), xv_ref[rows, :], preferred_element_type=jnp.float32)
        if i == 0:
            sums_ref[...] = dots
        else:
            sums_ref[...] += dots
    counts_ref[...] = jnp.broadcast_to(jnp.sum(counts, axis=1, keepdims=True), counts.shape)
    core = lax.axis_index("core")
    for out, which in ((keep_ref, core), (send_ref, 1 - core)):
        for h in range(parts):
            base = pl.multiple_of((which * parts + h) * sub, sub)
            for d in range(width // LANES):
                out[h, d * sub : (d + 1) * sub, :] = sums_ref[
                    pl.ds(base, sub), d * LANES : (d + 1) * LANES
                ]
            out[h, (width // LANES) * sub :, :] = pack_column(counts_ref, base, sub)


def halves_kernel(keep_ref, got_ref, a_ref, b_ref):
    a_ref[...] = keep_ref[0] + got_ref[0]
    b_ref[...] = keep_ref[1] + got_ref[1]


def updated(total, old):
    blocks, sub = len(old), old[0].shape[0]
    counts = total[blocks * sub :, :]
    under = [jnp.broadcast_to(counts[:, j : j + 1], (8, LANES)) + 1.0 for j in range(sub // 8)]
    parts = []
    for d in range(blocks):
        for j in range(sub // 8):
            at = d * sub + 8 * j
            parts.append((total[at : at + 8, :] + old[d][8 * j : 8 * j + 8, :]) / under[j])
    return jnp.concatenate(parts, axis=0), counts


def update_kernel(a_ref, a_got_ref, b_ref, b_got_ref, old_ref, out_ref):
    local_k, width = old_ref.shape
    blocks = width // LANES
    sub = local_k // 4
    core = lax.axis_index("core")
    for h, (ref, got_ref) in enumerate(((a_ref, a_got_ref), (b_ref, b_got_ref))):
        base = pl.multiple_of((core * 2 + h) * sub, sub)
        old = [old_ref[pl.ds(base, sub), d * LANES : (d + 1) * LANES] for d in range(blocks)]
        fresh, counts = updated(ref[...] + got_ref[...], old)
        out_ref[h, : blocks * sub, :] = fresh
        out_ref[h, blocks * sub :, :] = counts


def place_halves(mine_ref, theirs_ref, c_ref, counts_ref=None):
    local_k, width = c_ref.shape
    blocks = width // LANES
    sub = local_k // 4
    core = lax.axis_index("core")
    for ref, which in ((mine_ref, core), (theirs_ref, 1 - core)):
        for h in range(2):
            base = pl.multiple_of((which * 2 + h) * sub, sub)
            for d in range(blocks):
                c_ref[pl.ds(base, sub), d * LANES : (d + 1) * LANES] = ref[
                    h, d * sub : (d + 1) * sub, :
                ]
            if counts_ref is not None:
                for j in range(sub // 8):
                    counts_ref[pl.ds(base + 8 * j, 8), :] = jnp.broadcast_to(
                        ref[h, blocks * sub :, j : j + 1], (8, LANES)
                    )


def coarse_logits(g, f):
    inner = lax.dot_general(
        g,
        f,
        (((1,), (1,)), ((), ())),
        precision=lax.Precision.HIGHEST,
        preferred_element_type=jnp.float32,
    )
    sharp = 4.0 * g.shape[1] ** -0.5
    return sharp * (inner - 0.5 * jnp.sum(g * g, axis=1, keepdims=True))


def column_lse(logits):
    top = jnp.max(logits, axis=0, keepdims=True)
    return top + jnp.log(jnp.sum(jnp.exp(logits - top), axis=0, keepdims=True))


def pack_totals(totals, weights, out_ref, mass_ref):
    sub, width = totals.shape
    blocks = width // LANES
    for d in range(blocks):
        out_ref[d * sub : (d + 1) * sub, :] = totals[:, d * LANES : (d + 1) * LANES]
    mass_ref[...] = jnp.broadcast_to(jnp.sum(weights, axis=1, keepdims=True), (sub, LANES))
    out_ref[blocks * sub :, :] = pack_column(mass_ref, 0, sub)


def coarse_base():
    return pl.multiple_of((lax.axis_index("x") * 2 + lax.axis_index("core")) * SUB, SUB)


def coarse_first_kernel(
    mine_ref, theirs_ref, g_ref, out_ref, f_ref, row_ref, pass_ref, counts_ref, logits_ref, mass_ref
):
    pass_ref[...] = mine_ref[...]
    place_halves(mine_ref, theirs_ref, f_ref, counts_ref)
    row = jnp.transpose(counts_ref[...])[:1, :]
    row_ref[...] = row
    f = f_ref[...]
    logits = coarse_logits(g_ref[...], f)
    logits_ref[...] = logits
    weights = row * jnp.exp(logits_ref[pl.ds(coarse_base(), SUB), :] - column_lse(logits))
    totals = lax.dot_general(
        weights,
        f,
        (((1,), (0,)), ((), ())),
        precision=lax.Precision.HIGHEST,
        preferred_element_type=jnp.float32,
    )
    pack_totals(totals, weights, out_ref, mass_ref)


def read_old(old_ref):
    if old_ref.shape[1] == LANES:
        return [old_ref[at : at + SUB, :] for at in range(0, old_ref.shape[0], SUB)]
    base = coarse_base()
    return [old_ref[pl.ds(base, SUB), at : at + LANES] for at in range(0, old_ref.shape[1], LANES)]


def split_three(x):
    high = x.astype(jnp.bfloat16)
    rest = x - high.astype(jnp.float32)
    mid = rest.astype(jnp.bfloat16)
    low = (rest - mid.astype(jnp.float32)).astype(jnp.bfloat16)
    return high, mid, low


def six_products(x, f_parts, contract):
    high, mid, low = split_three(x)
    n = x.shape[0]
    dims = (((1,), (contract,)), ((), ()))

    def dot(a, b):
        return lax.dot_general(a, b, dims, preferred_element_type=jnp.float32)

    by_high = dot(jnp.concatenate([high, mid, low], axis=0), f_parts[0])
    by_mid = dot(jnp.concatenate([high, mid], axis=0), f_parts[1])
    by_low = dot(high, f_parts[2])
    small = (by_high[2 * n :] + by_low) + by_mid[n:]
    return (small + (by_high[n : 2 * n] + by_mid[:n])) + by_high[:n]


def coarse_logits_kernel(
    two_ref, one_ref, far_ref, part_ref, old_ref, f_high, f_mid, f_low, g_ref, logits_ref, lse_ref
):
    total = four_z(jnp.add, far_ref[...], one_ref[...], two_ref[...], part_ref[...])
    fresh, _ = updated(total, read_old(old_ref))
    g_ref[...] = fresh
    g = jnp.concatenate([fresh[at : at + SUB, :] for at in range(0, fresh.shape[0], SUB)], axis=1)
    inner = six_products(g, (f_high[...], f_mid[...], f_low[...]), 1)
    sharp = 4.0 * g.shape[1] ** -0.5
    logits = sharp * (inner - 0.5 * jnp.sum(g * g, axis=1, keepdims=True))
    logits_ref[...] = logits
    lse_ref[...] = column_lse(logits)


def pair_kernel(
    mine_ref, theirs_ref, f_ref, row_ref, score_ref,
    f_high, f_mid, f_low, row2_ref, f_out, row_out, score_out,
    counts_ref, other_ref, flat_ref, sems,
):
    copies = [
        pltpu.make_async_copy(f_ref, f_out, sems.at[0]),
        pltpu.make_async_copy(row_ref, row_out, sems.at[1]),
        pltpu.make_async_copy(flat_ref, score_out, sems.at[2]),
    ]
    copies[0].start()
    copies[1].start()
    per = score_ref.shape[1] // LANES
    for i in range(score_ref.shape[0]):
        for j in range(per):
            flat_ref[i * per + j : i * per + j + 1, :] = score_ref[
                i : i + 1, j * LANES : (j + 1) * LANES
            ]
    copies[2].start()
    local_k = f_ref.shape[0]
    place_halves(mine_ref, theirs_ref, other_ref, counts_ref)
    other_row = jnp.transpose(counts_ref[...])[:1, :]
    odd = lax.rem(lax.axis_index("z"), 2)
    for source, at in ((f_ref, odd), (other_ref, 1 - odd)):
        rows = pl.ds(pl.multiple_of(at * local_k, local_k), local_k)
        for out, part in zip((f_high, f_mid, f_low), split_three(source[...])):
            out[rows, :] = part
    row = row_ref[...]
    is_odd = jnp.full(row.shape, odd, jnp.int32) == 1
    row2_ref[:, :local_k] = jnp.where(is_odd, other_row, row)
    row2_ref[:, local_k:] = jnp.where(is_odd, row, other_row)
    for copy in copies:
        copy.wait()


def coarse_weights_kernel(
    two_ref, one_ref, far_ref, part_ref, logits_ref, row_ref, f_high, f_mid, f_low, out_ref, mass_ref
):
    norm = four(add_logs, far_ref[...], one_ref[...], two_ref[...], part_ref[...])
    weights = row_ref[...] * jnp.exp(logits_ref[...] - norm)
    totals = six_products(weights, (f_high[...], f_mid[...], f_low[...]), 0)
    pack_totals(totals, weights, out_ref, mass_ref)


def coarse_last_kernel(two_ref, one_ref, far_ref, part_ref, old_ref, out_ref):
    total = four_z(jnp.add, far_ref[...], one_ref[...], two_ref[...], part_ref[...])
    fresh, mass = updated(total, read_old(old_ref))
    out_ref[: fresh.shape[0], :] = fresh
    out_ref[fresh.shape[0] :, :] = mass


def stack_kernel(two_ref, one_ref, far_ref, x_ref, out_ref):
    for s, ref in enumerate((x_ref, one_ref, far_ref, two_ref)):
        out_ref[s] = ref[...]


def assemble_kernel(factor, mine_ref, theirs_ref, g_ref, row_ref, counts_ref):
    width = g_ref.shape[1]
    blocks = width // LANES
    chip, core = lax.axis_index("x"), lax.axis_index("core")
    for ref, which in ((mine_ref, core), (theirs_ref, 1 - core)):
        for s in range(mine_ref.shape[0]):
            base = pl.multiple_of((lax.bitwise_xor(chip, s) * 2 + which) * SUB, SUB)
            for d in range(blocks):
                g_ref[pl.ds(base, SUB), d * LANES : (d + 1) * LANES] = ref[
                    s, d * SUB : (d + 1) * SUB, :
                ]
            for j in range(SUB // 8):
                counts_ref[pl.ds(base + 8 * j, 8), :] = jnp.broadcast_to(
                    ref[s, blocks * SUB :, j : j + 1], (8, LANES)
                )
    row_ref[...] = jnp.transpose(counts_ref[...])[:1, :] * factor


def struct(*shape, dtype=jnp.float32):
    return jax.ShapeDtypeStruct(shape, dtype)


def kernel_call(body, out_shape, name, n_in, scratch=(), in_hbm=0, out_hbm=0):
    many = isinstance(out_shape, list)
    anywhere = pl.BlockSpec(memory_space=pl.ANY)
    spec = pl.BlockSpec(memory_space=pltpu.VMEM)
    return pl.pallas_call(
        body,
        out_shape=out_shape,
        in_specs=[anywhere] * in_hbm + [spec] * (n_in - in_hbm),
        out_specs=[spec] * (len(out_shape) - out_hbm) + [anywhere] * out_hbm if many else spec,
        scratch_shapes=list(scratch),
        compiler_params=pltpu.CompilerParams(vmem_limit_bytes=24 * 1024 * 1024),
        name=name,
    )


def per_device(sketches, centroids, coarse_init):
    nx, nc = lax.axis_size("x"), lax.axis_size("core")
    ny, nz = lax.axis_size("y"), lax.axis_size("z")
    n_row, n_cent = nx * nc, ny * nz
    rows, width = sketches.shape
    local_k = centroids.shape[0]
    tile = rows // TILES
    blocks = width // LANES

    small = struct(blocks * SUB + 8, LANES)
    half = struct(blocks * local_k // 4 + 8, LANES)
    halves = struct(2, blocks * local_k // 4 + 8, LANES)
    column = pltpu.VMEM((local_k, LANES), jnp.float32)
    exps_out = pltpu.VMEM((local_k, rows), jnp.float32)
    cents_out = pltpu.VMEM((local_k, width), jnp.float32)
    by_row = struct(TILES, tile)

    for round_index in range(ROUNDS):
        if round_index == 0:
            exps, held, cents, top, part = kernel_call(
                score_load_kernel,
                [exps_out, pltpu.VMEM((rows, width), jnp.bfloat16), cents_out, by_row, by_row],
                "scores_first",
                2,
                scratch=[pltpu.SemaphoreType.DMA((TILES * LOADS,)), pltpu.SemaphoreType.DMA],
                in_hbm=2,
            )(
                pltpu.with_memory_space_constraint(sketches, pltpu.HBM),
                pltpu.with_memory_space_constraint(centroids, pltpu.HBM),
            )
        else:
            exps, cents, top, part = kernel_call(
                score_kernel, [exps_out, cents_out, by_row, by_row], "scores", 3
            )(held, mine, theirs)
        part = kernel_call(combine_lse_kernel, by_row, "lse_y", 4)(
            *burst(part, "y"), part
        )
        part = add_logs(part, swap(part, "z", 1))
        keep, send, lse = kernel_call(
            sums_kernel,
            [halves, halves, by_row],
            "sums",
            7,
            scratch=[pltpu.VMEM((local_k, width), jnp.float32), column],
        )(*burst(part, "z"), part, exps, held, top)
        a, b = kernel_call(halves_kernel, [half, half], "halves", 2)(keep, swap(send, "core", 1))
        a_got, b_got = swap(a, "x", 1), swap(b, "x", 3)
        a, b = a + a_got, b + b_got
        mine = kernel_call(update_kernel, halves, "update", 5)(
            a, swap(a, "x", 3), b, swap(b, "x", 1), cents
        )
        theirs = swap(mine, "core", 1)

    mass = pltpu.VMEM((SUB, LANES), jnp.float32)
    for iteration in range(COARSE_ITERS):
        if iteration == 0:
            packed, cents, row, mine = kernel_call(
                coarse_first_kernel,
                [small, cents_out, pltpu.VMEM((1, local_k), jnp.float32), halves],
                "coarse_first",
                3,
                scratch=[column, pltpu.VMEM((coarse_init.shape[0], local_k), jnp.float32), mass],
            )(mine, theirs, coarse_init)
            old = coarse_init
        else:
            if iteration == 1:
                f_part = pltpu.VMEM((2 * local_k, width), jnp.bfloat16)
                *f_parts, row_pair, fine_centroids, fine_counts, row_score = kernel_call(
                    pair_kernel,
                    [f_part, f_part, f_part, pltpu.VMEM((1, 2 * local_k), jnp.float32)]
                    + [
                        pltpu.HBM((local_k, width), jnp.float32),
                        pltpu.HBM((1, local_k), jnp.float32),
                        pltpu.HBM((rows // LANES, LANES), jnp.float32),
                    ],
                    "pair",
                    5,
                    scratch=[
                        column,
                        pltpu.VMEM((local_k, width), jnp.float32),
                        pltpu.VMEM((rows // LANES, LANES), jnp.float32),
                        pltpu.SemaphoreType.DMA((3,)),
                    ],
                    out_hbm=3,
                )(*pair, cents, row, lse)
            old, logits, part = kernel_call(
                coarse_logits_kernel,
                [struct(blocks * SUB, LANES), struct(SUB, 2 * local_k), struct(1, 2 * local_k)],
                "coarse_logits",
                8,
            )(*z_parts, packed, old, *f_parts)
            part = add_logs(part, swap(part, "core", 1))
            packed = kernel_call(coarse_weights_kernel, small, "coarse_weights", 9, scratch=[mass])(
                *burst(part, "x"), part, logits, row_pair, *f_parts
            )
        parts = (*burst(packed, "y"), packed)
        if iteration == 0:
            packed, pair = kernel_call(combine_sum_pass_kernel, [small, halves], "sum_y_pass", 5)(
                *parts, swap(mine, "z", 1)
            )
            pair = (pair, swap(pair, "core", 1))
            packed = packed + swap(packed, "z", 1)
        else:
            packed = kernel_call(combine_sum_kernel, small, "sum_y", 4)(*parts)
        z_parts = burst(packed, "z")
    last = kernel_call(coarse_last_kernel, small, "coarse_last", 5)(*z_parts, packed, old)
    mine = kernel_call(stack_kernel, struct(nx, *small.shape), "stack", 4)(
        *burst(last, "x"), last
    )
    all_rows = rows * n_row
    all_cents = local_k * n_cent
    coarse, masses = kernel_call(
        functools.partial(assemble_kernel, all_cents / all_rows),
        [struct(local_k, width), struct(1, local_k)],
        "assemble",
        2,
        scratch=[column],
    )(mine, swap(mine, "core", 1))
    return (
        fine_centroids,
        fine_counts.reshape(local_k),
        coarse,
        masses.reshape(local_k),
        row_score.reshape(rows),
    )


def solution(mesh):
    n_row, n_cent = mesh.shape["row"], mesh.shape["cent"]
    fine = Mesh(mesh.devices.reshape(n_row // 2, 2, n_cent // 8, 8), ("x", "core", "y", "z"))
    row, cent = ("x", "core"), ("y", "z")
    in_specs = (P(row, None), P(cent, None), P())
    out_specs = (P(cent, None), P(cent), P(), P(), P(row))
    return jax.shard_map(
        per_device, mesh=fine, in_specs=in_specs, out_specs=out_specs, check_vma=False
    )
```

```python
import functools
import math

import jax
import jax.numpy as jnp
from jax import lax
from jax.experimental import pallas as pl
from jax.experimental.pallas import tpu as pltpu
from jax.sharding import Mesh, PartitionSpec as P

ROUNDS = 2
COARSE_ITERS = 3
LANES = 128
TILES = 8
WINDOW = 8
SUB = 32


def swap(x, axis, bits):
    size = lax.axis_size(axis)
    return lax.ppermute(x, axis, [(i, i ^ bits) for i in range(size)])


def add_logs(a, b):
    return jnp.maximum(a, b) + jnp.log1p(jnp.exp(-jnp.abs(a - b)))


def fetch(x, axis, source):
    return lax.ppermute(x, axis, [(source(i), i) for i in range(lax.axis_size(axis))])


def burst(x, axis):
    if axis == "z":
        size = lax.axis_size(axis)
        return [
            fetch(x, axis, lambda i: (i + 1 if i % 2 else i - 1) % size),
            fetch(x, axis, lambda i: (i - 2 if i % 2 else i + 2) % size),
            swap(x, axis, 5),
        ]
    return [swap(x, axis, bits) for bits in (3, 1, 2)]


def four(combine, far, one, two, x):
    return combine(combine(x, far), combine(one, two))


def four_z(combine, far, one, two, x):
    z = lax.axis_index("z")
    swapped = lax.rem(lax.shift_right_logical(z, 1) + lax.rem(z, 2), 2)
    mask = jnp.full(x.shape, swapped, jnp.int32) == 0
    first = jnp.where(mask, one, two)
    second = jnp.where(mask, two, one)
    return combine(combine(x, first), combine(second, far))


def tile_dots(c_bf, x_ref, i, tile):
    return lax.dot_general(
        c_bf,
        x_ref[i * tile : (i + 1) * tile, :],
        (((1,), (1,)), ((), ())),
        preferred_element_type=jnp.float32,
    )


def finish_tile(dots, half, i, factor, e_ref, top_ref, lse_ref):
    tile = dots.shape[1]
    dots = dots - half
    top = jnp.max(dots, axis=0, keepdims=True)
    exps = jnp.exp2((dots - top) * (factor * math.log2(math.e)))
    total = jnp.sum(exps, axis=0, keepdims=True)
    top = top * factor
    e_ref[:, i * tile : (i + 1) * tile] = exps
    top_ref[i : i + 1, :] = top
    lse_ref[i : i + 1, :] = top + jnp.log(total)


def score_all(c, xv_ref, e_ref, top_ref, lse_ref):
    tile = xv_ref.shape[0] // TILES
    factor = c.shape[1] ** -0.5
    c_bf = c.astype(jnp.bfloat16)
    half = 0.5 * jnp.sum(c * c, axis=1, keepdims=True)
    previous = None
    for i in range(TILES):
        dots = tile_dots(c_bf, xv_ref, i, tile)
        if i:
            finish_tile(previous, half, i - 1, factor, e_ref, top_ref, lse_ref)
        previous = dots
    finish_tile(previous, half, TILES - 1, factor, e_ref, top_ref, lse_ref)


def score_load_kernel(
    x_ref, c_ref, e_ref, xv_ref, cv_ref, top_ref, lse_ref, even_ref, odd_ref, sems, c_sem
):
    tile = even_ref.shape[1]
    count = xv_ref.shape[0] // tile

    def load(i):
        rows = pl.ds(pl.multiple_of(i * tile, tile), tile)
        return pltpu.make_async_copy(x_ref.at[rows], xv_ref.at[rows], sems.at[i])

    c_copy = pltpu.make_async_copy(c_ref, cv_ref, c_sem)
    c_copy.start()
    for i in range(WINDOW):
        load(i).start(priority=i % 2)
    c_copy.wait()
    c = cv_ref[...]
    factor = c.shape[1] ** -0.5
    c_bf = c.astype(jnp.bfloat16)
    half = 0.5 * jnp.sum(c * c, axis=1, keepdims=True)

    def dots(i, out_ref, parity):
        load(i).wait()

        @pl.when(i + WINDOW < count)
        def _():
            load(i + WINDOW).start(priority=parity)

        out_ref[...] = lax.dot_general(
            c_bf,
            xv_ref[pl.ds(pl.multiple_of(i * tile, tile), tile), :],
            (((1,), (1,)), ((), ())),
            preferred_element_type=jnp.float32,
        )

    def finish(j, parity, dots_ref):
        values = dots_ref[...] - half
        top = jnp.max(values, axis=0, keepdims=True)
        exps = jnp.exp2((values - top) * (factor * math.log2(math.e)))
        total = jnp.sum(exps, axis=0, keepdims=True)
        top = top * factor
        lanes = slice(parity * tile, (parity + 1) * tile)
        e_ref[:, pl.ds(pl.multiple_of((2 * j + parity) * tile, tile), tile)] = exps
        top_ref[pl.ds(j, 1), lanes] = top
        lse_ref[pl.ds(j, 1), lanes] = top + jnp.log(total)

    dots(0, even_ref, 0)

    def body(j, carry):
        dots(2 * j + 1, odd_ref, 1)
        finish(j, 0, even_ref)
        dots(2 * j + 2, even_ref, 0)
        finish(j, 1, odd_ref)
        return carry

    lax.fori_loop(0, count // 2 - 1, body, 0)
    dots(count - 1, odd_ref, 1)
    finish(count // 2 - 1, 0, even_ref)
    finish(count // 2 - 1, 1, odd_ref)


def score_kernel(xv_ref, mine_ref, theirs_ref, e_ref, cv_ref, top_ref, lse_ref):
    place_halves(mine_ref, theirs_ref, cv_ref)
    score_all(cv_ref[...], xv_ref, e_ref, top_ref, lse_ref)


def pack_column(ref, base, sub):
    lane = lax.broadcasted_iota(jnp.int32, (8, LANES), 1)
    packed = jnp.zeros((8, LANES), jnp.float32)
    for j in range(sub // 8):
        packed = jnp.where(lane == j, ref[pl.ds(base + 8 * j, 8), :], packed)
    return packed


def combine_lse_kernel(two_ref, one_ref, far_ref, x_ref, out_ref):
    out_ref[...] = four(add_logs, far_ref[...], one_ref[...], two_ref[...], x_ref[...])


def add_pass_kernel(x_ref, got_ref, other_ref, out_ref, pass_ref):
    out_ref[...] = x_ref[...] + got_ref[...]
    pass_ref[...] = other_ref[...]


def combine_sum_kernel(two_ref, one_ref, far_ref, x_ref, out_ref):
    out_ref[...] = four(jnp.add, far_ref[...], one_ref[...], two_ref[...], x_ref[...])


def sums_kernel(
    two_ref, one_ref, far_ref, part_ref, e_ref, xv_ref, top_ref,
    keep_ref, send_ref, lse_ref, sums_ref, counts_ref,
):
    tile = xv_ref.shape[0] // TILES
    local_k, width = sums_ref.shape
    parts = keep_ref.shape[0]
    sub = local_k // (2 * parts)
    lse = four_z(add_logs, far_ref[...], one_ref[...], two_ref[...], part_ref[...])
    lse_ref[...] = lse
    scales = jnp.exp(top_ref[...] - lse)
    counts = jnp.zeros((local_k, LANES), jnp.float32)
    for i in range(TILES):
        rows = slice(i * tile, (i + 1) * tile)
        p = e_ref[:, rows] * scales[i : i + 1, :]
        part = p[:, :LANES]
        for j in range(1, tile // LANES):
            part = part + p[:, j * LANES : (j + 1) * LANES]
        counts = counts + part
        dots = jnp.dot(p.astype(jnp.bfloat16), xv_ref[rows, :], preferred_element_type=jnp.float32)
        if i == 0:
            sums_ref[...] = dots
        else:
            sums_ref[...] += dots
    counts_ref[...] = jnp.broadcast_to(jnp.sum(counts, axis=1, keepdims=True), counts.shape)
    core = lax.axis_index("core")
    for out, which in ((keep_ref, core), (send_ref, 1 - core)):
        for h in range(parts):
            base = pl.multiple_of((which * parts + h) * sub, sub)
            for d in range(width // LANES):
                out[h, d * sub : (d + 1) * sub, :] = sums_ref[
                    pl.ds(base, sub), d * LANES : (d + 1) * LANES
                ]
            out[h, (width // LANES) * sub :, :] = pack_column(counts_ref, base, sub)


def halves_kernel(keep_ref, got_ref, a_ref, b_ref):
    a_ref[...] = keep_ref[0] + got_ref[0]
    b_ref[...] = keep_ref[1] + got_ref[1]


def updated(total, old):
    blocks, sub = len(old), old[0].shape[0]
    counts = total[blocks * sub :, :]
    under = [jnp.broadcast_to(counts[:, j : j + 1], (8, LANES)) + 1.0 for j in range(sub // 8)]
    parts = []
    for d in range(blocks):
        for j in range(sub // 8):
            at = d * sub + 8 * j
            parts.append((total[at : at + 8, :] + old[d][8 * j : 8 * j + 8, :]) / under[j])
    return jnp.concatenate(parts, axis=0), counts


def update_kernel(a_ref, a_got_ref, b_ref, b_got_ref, old_ref, out_ref):
    local_k, width = old_ref.shape
    blocks = width // LANES
    sub = local_k // 4
    core = lax.axis_index("core")
    for h, (ref, got_ref) in enumerate(((a_ref, a_got_ref), (b_ref, b_got_ref))):
        base = pl.multiple_of((core * 2 + h) * sub, sub)
        old = [old_ref[pl.ds(base, sub), d * LANES : (d + 1) * LANES] for d in range(blocks)]
        fresh, counts = updated(ref[...] + got_ref[...], old)
        out_ref[h, : blocks * sub, :] = fresh
        out_ref[h, blocks * sub :, :] = counts


def place_halves(mine_ref, theirs_ref, c_ref, counts_ref=None):
    local_k, width = c_ref.shape
    blocks = width // LANES
    sub = local_k // 4
    core = lax.axis_index("core")
    for ref, which in ((mine_ref, core), (theirs_ref, 1 - core)):
        for h in range(2):
            base = pl.multiple_of((which * 2 + h) * sub, sub)
            for d in range(blocks):
                c_ref[pl.ds(base, sub), d * LANES : (d + 1) * LANES] = ref[
                    h, d * sub : (d + 1) * sub, :
                ]
            if counts_ref is not None:
                for j in range(sub // 8):
                    counts_ref[pl.ds(base + 8 * j, 8), :] = jnp.broadcast_to(
                        ref[h, blocks * sub :, j : j + 1], (8, LANES)
                    )


def coarse_logits(g, f):
    inner = lax.dot_general(
        g,
        f,
        (((1,), (1,)), ((), ())),
        precision=lax.Precision.HIGHEST,
        preferred_element_type=jnp.float32,
    )
    sharp = 4.0 * g.shape[1] ** -0.5
    return sharp * (inner - 0.5 * jnp.sum(g * g, axis=1, keepdims=True))


def column_lse(logits):
    top = jnp.max(logits, axis=0, keepdims=True)
    return top + jnp.log(jnp.sum(jnp.exp(logits - top), axis=0, keepdims=True))


def pack_totals(totals, weights, out_ref, mass_ref):
    sub, width = totals.shape
    blocks = width // LANES
    for d in range(blocks):
        out_ref[d * sub : (d + 1) * sub, :] = totals[:, d * LANES : (d + 1) * LANES]
    mass_ref[...] = jnp.broadcast_to(jnp.sum(weights, axis=1, keepdims=True), (sub, LANES))
    out_ref[blocks * sub :, :] = pack_column(mass_ref, 0, sub)


def coarse_base():
    return pl.multiple_of((lax.axis_index("x") * 2 + lax.axis_index("core")) * SUB, SUB)


def coarse_first_kernel(
    mine_ref, theirs_ref, g_ref, out_ref, f_ref, row_ref, pass_ref, counts_ref, logits_ref, mass_ref
):
    pass_ref[...] = mine_ref[...]
    place_halves(mine_ref, theirs_ref, f_ref, counts_ref)
    row = jnp.transpose(counts_ref[...])[:1, :]
    row_ref[...] = row
    f = f_ref[...]
    logits = coarse_logits(g_ref[...], f)
    logits_ref[...] = logits
    weights = row * jnp.exp(logits_ref[pl.ds(coarse_base(), SUB), :] - column_lse(logits))
    totals = lax.dot_general(
        weights,
        f,
        (((1,), (0,)), ((), ())),
        precision=lax.Precision.HIGHEST,
        preferred_element_type=jnp.float32,
    )
    pack_totals(totals, weights, out_ref, mass_ref)


def read_old(old_ref):
    if old_ref.shape[1] == LANES:
        return [old_ref[at : at + SUB, :] for at in range(0, old_ref.shape[0], SUB)]
    base = coarse_base()
    return [old_ref[pl.ds(base, SUB), at : at + LANES] for at in range(0, old_ref.shape[1], LANES)]


def split_three(x):
    high = x.astype(jnp.bfloat16)
    rest = x - high.astype(jnp.float32)
    mid = rest.astype(jnp.bfloat16)
    low = (rest - mid.astype(jnp.float32)).astype(jnp.bfloat16)
    return high, mid, low


def six_products(x, f_parts, contract):
    high, mid, low = split_three(x)
    n = x.shape[0]
    dims = (((1,), (contract,)), ((), ()))

    def dot(a, b):
        return lax.dot_general(a, b, dims, preferred_element_type=jnp.float32)

    by_high = dot(jnp.concatenate([high, mid, low], axis=0), f_parts[0])
    by_mid = dot(jnp.concatenate([high, mid], axis=0), f_parts[1])
    by_low = dot(high, f_parts[2])
    small = (by_high[2 * n :] + by_low) + by_mid[n:]
    return (small + (by_high[n : 2 * n] + by_mid[:n])) + by_high[:n]


def coarse_logits_kernel(
    two_ref, one_ref, far_ref, part_ref, old_ref, f_high, f_mid, f_low, g_ref, logits_ref, lse_ref
):
    total = four_z(jnp.add, far_ref[...], one_ref[...], two_ref[...], part_ref[...])
    fresh, _ = updated(total, read_old(old_ref))
    g_ref[...] = fresh
    g = jnp.concatenate([fresh[at : at + SUB, :] for at in range(0, fresh.shape[0], SUB)], axis=1)
    inner = six_products(g, (f_high[...], f_mid[...], f_low[...]), 1)
    sharp = 4.0 * g.shape[1] ** -0.5
    logits = sharp * (inner - 0.5 * jnp.sum(g * g, axis=1, keepdims=True))
    logits_ref[...] = logits
    lse_ref[...] = column_lse(logits)


def pair_kernel(
    mine_ref, theirs_ref, f_ref, row_ref, score_ref,
    f_high, f_mid, f_low, row2_ref, f_out, row_out, score_out,
    counts_ref, other_ref, flat_ref, sems,
):
    copies = [
        pltpu.make_async_copy(f_ref, f_out, sems.at[0]),
        pltpu.make_async_copy(row_ref, row_out, sems.at[1]),
        pltpu.make_async_copy(flat_ref, score_out, sems.at[2]),
    ]
    copies[0].start()
    copies[1].start()
    per = score_ref.shape[1] // LANES
    for i in range(score_ref.shape[0]):
        for j in range(per):
            flat_ref[i * per + j : i * per + j + 1, :] = score_ref[
                i : i + 1, j * LANES : (j + 1) * LANES
            ]
    copies[2].start()
    local_k = f_ref.shape[0]
    place_halves(mine_ref, theirs_ref, other_ref, counts_ref)
    other_row = jnp.transpose(counts_ref[...])[:1, :]
    odd = lax.rem(lax.axis_index("z"), 2)
    for source, at in ((f_ref, odd), (other_ref, 1 - odd)):
        rows = pl.ds(pl.multiple_of(at * local_k, local_k), local_k)
        for out, part in zip((f_high, f_mid, f_low), split_three(source[...])):
            out[rows, :] = part
    row = row_ref[...]
    is_odd = jnp.full(row.shape, odd, jnp.int32) == 1
    row2_ref[:, :local_k] = jnp.where(is_odd, other_row, row)
    row2_ref[:, local_k:] = jnp.where(is_odd, row, other_row)
    for copy in copies:
        copy.wait()


def coarse_weights_kernel(
    two_ref, one_ref, far_ref, part_ref, logits_ref, row_ref, f_high, f_mid, f_low, out_ref, mass_ref
):
    norm = four(add_logs, far_ref[...], one_ref[...], two_ref[...], part_ref[...])
    weights = row_ref[...] * jnp.exp(logits_ref[...] - norm)
    totals = six_products(weights, (f_high[...], f_mid[...], f_low[...]), 0)
    pack_totals(totals, weights, out_ref, mass_ref)


def coarse_last_kernel(two_ref, one_ref, far_ref, part_ref, old_ref, out_ref):
    total = four_z(jnp.add, far_ref[...], one_ref[...], two_ref[...], part_ref[...])
    fresh, mass = updated(total, read_old(old_ref))
    out_ref[: fresh.shape[0], :] = fresh
    out_ref[fresh.shape[0] :, :] = mass


def stack_kernel(two_ref, one_ref, far_ref, x_ref, out_ref):
    for s, ref in enumerate((x_ref, one_ref, far_ref, two_ref)):
        out_ref[s] = ref[...]


def assemble_kernel(factor, mine_ref, theirs_ref, g_ref, row_ref, counts_ref):
    width = g_ref.shape[1]
    blocks = width // LANES
    chip, core = lax.axis_index("x"), lax.axis_index("core")
    for ref, which in ((mine_ref, core), (theirs_ref, 1 - core)):
        for s in range(mine_ref.shape[0]):
            base = pl.multiple_of((lax.bitwise_xor(chip, s) * 2 + which) * SUB, SUB)
            for d in range(blocks):
                g_ref[pl.ds(base, SUB), d * LANES : (d + 1) * LANES] = ref[
                    s, d * SUB : (d + 1) * SUB, :
                ]
            for j in range(SUB // 8):
                counts_ref[pl.ds(base + 8 * j, 8), :] = jnp.broadcast_to(
                    ref[s, blocks * SUB :, j : j + 1], (8, LANES)
                )
    row_ref[...] = jnp.transpose(counts_ref[...])[:1, :] * factor


def struct(*shape, dtype=jnp.float32):
    return jax.ShapeDtypeStruct(shape, dtype)


def kernel_call(body, out_shape, name, n_in, scratch=(), in_hbm=0, out_hbm=0):
    many = isinstance(out_shape, list)
    anywhere = pl.BlockSpec(memory_space=pl.ANY)
    spec = pl.BlockSpec(memory_space=pltpu.VMEM)
    return pl.pallas_call(
        body,
        out_shape=out_shape,
        in_specs=[anywhere] * in_hbm + [spec] * (n_in - in_hbm),
        out_specs=[spec] * (len(out_shape) - out_hbm) + [anywhere] * out_hbm if many else spec,
        scratch_shapes=list(scratch),
        compiler_params=pltpu.CompilerParams(vmem_limit_bytes=24 * 1024 * 1024),
        name=name,
    )


def per_device(sketches, centroids, coarse_init):
    nx, nc = lax.axis_size("x"), lax.axis_size("core")
    ny, nz = lax.axis_size("y"), lax.axis_size("z")
    n_row, n_cent = nx * nc, ny * nz
    rows, width = sketches.shape
    local_k = centroids.shape[0]
    tile = rows // TILES
    blocks = width // LANES

    small = struct(blocks * SUB + 8, LANES)
    half = struct(blocks * local_k // 4 + 8, LANES)
    halves = struct(2, blocks * local_k // 4 + 8, LANES)
    column = pltpu.VMEM((local_k, LANES), jnp.float32)
    exps_out = pltpu.VMEM((local_k, rows), jnp.float32)
    cents_out = pltpu.VMEM((local_k, width), jnp.float32)
    by_row = struct(TILES, tile)

    for round_index in range(ROUNDS):
        if round_index == 0:
            exps, held, cents, top, part = kernel_call(
                score_load_kernel,
                [exps_out, pltpu.VMEM((rows, width), jnp.bfloat16), cents_out, by_row, by_row],
                "scores_first",
                2,
                scratch=[
                    pltpu.VMEM((local_k, tile // 2), jnp.float32),
                    pltpu.VMEM((local_k, tile // 2), jnp.float32),
                    pltpu.SemaphoreType.DMA((2 * TILES,)),
                    pltpu.SemaphoreType.DMA,
                ],
                in_hbm=2,
            )(
                pltpu.with_memory_space_constraint(sketches, pltpu.HBM),
                pltpu.with_memory_space_constraint(centroids, pltpu.HBM),
            )
        else:
            exps, cents, top, part = kernel_call(
                score_kernel, [exps_out, cents_out, by_row, by_row], "scores", 3
            )(held, mine, theirs)
        part = kernel_call(combine_lse_kernel, by_row, "lse_y", 4)(
            *burst(part, "y"), part
        )
        part = add_logs(part, swap(part, "z", 1))
        keep, send, lse = kernel_call(
            sums_kernel,
            [halves, halves, by_row],
            "sums",
            7,
            scratch=[pltpu.VMEM((local_k, width), jnp.float32), column],
        )(*burst(part, "z"), part, exps, held, top)
        a, b = kernel_call(halves_kernel, [half, half], "halves", 2)(keep, swap(send, "core", 1))
        a_got, b_got = swap(a, "x", 1), swap(b, "x", 3)
        a, b = a + a_got, b + b_got
        mine = kernel_call(update_kernel, halves, "update", 5)(
            a, swap(a, "x", 3), b, swap(b, "x", 1), cents
        )
        theirs = swap(mine, "core", 1)

    mass = pltpu.VMEM((SUB, LANES), jnp.float32)
    for iteration in range(COARSE_ITERS):
        if iteration == 0:
            packed, cents, row, mine = kernel_call(
                coarse_first_kernel,
                [small, cents_out, pltpu.VMEM((1, local_k), jnp.float32), halves],
                "coarse_first",
                3,
                scratch=[column, pltpu.VMEM((coarse_init.shape[0], local_k), jnp.float32), mass],
            )(mine, theirs, coarse_init)
            old = coarse_init
        else:
            if iteration == 1:
                f_part = pltpu.VMEM((2 * local_k, width), jnp.bfloat16)
                *f_parts, row_pair, fine_centroids, fine_counts, row_score = kernel_call(
                    pair_kernel,
                    [f_part, f_part, f_part, pltpu.VMEM((1, 2 * local_k), jnp.float32)]
                    + [
                        pltpu.HBM((local_k, width), jnp.float32),
                        pltpu.HBM((1, local_k), jnp.float32),
                        pltpu.HBM((rows // LANES, LANES), jnp.float32),
                    ],
                    "pair",
                    5,
                    scratch=[
                        column,
                        pltpu.VMEM((local_k, width), jnp.float32),
                        pltpu.VMEM((rows // LANES, LANES), jnp.float32),
                        pltpu.SemaphoreType.DMA((3,)),
                    ],
                    out_hbm=3,
                )(*pair, cents, row, lse)
            old, logits, part = kernel_call(
                coarse_logits_kernel,
                [struct(blocks * SUB, LANES), struct(SUB, 2 * local_k), struct(1, 2 * local_k)],
                "coarse_logits",
                8,
            )(*z_parts, packed, old, *f_parts)
            part = add_logs(part, swap(part, "core", 1))
            packed = kernel_call(coarse_weights_kernel, small, "coarse_weights", 9, scratch=[mass])(
                *burst(part, "x"), part, logits, row_pair, *f_parts
            )
        packed = kernel_call(combine_sum_kernel, small, "sum_y", 4)(*burst(packed, "y"), packed)
        if iteration == 0:
            packed, pair = kernel_call(add_pass_kernel, [small, halves], "sum_pair", 3)(
                packed, swap(packed, "z", 1), swap(mine, "z", 1)
            )
            pair = (pair, swap(pair, "core", 1))
        z_parts = burst(packed, "z")
    last = kernel_call(coarse_last_kernel, small, "coarse_last", 5)(*z_parts, packed, old)
    mine = kernel_call(stack_kernel, struct(nx, *small.shape), "stack", 4)(
        *burst(last, "x"), last
    )
    all_rows = rows * n_row
    all_cents = local_k * n_cent
    coarse, masses = kernel_call(
        functools.partial(assemble_kernel, all_cents / all_rows),
        [struct(local_k, width), struct(1, local_k)],
        "assemble",
        2,
        scratch=[column],
    )(mine, swap(mine, "core", 1))
    return (
        fine_centroids,
        fine_counts.reshape(local_k),
        coarse,
        masses.reshape(local_k),
        row_score.reshape(rows),
    )


def solution(mesh):
    n_row, n_cent = mesh.shape["row"], mesh.shape["cent"]
    fine = Mesh(mesh.devices.reshape(n_row // 2, 2, n_cent // 8, 8), ("x", "core", "y", "z"))
    row, cent = ("x", "core"), ("y", "z")
    in_specs = (P(row, None), P(cent, None), P())
    out_specs = (P(cent, None), P(cent), P(), P(), P(row))
    return jax.shard_map(
        per_device, mesh=fine, in_specs=in_specs, out_specs=out_specs, check_vma=False
    )
```

```python
import functools
import math

import jax
import jax.numpy as jnp
from jax import lax
from jax.experimental import pallas as pl
from jax.experimental.pallas import tpu as pltpu
from jax.sharding import Mesh, PartitionSpec as P

ROUNDS = 2
COARSE_ITERS = 3
LANES = 128
TILES = 8
WINDOW = 4
LOADS = 2
SUB = 32


def swap(x, axis, bits):
    size = lax.axis_size(axis)
    return lax.ppermute(x, axis, [(i, i ^ bits) for i in range(size)])


def add_logs(a, b):
    return jnp.maximum(a, b) + jnp.log1p(jnp.exp(-jnp.abs(a - b)))


def fetch(x, axis, source):
    return lax.ppermute(x, axis, [(source(i), i) for i in range(lax.axis_size(axis))])


def burst(x, axis):
    if axis == "z":
        size = lax.axis_size(axis)
        return [
            fetch(x, axis, lambda i: (i + 1 if i % 2 else i - 1) % size),
            fetch(x, axis, lambda i: (i - 2 if i % 2 else i + 2) % size),
            swap(x, axis, 5),
        ]
    return [swap(x, axis, bits) for bits in (3, 1, 2)]


def four(combine, far, one, two, x):
    return combine(combine(x, far), combine(one, two))


def four_z(combine, far, one, two, x):
    z = lax.axis_index("z")
    swapped = lax.rem(lax.shift_right_logical(z, 1) + lax.rem(z, 2), 2)
    mask = jnp.full(x.shape, swapped, jnp.int32) == 0
    first = jnp.where(mask, one, two)
    second = jnp.where(mask, two, one)
    return combine(combine(x, first), combine(second, far))


def tile_dots(c_bf, x_ref, i, tile):
    return lax.dot_general(
        c_bf,
        x_ref[i * tile : (i + 1) * tile, :],
        (((1,), (1,)), ((), ())),
        preferred_element_type=jnp.float32,
    )


def finish_tile(dots, half, i, factor, e_ref, top_ref, lse_ref):
    tile = dots.shape[1]
    dots = dots - half
    top = jnp.max(dots, axis=0, keepdims=True)
    exps = jnp.exp2((dots - top) * (factor * math.log2(math.e)))
    total = jnp.sum(exps, axis=0, keepdims=True)
    top = top * factor
    e_ref[:, i * tile : (i + 1) * tile] = exps
    top_ref[i : i + 1, :] = top
    lse_ref[i : i + 1, :] = top + jnp.log(total)


def score_all(c, xv_ref, e_ref, top_ref, lse_ref, ready):
    tile = xv_ref.shape[0] // TILES
    factor = c.shape[1] ** -0.5
    c_bf = c.astype(jnp.bfloat16)
    half = 0.5 * jnp.sum(c * c, axis=1, keepdims=True)
    previous = None
    for i in range(TILES):
        ready(i)
        dots = tile_dots(c_bf, xv_ref, i, tile)
        if i:
            finish_tile(previous, half, i - 1, factor, e_ref, top_ref, lse_ref)
        previous = dots
    finish_tile(previous, half, TILES - 1, factor, e_ref, top_ref, lse_ref)


def score_load_kernel(x_ref, c_ref, e_ref, xv_ref, cv_ref, top_ref, lse_ref, sems, c_sem):
    step = xv_ref.shape[0] // (TILES * LOADS)
    c_copy = pltpu.make_async_copy(c_ref, cv_ref, c_sem)
    c_copy.start()
    copies = [
        pltpu.make_async_copy(
            x_ref.at[pl.ds(i * step, step)], xv_ref.at[pl.ds(i * step, step)], sems.at[i]
        )
        for i in range(TILES * LOADS)
    ]
    for i in range(WINDOW * LOADS):
        copies[i].start(priority=i % 2)
    c_copy.wait()

    def ready(i):
        for copy in copies[i * LOADS : (i + 1) * LOADS]:
            copy.wait()
        for j, copy in enumerate(copies[(i + WINDOW) * LOADS : (i + WINDOW + 1) * LOADS]):
            copy.start(priority=j % 2)

    score_all(cv_ref[...], xv_ref, e_ref, top_ref, lse_ref, ready)


def score_kernel(xv_ref, mine_ref, theirs_ref, e_ref, cv_ref, top_ref, lse_ref):
    place_halves(mine_ref, theirs_ref, cv_ref)
    score_all(cv_ref[...], xv_ref, e_ref, top_ref, lse_ref, lambda i: None)


def pack_column(ref, base, sub):
    lane = lax.broadcasted_iota(jnp.int32, (8, LANES), 1)
    packed = jnp.zeros((8, LANES), jnp.float32)
    for j in range(sub // 8):
        packed = jnp.where(lane == j, ref[pl.ds(base + 8 * j, 8), :], packed)
    return packed


def combine_lse_kernel(two_ref, one_ref, far_ref, x_ref, out_ref):
    out_ref[...] = four(add_logs, far_ref[...], one_ref[...], two_ref[...], x_ref[...])


def combine_sum_pass_kernel(two_ref, one_ref, far_ref, x_ref, other_ref, out_ref, pass_ref):
    out_ref[...] = four(jnp.add, far_ref[...], one_ref[...], two_ref[...], x_ref[...])
    pass_ref[...] = other_ref[...]


def combine_sum_kernel(two_ref, one_ref, far_ref, x_ref, out_ref):
    out_ref[...] = four(jnp.add, far_ref[...], one_ref[...], two_ref[...], x_ref[...])


def sums_kernel(
    two_ref, one_ref, far_ref, part_ref, e_ref, xv_ref, top_ref,
    keep_ref, send_ref, lse_ref, sums_ref, counts_ref,
):
    tile = xv_ref.shape[0] // TILES
    local_k, width = sums_ref.shape
    parts = keep_ref.shape[0]
    sub = local_k // (2 * parts)
    lse = four_z(add_logs, far_ref[...], one_ref[...], two_ref[...], part_ref[...])
    lse_ref[...] = lse
    scales = jnp.exp(top_ref[...] - lse)
    counts = jnp.zeros((local_k, LANES), jnp.float32)
    for i in range(TILES):
        rows = slice(i * tile, (i + 1) * tile)
        p = e_ref[:, rows] * scales[i : i + 1, :]
        part = p[:, :LANES]
        for j in range(1, tile // LANES):
            part = part + p[:, j * LANES : (j + 1) * LANES]
        counts = counts + part
        dots = jnp.dot(p.astype(jnp.bfloat16), xv_ref[rows, :], preferred_element_type=jnp.float32)
        if i == 0:
            sums_ref[...] = dots
        else:
            sums_ref[...] += dots
    counts_ref[...] = jnp.broadcast_to(jnp.sum(counts, axis=1, keepdims=True), counts.shape)
    core = lax.axis_index("core")
    for out, which in ((keep_ref, core), (send_ref, 1 - core)):
        for h in range(parts):
            base = pl.multiple_of((which * parts + h) * sub, sub)
            for d in range(width // LANES):
                out[h, d * sub : (d + 1) * sub, :] = sums_ref[
                    pl.ds(base, sub), d * LANES : (d + 1) * LANES
                ]
            out[h, (width // LANES) * sub :, :] = pack_column(counts_ref, base, sub)


def halves_kernel(keep_ref, got_ref, a_ref, b_ref):
    a_ref[...] = keep_ref[0] + got_ref[0]
    b_ref[...] = keep_ref[1] + got_ref[1]


def updated(total, old):
    blocks, sub = len(old), old[0].shape[0]
    counts = total[blocks * sub :, :]
    under = [jnp.broadcast_to(counts[:, j : j + 1], (8, LANES)) + 1.0 for j in range(sub // 8)]
    parts = []
    for d in range(blocks):
        for j in range(sub // 8):
            at = d * sub + 8 * j
            parts.append((total[at : at + 8, :] + old[d][8 * j : 8 * j + 8, :]) / under[j])
    return jnp.concatenate(parts, axis=0), counts


def update_kernel(a_ref, a_got_ref, b_ref, b_got_ref, old_ref, out_ref):
    local_k, width = old_ref.shape
    blocks = width // LANES
    sub = local_k // 4
    core = lax.axis_index("core")
    for h, (ref, got_ref) in enumerate(((a_ref, a_got_ref), (b_ref, b_got_ref))):
        base = pl.multiple_of((core * 2 + h) * sub, sub)
        old = [old_ref[pl.ds(base, sub), d * LANES : (d + 1) * LANES] for d in range(blocks)]
        fresh, counts = updated(ref[...] + got_ref[...], old)
        out_ref[h, : blocks * sub, :] = fresh
        out_ref[h, blocks * sub :, :] = counts


def place_halves(mine_ref, theirs_ref, c_ref, counts_ref=None):
    local_k, width = c_ref.shape
    blocks = width // LANES
    sub = local_k // 4
    core = lax.axis_index("core")
    for ref, which in ((mine_ref, core), (theirs_ref, 1 - core)):
        for h in range(2):
            base = pl.multiple_of((which * 2 + h) * sub, sub)
            for d in range(blocks):
                c_ref[pl.ds(base, sub), d * LANES : (d + 1) * LANES] = ref[
                    h, d * sub : (d + 1) * sub, :
                ]
            if counts_ref is not None:
                for j in range(sub // 8):
                    counts_ref[pl.ds(base + 8 * j, 8), :] = jnp.broadcast_to(
                        ref[h, blocks * sub :, j : j + 1], (8, LANES)
                    )


def coarse_logits(g, f):
    inner = lax.dot_general(
        g,
        f,
        (((1,), (1,)), ((), ())),
        precision=lax.Precision.HIGHEST,
        preferred_element_type=jnp.float32,
    )
    sharp = 4.0 * g.shape[1] ** -0.5
    return sharp * (inner - 0.5 * jnp.sum(g * g, axis=1, keepdims=True))


def column_lse(logits):
    top = jnp.max(logits, axis=0, keepdims=True)
    return top + jnp.log(jnp.sum(jnp.exp(logits - top), axis=0, keepdims=True))


def pack_totals(totals, weights, out_ref, mass_ref):
    sub, width = totals.shape
    blocks = width // LANES
    for d in range(blocks):
        out_ref[d * sub : (d + 1) * sub, :] = totals[:, d * LANES : (d + 1) * LANES]
    mass_ref[...] = jnp.broadcast_to(jnp.sum(weights, axis=1, keepdims=True), (sub, LANES))
    out_ref[blocks * sub :, :] = pack_column(mass_ref, 0, sub)


def coarse_base():
    return pl.multiple_of((lax.axis_index("x") * 2 + lax.axis_index("core")) * SUB, SUB)


def coarse_first_kernel(
    mine_ref, theirs_ref, g_ref, out_ref, f_ref, row_ref, pass_ref, counts_ref, logits_ref, mass_ref
):
    pass_ref[...] = mine_ref[...]
    place_halves(mine_ref, theirs_ref, f_ref, counts_ref)
    row = jnp.transpose(counts_ref[...])[:1, :]
    row_ref[...] = row
    f = f_ref[...]
    logits = coarse_logits(g_ref[...], f)
    logits_ref[...] = logits
    weights = row * jnp.exp(logits_ref[pl.ds(coarse_base(), SUB), :] - column_lse(logits))
    totals = lax.dot_general(
        weights,
        f,
        (((1,), (0,)), ((), ())),
        precision=lax.Precision.HIGHEST,
        preferred_element_type=jnp.float32,
    )
    pack_totals(totals, weights, out_ref, mass_ref)


def read_old(old_ref):
    if old_ref.shape[1] == LANES:
        return [old_ref[at : at + SUB, :] for at in range(0, old_ref.shape[0], SUB)]
    base = coarse_base()
    return [old_ref[pl.ds(base, SUB), at : at + LANES] for at in range(0, old_ref.shape[1], LANES)]


def split_three(x):
    high = x.astype(jnp.bfloat16)
    rest = x - high.astype(jnp.float32)
    mid = rest.astype(jnp.bfloat16)
    low = (rest - mid.astype(jnp.float32)).astype(jnp.bfloat16)
    return high, mid, low


def six_products(x, f_parts, contract):
    high, mid, low = split_three(x)
    n = x.shape[0]
    dims = (((1,), (contract,)), ((), ()))

    def dot(a, b):
        return lax.dot_general(a, b, dims, preferred_element_type=jnp.float32)

    by_high = dot(jnp.concatenate([high, mid, low], axis=0), f_parts[0])
    by_mid = dot(jnp.concatenate([high, mid], axis=0), f_parts[1])
    by_low = dot(high, f_parts[2])
    small = (by_high[2 * n :] + by_low) + by_mid[n:]
    return (small + (by_high[n : 2 * n] + by_mid[:n])) + by_high[:n]


def coarse_logits_kernel(
    two_ref, one_ref, far_ref, part_ref, old_ref, f_high, f_mid, f_low, g_ref, logits_ref, lse_ref
):
    total = four_z(jnp.add, far_ref[...], one_ref[...], two_ref[...], part_ref[...])
    fresh, _ = updated(total, read_old(old_ref))
    g_ref[...] = fresh
    g = jnp.concatenate([fresh[at : at + SUB, :] for at in range(0, fresh.shape[0], SUB)], axis=1)
    inner = six_products(g, (f_high[...], f_mid[...], f_low[...]), 1)
    sharp = 4.0 * g.shape[1] ** -0.5
    logits = sharp * (inner - 0.5 * jnp.sum(g * g, axis=1, keepdims=True))
    logits_ref[...] = logits
    lse_ref[...] = column_lse(logits)


def pair_kernel(
    mine_ref, theirs_ref, f_ref, row_ref, score_ref,
    f_high, f_mid, f_low, row2_ref, f_out, row_out, score_out,
    counts_ref, other_ref, flat_ref, sems,
):
    copies = [
        pltpu.make_async_copy(f_ref, f_out, sems.at[0]),
        pltpu.make_async_copy(row_ref, row_out, sems.at[1]),
        pltpu.make_async_copy(flat_ref, score_out, sems.at[2]),
    ]
    copies[0].start()
    copies[1].start()
    per = score_ref.shape[1] // LANES
    for i in range(score_ref.shape[0]):
        for j in range(per):
            flat_ref[i * per + j : i * per + j + 1, :] = score_ref[
                i : i + 1, j * LANES : (j + 1) * LANES
            ]
    copies[2].start()
    local_k = f_ref.shape[0]
    place_halves(mine_ref, theirs_ref, other_ref, counts_ref)
    other_row = jnp.transpose(counts_ref[...])[:1, :]
    odd = lax.rem(lax.axis_index("z"), 2)
    for source, at in ((f_ref, odd), (other_ref, 1 - odd)):
        rows = pl.ds(pl.multiple_of(at * local_k, local_k), local_k)
        for out, part in zip((f_high, f_mid, f_low), split_three(source[...])):
            out[rows, :] = part
    row = row_ref[...]
    is_odd = jnp.full(row.shape, odd, jnp.int32) == 1
    row2_ref[:, :local_k] = jnp.where(is_odd, other_row, row)
    row2_ref[:, local_k:] = jnp.where(is_odd, row, other_row)
    for copy in copies:
        copy.wait()


def coarse_weights_kernel(
    two_ref, one_ref, far_ref, part_ref, logits_ref, row_ref, f_high, f_mid, f_low, out_ref, mass_ref
):
    norm = four(add_logs, far_ref[...], one_ref[...], two_ref[...], part_ref[...])
    weights = row_ref[...] * jnp.exp(logits_ref[...] - norm)
    totals = six_products(weights, (f_high[...], f_mid[...], f_low[...]), 0)
    pack_totals(totals, weights, out_ref, mass_ref)


def coarse_last_kernel(two_ref, one_ref, far_ref, part_ref, old_ref, out_ref):
    total = four_z(jnp.add, far_ref[...], one_ref[...], two_ref[...], part_ref[...])
    fresh, mass = updated(total, read_old(old_ref))
    out_ref[: fresh.shape[0], :] = fresh
    out_ref[fresh.shape[0] :, :] = mass


def stack_kernel(two_ref, one_ref, far_ref, x_ref, out_ref):
    for s, ref in enumerate((x_ref, one_ref, far_ref, two_ref)):
        out_ref[s] = ref[...]


def assemble_kernel(factor, mine_ref, theirs_ref, g_ref, row_ref, counts_ref):
    width = g_ref.shape[1]
    blocks = width // LANES
    chip, core = lax.axis_index("x"), lax.axis_index("core")
    for ref, which in ((mine_ref, core), (theirs_ref, 1 - core)):
        for s in range(mine_ref.shape[0]):
            base = pl.multiple_of((lax.bitwise_xor(chip, s) * 2 + which) * SUB, SUB)
            for d in range(blocks):
                g_ref[pl.ds(base, SUB), d * LANES : (d + 1) * LANES] = ref[
                    s, d * SUB : (d + 1) * SUB, :
                ]
            for j in range(SUB // 8):
                counts_ref[pl.ds(base + 8 * j, 8), :] = jnp.broadcast_to(
                    ref[s, blocks * SUB :, j : j + 1], (8, LANES)
                )
    row_ref[...] = jnp.transpose(counts_ref[...])[:1, :] * factor


def struct(*shape, dtype=jnp.float32):
    return jax.ShapeDtypeStruct(shape, dtype)


def kernel_call(body, out_shape, name, n_in, scratch=(), in_hbm=0, out_hbm=0):
    many = isinstance(out_shape, list)
    anywhere = pl.BlockSpec(memory_space=pl.ANY)
    spec = pl.BlockSpec(memory_space=pltpu.VMEM)
    return pl.pallas_call(
        body,
        out_shape=out_shape,
        in_specs=[anywhere] * in_hbm + [spec] * (n_in - in_hbm),
        out_specs=[spec] * (len(out_shape) - out_hbm) + [anywhere] * out_hbm if many else spec,
        scratch_shapes=list(scratch),
        compiler_params=pltpu.CompilerParams(vmem_limit_bytes=24 * 1024 * 1024),
        name=name,
    )


def per_device(sketches, centroids, coarse_init):
    nx, nc = lax.axis_size("x"), lax.axis_size("core")
    ny, nz = lax.axis_size("y"), lax.axis_size("z")
    n_row, n_cent = nx * nc, ny * nz
    rows, width = sketches.shape
    local_k = centroids.shape[0]
    tile = rows // TILES
    blocks = width // LANES

    small = struct(blocks * SUB + 8, LANES)
    half = struct(blocks * local_k // 4 + 8, LANES)
    halves = struct(2, blocks * local_k // 4 + 8, LANES)
    column = pltpu.VMEM((local_k, LANES), jnp.float32)
    exps_out = pltpu.VMEM((local_k, rows), jnp.float32)
    cents_out = pltpu.VMEM((local_k, width), jnp.float32)
    by_row = struct(TILES, tile)

    for round_index in range(ROUNDS):
        if round_index == 0:
            exps, held, cents, top, part = kernel_call(
                score_load_kernel,
                [exps_out, pltpu.VMEM((rows, width), jnp.bfloat16), cents_out, by_row, by_row],
                "scores_first",
                2,
                scratch=[pltpu.SemaphoreType.DMA((TILES * LOADS,)), pltpu.SemaphoreType.DMA],
                in_hbm=2,
            )(
                pltpu.with_memory_space_constraint(sketches, pltpu.HBM),
                pltpu.with_memory_space_constraint(centroids, pltpu.HBM),
            )
        else:
            exps, cents, top, part = kernel_call(
                score_kernel, [exps_out, cents_out, by_row, by_row], "scores", 3
            )(held, mine, theirs)
        part = kernel_call(combine_lse_kernel, by_row, "lse_y", 4)(
            *burst(part, "y"), part
        )
        part = add_logs(part, swap(part, "z", 1))
        keep, send, lse = kernel_call(
            sums_kernel,
            [halves, halves, by_row],
            "sums",
            7,
            scratch=[pltpu.VMEM((local_k, width), jnp.float32), column],
        )(*burst(part, "z"), part, exps, held, top)
        a, b = kernel_call(halves_kernel, [half, half], "halves", 2)(keep, swap(send, "core", 1))
        a_got, b_got = swap(a, "x", 1), swap(b, "x", 3)
        a, b = a + a_got, b + b_got
        mine = kernel_call(update_kernel, halves, "update", 5)(
            a, swap(a, "x", 3), b, swap(b, "x", 1), cents
        )
        theirs = swap(mine, "core", 1)

    mass = pltpu.VMEM((SUB, LANES), jnp.float32)
    for iteration in range(COARSE_ITERS):
        if iteration == 0:
            packed, cents, row, mine = kernel_call(
                coarse_first_kernel,
                [small, cents_out, pltpu.VMEM((1, local_k), jnp.float32), halves],
                "coarse_first",
                3,
                scratch=[column, pltpu.VMEM((coarse_init.shape[0], local_k), jnp.float32), mass],
            )(mine, theirs, coarse_init)
            old = coarse_init
        else:
            if iteration == 1:
                f_part = pltpu.VMEM((2 * local_k, width), jnp.bfloat16)
                *f_parts, row_pair, fine_centroids, fine_counts, row_score = kernel_call(
                    pair_kernel,
                    [f_part, f_part, f_part, pltpu.VMEM((1, 2 * local_k), jnp.float32)]
                    + [
                        pltpu.HBM((local_k, width), jnp.float32),
                        pltpu.HBM((1, local_k), jnp.float32),
                        pltpu.HBM((rows // LANES, LANES), jnp.float32),
                    ],
                    "pair",
                    5,
                    scratch=[
                        column,
                        pltpu.VMEM((local_k, width), jnp.float32),
                        pltpu.VMEM((rows // LANES, LANES), jnp.float32),
                        pltpu.SemaphoreType.DMA((3,)),
                    ],
                    out_hbm=3,
                )(*pair, cents, row, lse)
            old, logits, part = kernel_call(
                coarse_logits_kernel,
                [struct(blocks * SUB, LANES), struct(SUB, 2 * local_k), struct(1, 2 * local_k)],
                "coarse_logits",
                8,
            )(*z_parts, packed, old, *f_parts)
            part = add_logs(part, swap(part, "core", 1))
            packed = kernel_call(coarse_weights_kernel, small, "coarse_weights", 9, scratch=[mass])(
                *burst(part, "x"), part, logits, row_pair, *f_parts
            )
        parts = (*burst(packed, "y"), packed)
        if iteration == 0:
            packed, pair = kernel_call(combine_sum_pass_kernel, [small, halves], "sum_y_pass", 5)(
                *parts, swap(mine, "z", 1)
            )
            pair = (pair, swap(pair, "core", 1))
            packed = packed + swap(packed, "z", 1)
        else:
            packed = kernel_call(combine_sum_kernel, small, "sum_y", 4)(*parts)
        z_parts = burst(packed, "z")
    last = kernel_call(coarse_last_kernel, small, "coarse_last", 5)(*z_parts, packed, old)
    mine = kernel_call(stack_kernel, struct(nx, *small.shape), "stack", 4)(
        *burst(last, "x"), last
    )
    all_rows = rows * n_row
    all_cents = local_k * n_cent
    coarse, masses = kernel_call(
        functools.partial(assemble_kernel, all_cents / all_rows),
        [struct(local_k, width), struct(1, local_k)],
        "assemble",
        2,
        scratch=[column],
    )(mine, swap(mine, "core", 1))
    return (
        fine_centroids,
        fine_counts.reshape(local_k),
        coarse,
        masses.reshape(local_k),
        row_score.reshape(rows),
    )


def solution(mesh):
    n_row, n_cent = mesh.shape["row"], mesh.shape["cent"]
    fine = Mesh(mesh.devices.reshape(n_row // 2, 2, n_cent // 8, 8), ("x", "core", "y", "z"))
    row, cent = ("x", "core"), ("y", "z")
    in_specs = (P(row, None), P(cent, None), P())
    out_specs = (P(cent, None), P(cent), P(), P(), P(row))
    return jax.shard_map(
        per_device, mesh=fine, in_specs=in_specs, out_specs=out_specs, check_vma=False
    )
```

```python
import functools
import math

import jax
import jax.numpy as jnp
from jax import lax
from jax.experimental import pallas as pl
from jax.experimental.pallas import tpu as pltpu
from jax.sharding import Mesh, PartitionSpec as P

ROUNDS = 2
COARSE_ITERS = 3
LANES = 128
TILES = 8
WINDOW = 4
LOADS = 1
SUB = 32


def swap(x, axis, bits):
    size = lax.axis_size(axis)
    return lax.ppermute(x, axis, [(i, i ^ bits) for i in range(size)])


def add_logs(a, b):
    return jnp.maximum(a, b) + jnp.log1p(jnp.exp(-jnp.abs(a - b)))


def fetch(x, axis, source):
    return lax.ppermute(x, axis, [(source(i), i) for i in range(lax.axis_size(axis))])


def burst(x, axis):
    if axis == "z":
        size = lax.axis_size(axis)
        return [
            fetch(x, axis, lambda i: (i + 1 if i % 2 else i - 1) % size),
            fetch(x, axis, lambda i: (i - 2 if i % 2 else i + 2) % size),
            swap(x, axis, 5),
        ]
    return [swap(x, axis, bits) for bits in (3, 1, 2)]


def four(combine, far, one, two, x):
    return combine(combine(x, far), combine(one, two))


def four_z(combine, far, one, two, x):
    z = lax.axis_index("z")
    swapped = lax.rem(lax.shift_right_logical(z, 1) + lax.rem(z, 2), 2)
    mask = jnp.full(x.shape, swapped, jnp.int32) == 0
    first = jnp.where(mask, one, two)
    second = jnp.where(mask, two, one)
    return combine(combine(x, first), combine(second, far))


def tile_dots(c_bf, x_ref, i, tile):
    return lax.dot_general(
        c_bf,
        x_ref[i * tile : (i + 1) * tile, :],
        (((1,), (1,)), ((), ())),
        preferred_element_type=jnp.float32,
    )


def finish_tile(dots, half, i, factor, e_ref, top_ref, lse_ref):
    tile = dots.shape[1]
    dots = dots - half
    top = jnp.max(dots, axis=0, keepdims=True)
    exps = jnp.exp2((dots - top) * (factor * math.log2(math.e)))
    total = jnp.sum(exps, axis=0, keepdims=True)
    top = top * factor
    e_ref[:, i * tile : (i + 1) * tile] = exps
    top_ref[i : i + 1, :] = top
    lse_ref[i : i + 1, :] = top + jnp.log(total)


def score_all(c, xv_ref, e_ref, top_ref, lse_ref, ready):
    tile = xv_ref.shape[0] // TILES
    factor = c.shape[1] ** -0.5
    c_bf = c.astype(jnp.bfloat16)
    half = 0.5 * jnp.sum(c * c, axis=1, keepdims=True)
    previous = None
    for i in range(TILES):
        ready(i)
        dots = tile_dots(c_bf, xv_ref, i, tile)
        if i:
            finish_tile(previous, half, i - 1, factor, e_ref, top_ref, lse_ref)
        previous = dots
    finish_tile(previous, half, TILES - 1, factor, e_ref, top_ref, lse_ref)


def score_load_kernel(x_ref, c_ref, e_ref, xv_ref, cv_ref, top_ref, lse_ref, sems, c_sem):
    step = xv_ref.shape[0] // (TILES * LOADS)
    c_copy = pltpu.make_async_copy(c_ref, cv_ref, c_sem)
    c_copy.start()
    copies = [
        pltpu.make_async_copy(
            x_ref.at[pl.ds(i * step, step)], xv_ref.at[pl.ds(i * step, step)], sems.at[i]
        )
        for i in range(TILES * LOADS)
    ]
    for i in range(WINDOW * LOADS):
        copies[i].start(priority=i % 2)
    c_copy.wait()

    def ready(i):
        for copy in copies[i * LOADS : (i + 1) * LOADS]:
            copy.wait()
        for j, copy in enumerate(copies[(i + WINDOW) * LOADS : (i + WINDOW + 1) * LOADS]):
            copy.start(priority=(i * LOADS + j) % 2)

    score_all(cv_ref[...], xv_ref, e_ref, top_ref, lse_ref, ready)


def score_kernel(xv_ref, mine_ref, theirs_ref, e_ref, cv_ref, top_ref, lse_ref):
    place_halves(mine_ref, theirs_ref, cv_ref)
    score_all(cv_ref[...], xv_ref, e_ref, top_ref, lse_ref, lambda i: None)


def pack_column(ref, base, sub):
    lane = lax.broadcasted_iota(jnp.int32, (8, LANES), 1)
    packed = jnp.zeros((8, LANES), jnp.float32)
    for j in range(sub // 8):
        packed = jnp.where(lane == j, ref[pl.ds(base + 8 * j, 8), :], packed)
    return packed


def combine_lse_kernel(two_ref, one_ref, far_ref, x_ref, out_ref):
    out_ref[...] = four(add_logs, far_ref[...], one_ref[...], two_ref[...], x_ref[...])


def combine_sum_pass_kernel(two_ref, one_ref, far_ref, x_ref, other_ref, out_ref, pass_ref):
    out_ref[...] = four(jnp.add, far_ref[...], one_ref[...], two_ref[...], x_ref[...])
    pass_ref[...] = other_ref[...]


def combine_sum_kernel(two_ref, one_ref, far_ref, x_ref, out_ref):
    out_ref[...] = four(jnp.add, far_ref[...], one_ref[...], two_ref[...], x_ref[...])


def sums_kernel(
    two_ref, one_ref, far_ref, part_ref, e_ref, xv_ref, top_ref,
    keep_ref, send_ref, lse_ref, sums_ref, counts_ref,
):
    tile = xv_ref.shape[0] // TILES
    local_k, width = sums_ref.shape
    parts = keep_ref.shape[0]
    sub = local_k // (2 * parts)
    lse = four_z(add_logs, far_ref[...], one_ref[...], two_ref[...], part_ref[...])
    lse_ref[...] = lse
    scales = jnp.exp(top_ref[...] - lse)
    counts = jnp.zeros((local_k, LANES), jnp.float32)
    for i in range(TILES):
        rows = slice(i * tile, (i + 1) * tile)
        p = e_ref[:, rows] * scales[i : i + 1, :]
        part = p[:, :LANES]
        for j in range(1, tile // LANES):
            part = part + p[:, j * LANES : (j + 1) * LANES]
        counts = counts + part
        dots = jnp.dot(p.astype(jnp.bfloat16), xv_ref[rows, :], preferred_element_type=jnp.float32)
        if i == 0:
            sums_ref[...] = dots
        else:
            sums_ref[...] += dots
    counts_ref[...] = jnp.broadcast_to(jnp.sum(counts, axis=1, keepdims=True), counts.shape)
    core = lax.axis_index("core")
    for out, which in ((keep_ref, core), (send_ref, 1 - core)):
        for h in range(parts):
            base = pl.multiple_of((which * parts + h) * sub, sub)
            for d in range(width // LANES):
                out[h, d * sub : (d + 1) * sub, :] = sums_ref[
                    pl.ds(base, sub), d * LANES : (d + 1) * LANES
                ]
            out[h, (width // LANES) * sub :, :] = pack_column(counts_ref, base, sub)


def halves_kernel(keep_ref, got_ref, a_ref, b_ref):
    a_ref[...] = keep_ref[0] + got_ref[0]
    b_ref[...] = keep_ref[1] + got_ref[1]


def updated(total, old):
    blocks, sub = len(old), old[0].shape[0]
    counts = total[blocks * sub :, :]
    under = [jnp.broadcast_to(counts[:, j : j + 1], (8, LANES)) + 1.0 for j in range(sub // 8)]
    parts = []
    for d in range(blocks):
        for j in range(sub // 8):
            at = d * sub + 8 * j
            parts.append((total[at : at + 8, :] + old[d][8 * j : 8 * j + 8, :]) / under[j])
    return jnp.concatenate(parts, axis=0), counts


def update_kernel(a_ref, a_got_ref, b_ref, b_got_ref, old_ref, out_ref):
    local_k, width = old_ref.shape
    blocks = width // LANES
    sub = local_k // 4
    core = lax.axis_index("core")
    for h, (ref, got_ref) in enumerate(((a_ref, a_got_ref), (b_ref, b_got_ref))):
        base = pl.multiple_of((core * 2 + h) * sub, sub)
        old = [old_ref[pl.ds(base, sub), d * LANES : (d + 1) * LANES] for d in range(blocks)]
        fresh, counts = updated(ref[...] + got_ref[...], old)
        out_ref[h, : blocks * sub, :] = fresh
        out_ref[h, blocks * sub :, :] = counts


def place_halves(mine_ref, theirs_ref, c_ref, counts_ref=None):
    local_k, width = c_ref.shape
    blocks = width // LANES
    sub = local_k // 4
    core = lax.axis_index("core")
    for ref, which in ((mine_ref, core), (theirs_ref, 1 - core)):
        for h in range(2):
            base = pl.multiple_of((which * 2 + h) * sub, sub)
            for d in range(blocks):
                c_ref[pl.ds(base, sub), d * LANES : (d + 1) * LANES] = ref[
                    h, d * sub : (d + 1) * sub, :
                ]
            if counts_ref is not None:
                for j in range(sub // 8):
                    counts_ref[pl.ds(base + 8 * j, 8), :] = jnp.broadcast_to(
                        ref[h, blocks * sub :, j : j + 1], (8, LANES)
                    )


def coarse_logits(g, f):
    inner = lax.dot_general(
        g,
        f,
        (((1,), (1,)), ((), ())),
        precision=lax.Precision.HIGHEST,
        preferred_element_type=jnp.float32,
    )
    sharp = 4.0 * g.shape[1] ** -0.5
    return sharp * (inner - 0.5 * jnp.sum(g * g, axis=1, keepdims=True))


def column_lse(logits):
    top = jnp.max(logits, axis=0, keepdims=True)
    return top + jnp.log(jnp.sum(jnp.exp(logits - top), axis=0, keepdims=True))


def pack_totals(totals, weights, out_ref, mass_ref):
    sub, width = totals.shape
    blocks = width // LANES
    for d in range(blocks):
        out_ref[d * sub : (d + 1) * sub, :] = totals[:, d * LANES : (d + 1) * LANES]
    mass_ref[...] = jnp.broadcast_to(jnp.sum(weights, axis=1, keepdims=True), (sub, LANES))
    out_ref[blocks * sub :, :] = pack_column(mass_ref, 0, sub)


def coarse_base():
    return pl.multiple_of((lax.axis_index("x") * 2 + lax.axis_index("core")) * SUB, SUB)


def coarse_first_kernel(
    mine_ref, theirs_ref, g_ref, out_ref, f_ref, row_ref, pass_ref, counts_ref, logits_ref, mass_ref
):
    pass_ref[...] = mine_ref[...]
    place_halves(mine_ref, theirs_ref, f_ref, counts_ref)
    row = jnp.transpose(counts_ref[...])[:1, :]
    row_ref[...] = row
    f = f_ref[...]
    logits = coarse_logits(g_ref[...], f)
    logits_ref[...] = logits
    weights = row * jnp.exp(logits_ref[pl.ds(coarse_base(), SUB), :] - column_lse(logits))
    pack_totals(six_products(weights, split_three(f), 0), weights, out_ref, mass_ref)


def read_old(old_ref):
    if old_ref.shape[1] == LANES:
        return [old_ref[at : at + SUB, :] for at in range(0, old_ref.shape[0], SUB)]
    base = coarse_base()
    return [old_ref[pl.ds(base, SUB), at : at + LANES] for at in range(0, old_ref.shape[1], LANES)]


def split_three(x):
    high = x.astype(jnp.bfloat16)
    rest = x - high.astype(jnp.float32)
    mid = rest.astype(jnp.bfloat16)
    low = (rest - mid.astype(jnp.float32)).astype(jnp.bfloat16)
    return high, mid, low


def six_products(x, f_parts, contract):
    high, mid, low = split_three(x)
    n = x.shape[0]
    dims = (((1,), (contract,)), ((), ()))

    def dot(a, b):
        return lax.dot_general(a, b, dims, preferred_element_type=jnp.float32)

    by_high = dot(jnp.concatenate([high, mid, low], axis=0), f_parts[0])
    by_mid = dot(jnp.concatenate([high, mid], axis=0), f_parts[1])
    by_low = dot(high, f_parts[2])
    small = (by_high[2 * n :] + by_low) + by_mid[n:]
    return (small + (by_high[n : 2 * n] + by_mid[:n])) + by_high[:n]


def coarse_logits_kernel(
    two_ref, one_ref, far_ref, part_ref, old_ref, f_high, f_mid, f_low, g_ref, logits_ref, lse_ref
):
    total = four_z(jnp.add, far_ref[...], one_ref[...], two_ref[...], part_ref[...])
    fresh, _ = updated(total, read_old(old_ref))
    g_ref[...] = fresh
    g = jnp.concatenate([fresh[at : at + SUB, :] for at in range(0, fresh.shape[0], SUB)], axis=1)
    inner = six_products(g, (f_high[...], f_mid[...], f_low[...]), 1)
    sharp = 4.0 * g.shape[1] ** -0.5
    logits = sharp * (inner - 0.5 * jnp.sum(g * g, axis=1, keepdims=True))
    logits_ref[...] = logits
    lse_ref[...] = column_lse(logits)


def pair_kernel(
    mine_ref, theirs_ref, f_ref, row_ref, score_ref,
    f_high, f_mid, f_low, row2_ref, f_out, row_out, score_out,
    counts_ref, other_ref, flat_ref, sems,
):
    copies = [
        pltpu.make_async_copy(f_ref, f_out, sems.at[0]),
        pltpu.make_async_copy(row_ref, row_out, sems.at[1]),
        pltpu.make_async_copy(flat_ref, score_out, sems.at[2]),
    ]
    copies[0].start()
    copies[1].start()
    per = score_ref.shape[1] // LANES
    for i in range(score_ref.shape[0]):
        for j in range(per):
            flat_ref[i * per + j : i * per + j + 1, :] = score_ref[
                i : i + 1, j * LANES : (j + 1) * LANES
            ]
    copies[2].start()
    local_k = f_ref.shape[0]
    place_halves(mine_ref, theirs_ref, other_ref, counts_ref)
    other_row = jnp.transpose(counts_ref[...])[:1, :]
    odd = lax.rem(lax.axis_index("z"), 2)
    for source, at in ((f_ref, odd), (other_ref, 1 - odd)):
        rows = pl.ds(pl.multiple_of(at * local_k, local_k), local_k)
        for out, part in zip((f_high, f_mid, f_low), split_three(source[...])):
            out[rows, :] = part
    row = row_ref[...]
    is_odd = jnp.full(row.shape, odd, jnp.int32) == 1
    row2_ref[:, :local_k] = jnp.where(is_odd, other_row, row)
    row2_ref[:, local_k:] = jnp.where(is_odd, row, other_row)
    for copy in copies:
        copy.wait()


def coarse_weights_kernel(
    two_ref, one_ref, far_ref, part_ref, logits_ref, row_ref, f_high, f_mid, f_low, out_ref, mass_ref
):
    norm = four(add_logs, far_ref[...], one_ref[...], two_ref[...], part_ref[...])
    weights = row_ref[...] * jnp.exp(logits_ref[...] - norm)
    totals = six_products(weights, (f_high[...], f_mid[...], f_low[...]), 0)
    pack_totals(totals, weights, out_ref, mass_ref)


def coarse_last_kernel(two_ref, one_ref, far_ref, part_ref, old_ref, out_ref):
    total = four_z(jnp.add, far_ref[...], one_ref[...], two_ref[...], part_ref[...])
    fresh, mass = updated(total, read_old(old_ref))
    out_ref[: fresh.shape[0], :] = fresh
    out_ref[fresh.shape[0] :, :] = mass


def stack_kernel(two_ref, one_ref, far_ref, x_ref, out_ref):
    for s, ref in enumerate((x_ref, one_ref, far_ref, two_ref)):
        out_ref[s] = ref[...]


def assemble_kernel(factor, mine_ref, theirs_ref, g_ref, row_ref, counts_ref):
    width = g_ref.shape[1]
    blocks = width // LANES
    chip, core = lax.axis_index("x"), lax.axis_index("core")
    for ref, which in ((mine_ref, core), (theirs_ref, 1 - core)):
        for s in range(mine_ref.shape[0]):
            base = pl.multiple_of((lax.bitwise_xor(chip, s) * 2 + which) * SUB, SUB)
            for d in range(blocks):
                g_ref[pl.ds(base, SUB), d * LANES : (d + 1) * LANES] = ref[
                    s, d * SUB : (d + 1) * SUB, :
                ]
            for j in range(SUB // 8):
                counts_ref[pl.ds(base + 8 * j, 8), :] = jnp.broadcast_to(
                    ref[s, blocks * SUB :, j : j + 1], (8, LANES)
                )
    row_ref[...] = jnp.transpose(counts_ref[...])[:1, :] * factor


def struct(*shape, dtype=jnp.float32):
    return jax.ShapeDtypeStruct(shape, dtype)


def kernel_call(body, out_shape, name, n_in, scratch=(), in_hbm=0, out_hbm=0):
    many = isinstance(out_shape, list)
    anywhere = pl.BlockSpec(memory_space=pl.ANY)
    spec = pl.BlockSpec(memory_space=pltpu.VMEM)
    return pl.pallas_call(
        body,
        out_shape=out_shape,
        in_specs=[anywhere] * in_hbm + [spec] * (n_in - in_hbm),
        out_specs=[spec] * (len(out_shape) - out_hbm) + [anywhere] * out_hbm if many else spec,
        scratch_shapes=list(scratch),
        compiler_params=pltpu.CompilerParams(vmem_limit_bytes=24 * 1024 * 1024),
        name=name,
    )


def per_device(sketches, centroids, coarse_init):
    nx, nc = lax.axis_size("x"), lax.axis_size("core")
    ny, nz = lax.axis_size("y"), lax.axis_size("z")
    n_row, n_cent = nx * nc, ny * nz
    rows, width = sketches.shape
    local_k = centroids.shape[0]
    tile = rows // TILES
    blocks = width // LANES

    small = struct(blocks * SUB + 8, LANES)
    half = struct(blocks * local_k // 4 + 8, LANES)
    halves = struct(2, blocks * local_k // 4 + 8, LANES)
    column = pltpu.VMEM((local_k, LANES), jnp.float32)
    exps_out = pltpu.VMEM((local_k, rows), jnp.float32)
    cents_out = pltpu.VMEM((local_k, width), jnp.float32)
    by_row = struct(TILES, tile)

    for round_index in range(ROUNDS):
        if round_index == 0:
            exps, held, cents, top, part = kernel_call(
                score_load_kernel,
                [exps_out, pltpu.VMEM((rows, width), jnp.bfloat16), cents_out, by_row, by_row],
                "scores_first",
                2,
                scratch=[pltpu.SemaphoreType.DMA((TILES * LOADS,)), pltpu.SemaphoreType.DMA],
                in_hbm=2,
            )(
                pltpu.with_memory_space_constraint(sketches, pltpu.HBM),
                pltpu.with_memory_space_constraint(centroids, pltpu.HBM),
            )
        else:
            exps, cents, top, part = kernel_call(
                score_kernel, [exps_out, cents_out, by_row, by_row], "scores", 3
            )(held, mine, theirs)
        part = kernel_call(combine_lse_kernel, by_row, "lse_y", 4)(
            *burst(part, "y"), part
        )
        part = add_logs(part, swap(part, "z", 1))
        keep, send, lse = kernel_call(
            sums_kernel,
            [halves, halves, by_row],
            "sums",
            7,
            scratch=[pltpu.VMEM((local_k, width), jnp.float32), column],
        )(*burst(part, "z"), part, exps, held, top)
        a, b = kernel_call(halves_kernel, [half, half], "halves", 2)(keep, swap(send, "core", 1))
        a_got, b_got = swap(a, "x", 1), swap(b, "x", 3)
        a, b = a + a_got, b + b_got
        mine = kernel_call(update_kernel, halves, "update", 5)(
            a, swap(a, "x", 3), b, swap(b, "x", 1), cents
        )
        theirs = swap(mine, "core", 1)

    mass = pltpu.VMEM((SUB, LANES), jnp.float32)
    for iteration in range(COARSE_ITERS):
        if iteration == 0:
            packed, cents, row, mine = kernel_call(
                coarse_first_kernel,
                [small, cents_out, pltpu.VMEM((1, local_k), jnp.float32), halves],
                "coarse_first",
                3,
                scratch=[column, pltpu.VMEM((coarse_init.shape[0], local_k), jnp.float32), mass],
            )(mine, theirs, coarse_init)
            old = coarse_init
        else:
            if iteration == 1:
                f_part = pltpu.VMEM((2 * local_k, width), jnp.bfloat16)
                *f_parts, row_pair, fine_centroids, fine_counts, row_score = kernel_call(
                    pair_kernel,
                    [f_part, f_part, f_part, pltpu.VMEM((1, 2 * local_k), jnp.float32)]
                    + [
                        pltpu.HBM((local_k, width), jnp.float32),
                        pltpu.HBM((1, local_k), jnp.float32),
                        pltpu.HBM((rows // LANES, LANES), jnp.float32),
                    ],
                    "pair",
                    5,
                    scratch=[
                        column,
                        pltpu.VMEM((local_k, width), jnp.float32),
                        pltpu.VMEM((rows // LANES, LANES), jnp.float32),
                        pltpu.SemaphoreType.DMA((3,)),
                    ],
                    out_hbm=3,
                )(*pair, cents, row, lse)
            old, logits, part = kernel_call(
                coarse_logits_kernel,
                [struct(blocks * SUB, LANES), struct(SUB, 2 * local_k), struct(1, 2 * local_k)],
                "coarse_logits",
                8,
            )(*z_parts, packed, old, *f_parts)
            part = add_logs(part, swap(part, "core", 1))
            packed = kernel_call(coarse_weights_kernel, small, "coarse_weights", 9, scratch=[mass])(
                *burst(part, "x"), part, logits, row_pair, *f_parts
            )
        parts = (*burst(packed, "y"), packed)
        if iteration == 0:
            packed, pair = kernel_call(combine_sum_pass_kernel, [small, halves], "sum_y_pass", 5)(
                *parts, swap(mine, "z", 1)
            )
            pair = (pair, swap(pair, "core", 1))
            packed = packed + swap(packed, "z", 1)
        else:
            packed = kernel_call(combine_sum_kernel, small, "sum_y", 4)(*parts)
        z_parts = burst(packed, "z")
    last = kernel_call(coarse_last_kernel, small, "coarse_last", 5)(*z_parts, packed, old)
    mine = kernel_call(stack_kernel, struct(nx, *small.shape), "stack", 4)(
        *burst(last, "x"), last
    )
    all_rows = rows * n_row
    all_cents = local_k * n_cent
    coarse, masses = kernel_call(
        functools.partial(assemble_kernel, all_cents / all_rows),
        [struct(local_k, width), struct(1, local_k)],
        "assemble",
        2,
        scratch=[column],
    )(mine, swap(mine, "core", 1))
    return (
        fine_centroids,
        fine_counts.reshape(local_k),
        coarse,
        masses.reshape(local_k),
        row_score.reshape(rows),
    )


def solution(mesh):
    n_row, n_cent = mesh.shape["row"], mesh.shape["cent"]
    fine = Mesh(mesh.devices.reshape(n_row // 2, 2, n_cent // 8, 8), ("x", "core", "y", "z"))
    row, cent = ("x", "core"), ("y", "z")
    in_specs = (P(row, None), P(cent, None), P())
    out_specs = (P(cent, None), P(cent), P(), P(), P(row))
    return jax.shard_map(
        per_device, mesh=fine, in_specs=in_specs, out_specs=out_specs, check_vma=False
    )
```
